32 devices in a mesh: gx: 4 (over z), gy: 8 (over y, x, core).
Axes of the slice: x: 2, y: 2, z: 4, core: 2. Of those that a mesh axis runs over, the one named last changes fastest.
Arguments:
- populations: float32 [19, 128, 16, 16, 128], P(None, ('gx', 'gy')), may hold values from 0.01 to 0.1
- charge: float32 [128, 16, 16, 128], P(('gx', 'gy')), may hold values from -6 to 6
- fluid_mask: int32 [128, 18, 18, 128], P(('gx', 'gy')), may hold values from 0 to 1, as said below
- tile_ids: int32 [128], P(('gx', 'gy')), may hold values from 0 to 31, as said below
- phase_label: int32 [128, 256, 128], P('gx', 'gy'), may hold values from 0 to 3
- permittivity: float32 [4], replicated, may hold values from 0.5 to 5
Outputs:
- populations_next: float32 [19, 128, 16, 16, 128], P(None, ('gx', 'gy'))
- charge_next: float32 [128, 16, 16, 128], P(('gx', 'gy'))
- potential: float32 [128, 256, 128], P('gx', 'gy')
The draws below stay inside these ranges and needn't reach their ends.
Inputs may be any that keep to these rules, and one draw needn't show every extreme that they name: Within the slots of the devices of one gx index, tile_ids is a permutation of 0 to 31. Position p belongs to the regular block of gy index (p % 16) // 2; every device holds at most 1 positions of any one such block, and some device holds exactly 1. fluid_mask[s, i, j, z] is the fluid flag of grid cell (x0 + i - 1, y0 + j - 1, z), periodic, where (x0, y0) is the first cell of slot s's tile; the rim repeats flags of the neighbouring tiles.
All inputs are finite; a program needn't handle non-finite values.
Results may differ from the reference program's by a relative error of at most 0.0003.
Values sent between devices are 32-bit elements; how exact they have to be, the bound alone decides.
No kernel may reach another device: no remote copies, remote signals or barrier semaphores. Data moves between devices by JAX's collectives and lax.ppermute only.
A program may use at most 192 MiB of HBM per device.

```python
import math
import jax
import jax.numpy as jnp

EDGE = 16
DEPTH = 128
TILE_ROWS = 2
TILE_COLS = 2
PHASES = 4
SWEEPS = 4
TILES_DEV = 4
CAPACITY = 1
BAND_COLS = 16
TILES = 128
GRID_X = 128
GRID_Y = 256
N_GX = 4
N_GY = 8


def band_layout(band_key):
    band_keys = jax.random.split(band_key, 6)
    favored = jax.random.randint(band_keys[0], (), 0, N_GY)
    others = (favored + 1 + jnp.arange(N_GY - 1, dtype=jnp.int32)) % N_GY
    others_pool = jax.random.permutation(band_keys[1], jnp.tile(others, CAPACITY))
    offsets = jnp.concatenate([jnp.full((CAPACITY,), favored, jnp.int32), others_pool[:TILES_DEV - CAPACITY].astype(jnp.int32)])
    offsets = jax.random.permutation(band_keys[2], offsets)
    relabel = jax.random.permutation(band_keys[3], N_GY)
    block_order = jax.vmap(lambda sub_key: jax.random.permutation(sub_key, TILES_DEV))(jax.random.split(band_keys[4], N_GY))
    owners = jnp.arange(N_GY, dtype=jnp.int32)[:, None]
    holder = relabel[(owners + offsets[None, :]) % N_GY]
    position = block_order // TILE_COLS * BAND_COLS + owners * TILE_COLS + block_order % TILE_COLS
    shuffle = jax.random.permutation(band_keys[5], N_GY * TILES_DEV)
    slot_order = jnp.argsort(holder.reshape(-1) * (N_GY * TILES_DEV) + shuffle)
    return position.reshape(-1)[slot_order].astype(jnp.int32)


def layout_all(key):
    band_keys = jax.random.split(jax.random.fold_in(key, 7001), N_GX)
    return jax.vmap(band_layout)(band_keys).reshape(-1).astype(jnp.int32)


def draw_tile_ids(key, part):
    return layout_all(key)


def draw_fluid_mask(key, part):
    tile_ids = layout_all(key)
    fluid_flags = (jax.random.randint(jax.random.fold_in(key, 7002), (GRID_X, GRID_Y, DEPTH), 0, 5) > 0).astype(jnp.int32)
    band_index = jnp.arange(TILES, dtype=jnp.int32) // (N_GY * TILES_DEV)
    first_x = (band_index * TILE_ROWS + tile_ids // BAND_COLS) * EDGE
    first_y = tile_ids % BAND_COLS * EDGE
    spread = jnp.arange(EDGE + 2, dtype=jnp.int32) - 1
    row_index = (first_x[:, None] + spread[None, :]) % GRID_X
    col_index = (first_y[:, None] + spread[None, :]) % GRID_Y
    return fluid_flags[row_index[:, :, None], col_index[:, None, :]].astype(jnp.int32)


def plant(drawn, own_key, low, largest):
    shape = drawn.shape
    index_at = [jax.random.randint(jax.random.fold_in(own_key, axis), (), 0, shape[axis]) for axis in range(len(shape))]
    drawn = drawn.at[tuple(index_at)].set(low)
    longest = shape.index(max(shape))
    index_at[longest] = (index_at[longest] + 1) % shape[longest]
    return drawn.at[tuple(index_at)].set(largest)


def levels(own_key, extent, shards, low, largest):
    loudness = 1.0
    for dim, shards_of in shards:
        draws = jax.random.uniform(jax.random.fold_in(jax.random.fold_in(own_key, 6), dim), (shards_of,), jnp.float32, low / len(shards), largest / len(shards))
        loudness = loudness * jnp.repeat(jnp.exp(draws), extent[dim] // shards_of).reshape((-1,) + (1,) * (len(extent) - 1 - dim))
    return loudness


def centred(own_key, dims, width, reach, shards=(), kind=jnp.bfloat16):
    gain = levels(own_key, dims, shards, -0.22, 0.18) if shards else 1.0
    values = jax.random.normal(own_key, dims, jnp.float32) * width * gain
    return jnp.minimum(jnp.maximum(values, -reach), reach).astype(kind)


def setup_inputs(seed: int = 0) -> dict:
    streams_of = jax.random.split(jax.random.key(seed), 7)
    return {
        "populations": jnp.clip(0.01 + 0.09 * jax.random.uniform(streams_of[0], (19, TILES, EDGE, EDGE, DEPTH), jnp.float32) ** levels(streams_of[0], (19, TILES, EDGE, EDGE, DEPTH), ((1, 32),), -0.2, 0.2), 0.01, 0.1),
        "charge": centred(streams_of[1], (TILES, EDGE, EDGE, DEPTH), 1.0, 6.0, ((0, 32),), jnp.float32),
        "fluid_mask": draw_fluid_mask(jax.random.fold_in(streams_of[6], 71), 0),
        "tile_ids": draw_tile_ids(jax.random.fold_in(streams_of[6], 71), 0),
        "phase_label": plant(jax.random.randint(streams_of[4], (GRID_X, GRID_Y, DEPTH), 0, PHASES), jax.random.fold_in(streams_of[4], 1), 0, PHASES - 1).astype(jnp.int32),
        "permittivity": jnp.clip(jnp.exp(jax.random.uniform(streams_of[5], (PHASES,), jnp.float32, math.log(0.5), math.log(5.0))), 0.5, 5.0),
    }


LATTICE = ((0, 0, 0), (1, 0, 0), (-1, 0, 0), (0, 1, 0), (0, -1, 0), (0, 0, 1), (0, 0, -1),
           (1, 1, 0), (-1, -1, 0), (1, -1, 0), (-1, 1, 0), (1, 0, 1), (-1, 0, -1),
           (1, 0, -1), (-1, 0, 1), (0, 1, 1), (0, -1, -1), (0, 1, -1), (0, -1, 1))
relax_time = 0.8
screening = 0.001
spectrum_low = 0.1
spectrum_high = 2.0


def lattice_weight(direction):
    length = sum(abs(entry) for entry in LATTICE[direction])
    if length == 0:
        return 1.0 / 3.0
    if length == 1:
        return 1.0 / 18.0
    return 1.0 / 36.0


def opposite(direction):
    return LATTICE.index(tuple(-entry for entry in LATTICE[direction]))


def population_sum(population):
    density = population[0]
    for direction in range(1, 19):
        density = density + population[direction]
    return density


def velocity_sums(population):
    sums_list = []
    for axis_index in range(3):
        total = None
        for direction in range(19):
            component = LATTICE[direction][axis_index]
            if component != 0:
                contrib = population[direction] if component > 0 else -population[direction]
                total = contrib if total is None else total + contrib
        sums_list.append(total)
    return sums_list


def collide(population, density, velocity, body_force):
    speed_sq = velocity[0] * velocity[0] + velocity[1] * velocity[1] + velocity[2] * velocity[2]
    source_scale = 1.0 - 0.5 / relax_time
    result = []
    for direction in range(19):
        lattice_step = LATTICE[direction]
        weight = lattice_weight(direction)
        projected = lattice_step[0] * velocity[0] + lattice_step[1] * velocity[1] + lattice_step[2] * velocity[2]
        force_dot = lattice_step[0] * body_force[0] + lattice_step[1] * body_force[1] + lattice_step[2] * body_force[2]
        drift_dot = ((lattice_step[0] - velocity[0]) * body_force[0] + (lattice_step[1] - velocity[1]) * body_force[1]
                     + (lattice_step[2] - velocity[2]) * body_force[2])
        equilibrium = weight * density * (1.0 + 3.0 * projected + 4.5 * projected * projected - 1.5 * speed_sq)
        source = source_scale * weight * (3.0 * drift_dot + 9.0 * projected * force_dot)
        result.append(population[direction] - (population[direction] - equilibrium) / relax_time + source)
    return result


def harmonic(left_value, right_value):
    return 2.0 * left_value * right_value / (left_value + right_value)


def placement(tile_ids):
    band_index = jnp.arange(TILES, dtype=jnp.int32) // (N_GY * TILES_DEV)
    tile_row = band_index * TILE_ROWS + tile_ids // BAND_COLS
    tile_col = tile_ids % BAND_COLS
    slot_at = jnp.zeros((GRID_X // EDGE, GRID_Y // EDGE), jnp.int32).at[tile_row, tile_col].set(
        jnp.arange(TILES, dtype=jnp.int32))
    return tile_row, tile_col, slot_at


def tiles_to_grid(tile_data, slot_at):
    leading = tile_data.shape[0]
    picked = tile_data[:, slot_at]
    picked = jnp.transpose(picked, (0, 1, 3, 2, 4, 5))
    return picked.reshape(leading, GRID_X, GRID_Y, DEPTH)


def grid_to_tiles(grid_data, tile_row, tile_col):
    leading = grid_data.shape[0]
    blocks = grid_data.reshape(leading, GRID_X // EDGE, EDGE, GRID_Y // EDGE, EDGE, DEPTH)
    blocks = jnp.transpose(blocks, (0, 1, 3, 2, 4, 5))
    return blocks[:, tile_row, tile_col]


def apply_operator(field_value, weights_plus, weights_minus, diagonal):
    result = diagonal * field_value
    for axis_index in range(3):
        result = (result - weights_plus[axis_index] * jnp.roll(field_value, -1, axis_index)
                  - weights_minus[axis_index] * jnp.roll(field_value, 1, axis_index))
    return result


def reference(populations, charge, fluid_mask, tile_ids, phase_label, permittivity):
    tile_row, tile_col, slot_at = placement(tile_ids)
    fluid_tiles = fluid_mask[:, 1:EDGE + 1, 1:EDGE + 1].astype(jnp.float32)
    fluid_grid = tiles_to_grid(fluid_tiles[None], slot_at)[0]
    charge_grid = tiles_to_grid(charge[None], slot_at)[0]
    source = charge_grid * fluid_grid
    permit = permittivity[phase_label]
    weights_plus = [harmonic(permit, jnp.roll(permit, -1, axis_index)) for axis_index in range(3)]
    weights_minus = [jnp.roll(weights_plus[axis_index], 1, axis_index) for axis_index in range(3)]
    diagonal = (weights_plus[0] + weights_minus[0] + weights_plus[1] + weights_minus[1]
                + weights_plus[2] + weights_minus[2] + screening)
    center_value = 0.5 * (spectrum_high + spectrum_low)
    half_width = 0.5 * (spectrum_high - spectrum_low)
    ratio_value = center_value / half_width
    rho_old = 1.0 / ratio_value
    residual = source / diagonal
    update = residual / center_value
    potential = update
    for sweep_index in range(SWEEPS - 1):
        residual = residual - apply_operator(update, weights_plus, weights_minus, diagonal) / diagonal
        rho_new = 1.0 / (2.0 * ratio_value - rho_old)
        update = (rho_new * rho_old) * update + (2.0 * rho_new / half_width) * residual
        potential = potential + update
        rho_old = rho_new
    field_grid = jnp.stack([0.5 * (jnp.roll(potential, 1, axis_index) - jnp.roll(potential, -1, axis_index))
                            for axis_index in range(3)])
    field_tiles = grid_to_tiles(field_grid, tile_row, tile_col)
    body_force = [charge * field_tiles[axis_index] for axis_index in range(3)]
    density = population_sum(populations)
    momentum = velocity_sums(populations)
    velocity = [(momentum[axis_index] + 0.5 * body_force[axis_index]) / density for axis_index in range(3)]
    relaxed = collide(populations, density, velocity, body_force)
    outputs = []
    for direction in range(19):
        lattice_step = LATTICE[direction]
        moved = jnp.roll(tiles_to_grid(relaxed[direction][None], slot_at)[0], lattice_step, (0, 1, 2))
        source_fluid = jnp.roll(fluid_grid, lattice_step, (0, 1, 2)) > 0.5
        bounced = tiles_to_grid(relaxed[opposite(direction)][None], slot_at)[0]
        grid_new = jnp.where(source_fluid, moved, bounced)
        tile_new = grid_to_tiles(grid_new[None], tile_row, tile_col)[0]
        outputs.append(jnp.where(fluid_tiles > 0.5, tile_new, populations[direction]))
    populations_next = jnp.stack(outputs)
    change = None
    for axis_index in range(3):
        speed_grid = tiles_to_grid(velocity[axis_index][None], slot_at)[0]
        face_vel = 0.5 * (speed_grid + jnp.roll(speed_grid, -1, axis_index))
        upwind = jnp.where(face_vel > 0, charge_grid, jnp.roll(charge_grid, -1, axis_index))
        face_flux = face_vel * upwind * fluid_grid * jnp.roll(fluid_grid, -1, axis_index)
        flux_term = face_flux - jnp.roll(face_flux, 1, axis_index)
        change = flux_term if change is None else change + flux_term
    change_tiles = grid_to_tiles(change[None], tile_row, tile_col)[0]
    charge_next = jnp.where(fluid_tiles > 0.5, charge - change_tiles, charge)
    return (populations_next, charge_next, potential)
```

```python
import functools

import jax
import jax.numpy as jnp
from jax import lax
from jax.experimental import pallas as pl
from jax.experimental.pallas import tpu as pltpu
from jax.sharding import PartitionSpec as P

EDGE = 16
DEPTH = 128
TILE_ROWS = 2
TILE_COLS = 2
PHASES = 4
SWEEPS = 4

LATTICE = (
    (0, 0, 0),
    (1, 0, 0),
    (-1, 0, 0),
    (0, 1, 0),
    (0, -1, 0),
    (0, 0, 1),
    (0, 0, -1),
    (1, 1, 0),
    (-1, -1, 0),
    (1, -1, 0),
    (-1, 1, 0),
    (1, 0, 1),
    (-1, 0, -1),
    (1, 0, -1),
    (-1, 0, 1),
    (0, 1, 1),
    (0, -1, -1),
    (0, 1, -1),
    (0, -1, 1),
)
relax_time = 0.8
screening = 0.001
spectrum_low = 0.1
spectrum_high = 2.0

AREA = EDGE * EDGE
SIDE = 8
RING = 2
WIDE = RING + SWEEPS - 1
WIDER = WIDE + 1
FRAME = EDGE + 2 * RING
PADDED = EDGE + 2 * SIDE
CHANNELS = 10
HALVES = 2 * CHANNELS
VMEM = pl.BlockSpec(memory_space=pltpu.VMEM)
SMEM = pl.BlockSpec(memory_space=pltpu.SMEM)
PARAMS = pltpu.CompilerParams(vmem_limit_bytes=56 * 2**20)


def crossing(axis_index, face_sign):
    return [q for q in range(19) if LATTICE[q][axis_index] == face_sign]


def opposite(direction):
    return LATTICE.index(tuple(-entry for entry in LATTICE[direction]))


def lattice_weight(direction):
    return (1.0 / 3.0, 1.0 / 18.0, 1.0 / 36.0)[sum(abs(e) for e in LATTICE[direction])]


def along(direction, vector):
    total = None
    for entry, part in zip(LATTICE[direction], vector):
        if entry:
            term = part if entry > 0 else -part
            total = term if total is None else total + term
    return total


def moments(pops):
    density = pops[0]
    for q in range(1, 19):
        density = density + pops[q]
    momentum = []
    for axis in range(3):
        plus = sum_of([pops[q] for q in crossing(axis, 1)])
        minus = sum_of([pops[q] for q in crossing(axis, -1)])
        momentum.append(plus - minus)
    return density, momentum


def sum_of(values):
    total = values[0]
    for value in values[1:]:
        total = total + value
    return total


def collide(pops, density, momentum, force):
    source_scale = 1.0 - 0.5 / relax_time
    gain = 1.0 / relax_time
    inverse = 1.0 / density
    carried = [m + 0.5 * f for m, f in zip(momentum, force)]
    velocity = [c * inverse for c in carried]
    energy = sum_of([c * v for c, v in zip(carried, velocity)])
    power = sum_of([v * f for v, f in zip(velocity, force)])
    base = gain * density - (1.5 * gain) * energy - (3.0 * source_scale) * power
    relaxed = {}
    for q in pops:
        weight = lattice_weight(q)
        kept = (1.0 - gain) * pops[q]
        if q == 0:
            relaxed[q] = kept + weight * base
            continue
        if q in relaxed:
            continue
        p, g, rp = along(q, velocity), along(q, force), along(q, carried)
        even = weight * base + p * ((4.5 * gain * weight) * rp + (9.0 * source_scale * weight) * g)
        odd = (3.0 * gain * weight) * rp + (3.0 * source_scale * weight) * g
        relaxed[q] = kept + (even + odd)
        back = opposite(q)
        if back in pops:
            relaxed[back] = (1.0 - gain) * pops[back] + (even - odd)
    return relaxed, velocity


def ring_pairs(axis):
    size = lax.axis_size(axis)
    up = [(i, (i + 1) % size) for i in range(size)]
    return up, [(j, i) for i, j in up]


def pack_source(tiles, band_cols, ids, charge, mask, out):
    out[...] = jnp.zeros_like(out)
    lane = lax.broadcasted_iota(jnp.int32, (8, DEPTH), 1)
    header = jnp.zeros((8, DEPTH), jnp.int32)
    for t in range(tiles):
        owner = ids[t] % band_cols // TILE_COLS
        header = jnp.where(lane == t, ids[t], header)
        for i in range(EDGE):
            flags = mask[t, i + 1, 1 : EDGE + 1, :].astype(jnp.float32)
            out[owner, pl.ds(i * EDGE, EDGE), :] = charge[t, pl.ds(i * EDGE, EDGE), :] * flags
    for peer in range(out.shape[0]):
        out[peer, pl.ds(AREA, 8), :] = header.astype(jnp.float32)


def assemble(hold, arrived, block, left, right):
    for local in range(TILE_ROWS * TILE_COLS):
        r, c = local // TILE_COLS, local % TILE_COLS
        slot = hold[local]
        for i in range(EDGE):
            row = r * EDGE + i
            cells = arrived[slot, pl.ds(i * EDGE, EDGE), :]
            block[row, pl.ds(c * EDGE, EDGE), :] = cells
            if c == 0:
                left[row] = cells[:SIDE]
            if c == TILE_COLS - 1:
                right[row] = cells[EDGE - SIDE :]


def harmonic(a, b):
    return 2.0 * a * b / (a + b)


def face_weights(table, labels, before, after, wx, wy, wz, inverse, permit):
    rows = labels.shape[0]
    total = rows + 2 * WIDER

    def look(label):
        value = jnp.full(label.shape, table[PHASES - 1], jnp.float32)
        for phase in range(PHASES - 1):
            value = jnp.where(label == phase, table[phase], value)
        return value

    for row in range(WIDER):
        permit[row] = look(before[row])
        permit[WIDER + rows + row] = look(after[row])

    def fill(row, carry):
        permit[WIDER + row] = look(labels[row])
        return carry

    lax.fori_loop(0, rows, fill, 0, unroll=2)
    width = labels.shape[1]
    wx[0] = harmonic(permit[0], permit[1])

    def weigh(row, carry):
        here = permit[row]
        x_plus = harmonic(here, permit[row + 1])
        y_plus = harmonic(here, pltpu.roll(here, width - 1, 0))
        z_plus = harmonic(here, pltpu.roll(here, DEPTH - 1, 1))
        wx[row] = x_plus
        wy[row] = y_plus
        wz[row] = z_plus
        diagonal = x_plus + wx[row - 1] + y_plus + pltpu.roll(y_plus, 1, 0)
        diagonal = diagonal + z_plus + pltpu.roll(z_plus, 1, 1) + screening
        inverse[row] = 1.0 / diagonal
        return carry

    lax.fori_loop(1, total - 1, weigh, 0, unroll=2)


def solve(hold, middle, before, after, wx, wy, wz, inverse, out, frames, u0, u1, residual, potential):
    rows, width = middle.shape[0], middle.shape[1]
    center_value = 0.5 * (spectrum_high + spectrum_low)
    half_width = 0.5 * (spectrum_high - spectrum_low)
    ratio = center_value / half_width

    def start(row, source):
        r = source * inverse[row]
        residual[row] = r
        u = r * (1.0 / center_value)
        u0[row] = u
        potential[row] = u

    for row in range(WIDE):
        start(1 + row, before[row])
        start(1 + WIDE + rows + row, after[row])

    def begin(row, carry):
        start(1 + WIDE + row, middle[row])
        return carry

    lax.fori_loop(0, rows, begin, 0, unroll=2)
    old, new = u0, u1
    rho = 1.0 / ratio
    for sweep in range(1, SWEEPS):
        rho_new = 1.0 / (2.0 * ratio - rho)
        a, b = rho_new * rho, 2.0 * rho_new / half_width
        last = sweep == SWEEPS - 1

        def step(row, carry):
            u = old[row]
            y_weight, z_weight = wy[row], wz[row]
            spread = wx[row] * old[row + 1] + wx[row - 1] * old[row - 1]
            spread = spread + y_weight * pltpu.roll(u, width - 1, 0) + pltpu.roll(y_weight * u, 1, 0)
            spread = spread + z_weight * pltpu.roll(u, DEPTH - 1, 1) + pltpu.roll(z_weight * u, 1, 1)
            r = residual[row] - u + inverse[row] * spread
            u = a * u + b * r
            potential[row] = potential[row] + u
            if not last:
                residual[row] = r
                new[row] = u
            return carry

        lax.fori_loop(1 + sweep, rows + 2 * WIDER - 1 - sweep, step, 0, unroll=2)
        old, new = new, old
        rho = rho_new
    inner = width - 2 * SIDE

    def give(row, carry):
        out[row] = potential[WIDER + row, pl.ds(SIDE, inner), :]
        return carry

    lax.fori_loop(0, rows, give, 0, unroll=2)
    frames[...] = jnp.zeros_like(frames)
    for local in range(TILE_ROWS * TILE_COLS):
        r, c = local // TILE_COLS, local % TILE_COLS
        slot = hold[local]
        for a in range(FRAME):
            frames[slot, pl.ds(a * FRAME, FRAME), :] = potential[
                WIDER + r * EDGE - RING + a, pl.ds(SIDE + c * EDGE - RING, FRAME), :
            ]


def unit_counts(peers):
    per_x = -(-HALVES // peers)
    per_y = -(-2 * HALVES // peers)
    return per_x, per_y


def unit_places(peers):
    per_x, per_y = unit_counts(peers)
    places = {}
    for unit in range(HALVES):
        for face in range(2):
            places[face, unit // 2, unit % 2] = (unit % peers, (face * per_x + unit // peers) * 8)
    for unit in range(2 * HALVES):
        face, rest = 2 + unit // HALVES, unit % HALVES
        places[face, rest // 2, rest % 2] = (unit % peers, (2 * per_x + unit // peers) * 8)
    return places


FACES = ((0, -1), (0, 1), (1, -1), (1, 1))


def raw_faces(peers, pops, charge, out):
    places = unit_places(peers)
    taken = set(places.values())
    for peer in range(peers):
        for row in range(0, out.shape[2], 8):
            if (peer, row) not in taken:
                out[peer, 0, pl.ds(row, 8), :] = jnp.zeros((8, DEPTH), jnp.float32)
    for face, (axis, sign) in enumerate(FACES):
        layer = 0 if sign < 0 else EDGE - 1
        for half in range(2):
            if axis == 0:
                where = pl.ds(layer * EDGE + 8 * half, 8)
            else:
                where = pl.ds(8 * half * EDGE + layer, 8, stride=EDGE)
            values = [pops[q, 0, where, :] for q in range(19)]
            density, momentum = moments(values)
            channels = [values[q] for q in crossing(axis, sign)]
            channels += [density] + momentum + [charge[0, where, :]]
            for channel, value in enumerate(channels):
                peer, row = places[face, channel, half]
                out[peer, 0, pl.ds(row, 8), :] = value


def outer_rows(band_cols, per_x, slot_of, arrived, low, high):
    size = per_x * 8
    for col in range(band_cols):
        low[col] = arrived[slot_of[col], pl.ds(0, size), :]
        high[col] = arrived[slot_of[(TILE_ROWS - 1) * band_cols + col], pl.ds(size, size), :]


def turn_faces(band_cols, per_x, slot_of, tile_at, odd, arrived, below, above, out, from_low, from_high):
    size = per_x * 8
    rest = arrived.shape[1] - 2 * size

    def lay(col, carry):
        from_low[col] = below[col]
        from_high[(TILE_ROWS - 1) * band_cols + col] = above[col]
        for row in range(1, TILE_ROWS):
            from_low[row * band_cols + col] = arrived[slot_of[(row - 1) * band_cols + col], pl.ds(size, size), :]
            from_high[(row - 1) * band_cols + col] = arrived[slot_of[row * band_cols + col], pl.ds(0, size), :]
        return carry

    lax.fori_loop(0, band_cols, lay, 0)
    half = odd[0]
    pick = 7 * half
    per_y = rest // 8
    me = odd[1]
    peers = out.shape[0] // (out.shape[0] // (band_cols // TILE_COLS))

    def send(d, carry):
        p = tile_at[d]
        row, col = p // band_cols, p % band_cols
        right, left = (col + 1) % band_cols, (col + band_cols - 1) % band_cols
        out[d, pl.ds(0, size), :] = from_high[p]
        out[d, pl.ds(size, size), :] = from_low[p]
        slot_right = slot_of[row * band_cols + right]
        slot_left = slot_of[row * band_cols + left]
        for q in range(per_y):
            is_low = q * peers + me < HALVES
            slot = jnp.where(is_low, slot_right, slot_left)
            out[d, pl.ds(2 * size + q * 8, 8), :] = arrived[slot, pl.ds(2 * size + q * 8, 8), :]
        beside = row * band_cols + jnp.where(half == 0, right, left)
        for q in range(per_x):
            out[d, pl.ds(2 * size + rest + q, 1), :] = from_high[beside, pl.ds(q * 8 + pick, 1), :]
            out[d, pl.ds(2 * size + rest + per_x + q, 1), :] = from_low[beside, pl.ds(q * 8 + pick, 1), :]
        return carry

    lax.fori_loop(0, out.shape[0], send, 0)


def step_tile(peers, ids, pops, charge, mask, frame, rims, out, charge_out,
              near, flags, relaxed, rim, conc, vx, vy, vz):
    per_x, per_y = unit_counts(peers)
    places = unit_places(peers)
    corner_row = (2 * per_x + per_y) * 8

    for a in range(FRAME):
        near[a, pl.ds(SIDE - RING, FRAME), :] = frame[0, pl.ds(a * FRAME, FRAME), :]
    for i in range(EDGE + 2):
        row = mask[0, i]
        flags[1, i, pl.ds(SIDE - 1, EDGE + 2), :] = row
        flags[2, i, pl.ds(SIDE - 1, EDGE + 2), :] = pltpu.roll(row, 1, 1)
        flags[0, i, pl.ds(SIDE - 1, EDGE + 2), :] = pltpu.roll(row, DEPTH - 1, 1)

    def field_of(x_low, x_high, y_low, y_high, here):
        return [
            0.5 * (x_low - x_high),
            0.5 * (y_low - y_high),
            0.5 * (pltpu.roll(here, 1, 1) - pltpu.roll(here, DEPTH - 1, 1)),
        ]

    for face, layer in ((1, 0), (0, EDGE + 1)):
        for channel in range(CHANNELS):
            for half in range(2):
                peer, row = places[face, channel, half]
                rim[channel, pl.ds(SIDE + 8 * half, 8), :] = rims[peer, 0, pl.ds(row, 8), :]
                corner = corner_row + row // 8
                column = SIDE + EDGE if half == 0 else SIDE - 1
                rim[channel, pl.ds(column, 1), :] = rims[peer, 0, pl.ds(corner, 1), :]
        here = near[layer + 1]
        field = field_of(near[layer], near[layer + 2], pltpu.roll(here, 1, 0), pltpu.roll(here, PADDED - 1, 0), here)
        density, momentum, held = rim[5], [rim[6], rim[7], rim[8]], rim[9]
        force = [held * f for f in field]
        dirs = crossing(*FACES[face])
        done, velocity = collide({q: rim[n] for n, q in enumerate(dirs)}, density, momentum, force)
        for q in dirs:
            relaxed[q, layer] = done[q]
        conc[layer] = held
        vx[layer] = velocity[0]

    flat_near = near.reshape(FRAME * PADDED, DEPTH)
    flat_relaxed = relaxed.reshape(19, (EDGE + 2) * PADDED, DEPTH)
    flat_conc = conc.reshape((EDGE + 2) * PADDED, DEPTH)
    flat_vy = vy.reshape((EDGE + 2) * PADDED, DEPTH)
    for face, column in ((3, SIDE - 1), (2, SIDE + EDGE)):
        for half in range(2):
            def at(row, col):
                return flat_near[pl.ds((RING + 8 * half + row) * PADDED + col, 8, stride=PADDED), :]

            raw = [rims[places[face, c, half][0], 0, pl.ds(places[face, c, half][1], 8), :] for c in range(CHANNELS)]
            field = field_of(at(-1, column), at(1, column), at(0, column - 1), at(0, column + 1), at(0, column))
            force = [raw[9] * f for f in field]
            dirs = crossing(*FACES[face])
            done, velocity = collide({q: raw[n] for n, q in enumerate(dirs)}, raw[5], raw[6:9], force)
            target = pl.ds((1 + 8 * half) * PADDED + column, 8, stride=PADDED)
            for q in dirs:
                flat_relaxed[q, target, :] = done[q]
            flat_conc[target, :] = raw[9]
            flat_vy[target, :] = velocity[1]

    def relax_row(i, carry):
        for half in range(2):
            cells = pl.ds(pl.multiple_of(i * EDGE + 8 * half, 8), 8)
            base = SIDE + 8 * half
            field = field_of(
                near[i + RING - 1, pl.ds(base, 8), :], near[i + RING + 1, pl.ds(base, 8), :],
                near[i + RING, pl.ds(base - 1, 8), :], near[i + RING, pl.ds(base + 1, 8), :],
                near[i + RING, pl.ds(base, 8), :],
            )
            values = [pops[q, 0, cells, :] for q in range(19)]
            held = charge[0, cells, :]
            force = [held * f for f in field]
            density, momentum = moments(values)
            done, velocity = collide(dict(enumerate(values)), density, momentum, force)
            for q in range(19):
                relaxed[q, i + 1, pl.ds(base, 8), :] = done[q]
            conc[i + 1, pl.ds(base, 8), :] = held
            vx[i + 1, pl.ds(base, 8), :] = velocity[0]
            vy[i + 1, pl.ds(base, 8), :] = velocity[1]
            vz[i + 1, pl.ds(base, 8), :] = velocity[2]
        return carry

    lax.fori_loop(0, EDGE, relax_row, 0)

    def flux(speed_a, speed_b, a, b, flag_a, flag_b):
        face = 0.5 * (speed_a + speed_b)
        return jnp.where((flag_a == 1) & (flag_b == 1), face * jnp.where(face > 0, a, b), 0.0)

    def stream_row(i, carry):
        for half in range(2):
            cells = pl.ds(pl.multiple_of(i * EDGE + 8 * half, 8), 8)
            base = SIDE + 8 * half
            here = i + 1
            mid = pl.ds(base, 8)
            own = flags[1, here, mid, :] == 1
            for q in range(19):
                cx, cy, cz = LATTICE[q]
                from_columns = pl.ds(base - cy, 8)
                pulled = relaxed[q, here - cx, from_columns, :]
                if cz:
                    pulled = pltpu.roll(pulled, cz % DEPTH, 1)
                if q:
                    open_side = flags[cz + 1, here - cx, from_columns, :] == 1
                    pulled = jnp.where(open_side, pulled, relaxed[opposite(q), here, mid, :])
                out[q, 0, cells, :] = jnp.where(own, pulled, pops[q, 0, cells, :])
            held = conc[here, mid, :]
            flag = flags[1, here, mid, :]
            change = flux(vx[here, mid, :], vx[here + 1, mid, :], held, conc[here + 1, mid, :],
                          flag, flags[1, here + 1, mid, :])
            change = change - flux(vx[here - 1, mid, :], vx[here, mid, :], conc[here - 1, mid, :], held,
                                   flags[1, here - 1, mid, :], flag)
            low, high = pl.ds(base - 1, 8), pl.ds(base + 1, 8)
            change = change + flux(vy[here, mid, :], vy[here, high, :], held, conc[here, high, :],
                                   flag, flags[1, here, high, :])
            change = change - flux(vy[here, low, :], vy[here, mid, :], conc[here, low, :], held,
                                   flags[1, here, low, :], flag)
            speed = vz[here, mid, :]
            z_flux = flux(speed, pltpu.roll(speed, DEPTH - 1, 1), held, pltpu.roll(held, DEPTH - 1, 1),
                          flag, flags[0, here, mid, :])
            change = change + (z_flux - pltpu.roll(z_flux, 1, 1))
            charge_out[0, cells, :] = jnp.where(own, held - change, held)
        return carry

    lax.fori_loop(0, EDGE, stream_row, 0)


def per_device(populations, charge, fluid_mask, tile_ids, phase_label, permittivity):
    peers = lax.axis_size("gy")
    tiles = charge.shape[0]
    rows, cols = phase_label.shape[0], phase_label.shape[1]
    band_cols = TILE_COLS * peers
    band = peers * tiles
    per_x, per_y = unit_counts(peers)
    out_rows = (2 * per_x + per_y) * 8
    in_rows = out_rows + -(-2 * per_x // 8) * 8
    f32 = jnp.float32
    shape = jax.ShapeDtypeStruct
    gx_up, gx_down = ring_pairs("gx")
    gy_up, gy_down = ring_pairs("gy")
    me = lax.axis_index("gy").astype(jnp.int32)
    pops = populations.reshape(19, tiles, AREA, DEPTH)
    held = charge.reshape(tiles, AREA, DEPTH)

    outgoing = pl.pallas_call(
        functools.partial(pack_source, tiles, band_cols),
        out_shape=shape((peers, AREA + 8, DEPTH), f32),
        in_specs=[SMEM, VMEM, VMEM], out_specs=VMEM, compiler_params=PARAMS, name="pack_source",
    )(tile_ids, held, fluid_mask)
    arrived = lax.all_to_all(outgoing, "gy", split_axis=0, concat_axis=0, tiled=True)

    tile_at = arrived[:, AREA, :tiles].astype(jnp.int32).reshape(band)
    slots = jnp.arange(band, dtype=jnp.int32)
    slot_of = jnp.sum(jnp.where(tile_at[None, :] == slots[:, None], slots[None, :], 0), axis=1)
    local = jnp.arange(tiles, dtype=jnp.int32)
    mine = local // TILE_COLS * band_cols + TILE_COLS * me + local % TILE_COLS
    hold = jnp.sum(jnp.where(tile_at[None, :] == mine[:, None], slots[None, :] // tiles, 0), axis=1)

    before = lax.ppermute(phase_label[:, cols - SIDE :], "gy", gy_up)
    after = lax.ppermute(phase_label[:, :SIDE], "gy", gy_down)
    labels = jnp.concatenate([before, phase_label, after], axis=1)
    before = lax.ppermute(labels[rows - WIDER :], "gx", gx_up)
    after = lax.ppermute(labels[:WIDER], "gx", gx_down)
    wide = shape((rows + 2 * WIDER, cols + 2 * SIDE, DEPTH), f32)
    scratch = pltpu.VMEM(wide.shape, f32)
    weights = pl.pallas_call(
        face_weights, out_shape=[wide] * 4, in_specs=[SMEM, VMEM, VMEM, VMEM], out_specs=[VMEM] * 4,
        scratch_shapes=[scratch], compiler_params=PARAMS, name="face_weights",
    )(permittivity, labels, before, after)

    raw = pl.pallas_call(
        functools.partial(raw_faces, peers),
        grid=(tiles,),
        out_shape=shape((peers, tiles, out_rows, DEPTH), f32),
        in_specs=[
            pl.BlockSpec((19, 1, AREA, DEPTH), lambda t: (0, t, 0, 0)),
            pl.BlockSpec((1, AREA, DEPTH), lambda t: (t, 0, 0)),
        ],
        out_specs=pl.BlockSpec((peers, 1, out_rows, DEPTH), lambda t: (0, t, 0, 0)),
        compiler_params=PARAMS, name="raw_faces",
    )(pops, held)
    faces = lax.all_to_all(raw, "gy", split_axis=0, concat_axis=0, tiled=True).reshape(band, out_rows, DEPTH)
    strip = shape((band_cols, per_x * 8, DEPTH), f32)
    low, high = pl.pallas_call(
        functools.partial(outer_rows, band_cols, per_x),
        out_shape=[strip, strip], in_specs=[SMEM, VMEM], out_specs=[VMEM, VMEM],
        compiler_params=PARAMS, name="outer_rows",
    )(slot_of, faces)
    below = lax.ppermute(high, "gx", gx_up)
    above = lax.ppermute(low, "gx", gx_down)
    table = pltpu.VMEM((band, per_x * 8, DEPTH), f32)
    turned = pl.pallas_call(
        functools.partial(turn_faces, band_cols, per_x),
        out_shape=shape((band, in_rows, DEPTH), f32),
        in_specs=[SMEM, SMEM, SMEM, VMEM, VMEM, VMEM], out_specs=VMEM,
        scratch_shapes=[table, table], compiler_params=PARAMS, name="turn_faces",
    )(slot_of, tile_at, jnp.stack([me % 2, me]), faces, below, above)
    rims = lax.all_to_all(turned.reshape(peers, tiles, in_rows, DEPTH), "gy", split_axis=0, concat_axis=0, tiled=True)

    block, left, right = pl.pallas_call(
        assemble,
        out_shape=[shape((rows, cols, DEPTH), f32), shape((rows, SIDE, DEPTH), f32), shape((rows, SIDE, DEPTH), f32)],
        in_specs=[SMEM, VMEM], out_specs=[VMEM] * 3, compiler_params=PARAMS, name="assemble",
    )(hold, arrived)
    before = lax.ppermute(right, "gy", gy_up)
    after = lax.ppermute(left, "gy", gy_down)
    middle = jnp.concatenate([before, block, after], axis=1)
    before = lax.ppermute(middle[rows - WIDE :], "gx", gx_up)
    after = lax.ppermute(middle[:WIDE], "gx", gx_down)
    potential, frames = pl.pallas_call(
        solve,
        out_shape=[shape((rows, cols, DEPTH), f32), shape((peers, FRAME * FRAME, DEPTH), f32)],
        in_specs=[SMEM] + [VMEM] * 7, out_specs=[VMEM, VMEM],
        scratch_shapes=[scratch] * 4, compiler_params=PARAMS, name="solve",
    )(hold, middle, before, after, *weights)
    frames = lax.all_to_all(frames, "gy", split_axis=0, concat_axis=0, tiled=True)

    padded = pltpu.VMEM((EDGE + 2, PADDED, DEPTH), f32)
    by_tile = lambda t, ids: (t, 0, 0)
    populations_next, charge_next = pl.pallas_call(
        functools.partial(step_tile, peers),
        grid_spec=pltpu.PrefetchScalarGridSpec(
            num_scalar_prefetch=1,
            grid=(tiles,),
            in_specs=[
                pl.BlockSpec((19, 1, AREA, DEPTH), lambda t, ids: (0, t, 0, 0)),
                pl.BlockSpec((1, AREA, DEPTH), by_tile),
                pl.BlockSpec((1, EDGE + 2, EDGE + 2, DEPTH), lambda t, ids: (t, 0, 0, 0)),
                pl.BlockSpec((1, FRAME * FRAME, DEPTH), lambda t, ids: (ids[t] % band_cols // TILE_COLS, 0, 0)),
                pl.BlockSpec((peers, 1, in_rows, DEPTH), lambda t, ids: (0, t, 0, 0)),
            ],
            out_specs=[
                pl.BlockSpec((19, 1, AREA, DEPTH), lambda t, ids: (0, t, 0, 0)),
                pl.BlockSpec((1, AREA, DEPTH), by_tile),
            ],
            scratch_shapes=[
                pltpu.VMEM((FRAME, PADDED, DEPTH), f32),
                pltpu.VMEM((3, EDGE + 2, PADDED, DEPTH), jnp.int32),
                pltpu.VMEM((19, EDGE + 2, PADDED, DEPTH), f32),
                pltpu.VMEM((CHANNELS, PADDED, DEPTH), f32),
                padded, padded, padded, padded,
            ],
        ),
        out_shape=[shape(pops.shape, f32), shape(held.shape, f32)],
        compiler_params=PARAMS, name="step_tile",
    )(tile_ids, pops, held, fluid_mask, frames, rims)
    return (populations_next.reshape(populations.shape), charge_next.reshape(charge.shape), potential)


def solution(mesh):
    placed = (
        P(None, ("gx", "gy"), None, None, None),
        P(("gx", "gy"), None, None, None),
        P(("gx", "gy"), None, None, None),
        P(("gx", "gy")),
        P("gx", "gy", None),
        P(),
    )
    return jax.shard_map(
        per_device,
        mesh=mesh,
        in_specs=placed,
        out_specs=(
            P(None, ("gx", "gy"), None, None, None),
            P(("gx", "gy"), None, None, None),
            P("gx", "gy", None),
        ),
        check_vma=False,
    )
```

```python
import functools

import jax
import jax.numpy as jnp
from jax import lax
from jax.experimental import pallas as pl
from jax.experimental.pallas import tpu as pltpu
from jax.sharding import PartitionSpec as P

EDGE = 16
DEPTH = 128
TILE_ROWS = 2
TILE_COLS = 2
PHASES = 4
SWEEPS = 4

LATTICE = (
    (0, 0, 0),
    (1, 0, 0),
    (-1, 0, 0),
    (0, 1, 0),
    (0, -1, 0),
    (0, 0, 1),
    (0, 0, -1),
    (1, 1, 0),
    (-1, -1, 0),
    (1, -1, 0),
    (-1, 1, 0),
    (1, 0, 1),
    (-1, 0, -1),
    (1, 0, -1),
    (-1, 0, 1),
    (0, 1, 1),
    (0, -1, -1),
    (0, 1, -1),
    (0, -1, 1),
)
relax_time = 0.8
screening = 0.001
spectrum_low = 0.1
spectrum_high = 2.0

AREA = EDGE * EDGE
SIDE = 8
RING = 2
WIDE = RING + SWEEPS - 1
WIDER = WIDE + 1
FRAME = EDGE + 2 * RING
PADDED = EDGE + 2 * SIDE
CHANNELS = 10
HALVES = 2 * CHANNELS
VMEM = pl.BlockSpec(memory_space=pltpu.VMEM)
SMEM = pl.BlockSpec(memory_space=pltpu.SMEM)


def room(mebibytes):
    return pltpu.CompilerParams(vmem_limit_bytes=mebibytes * 2**20)


def crossing(axis_index, face_sign):
    return [q for q in range(19) if LATTICE[q][axis_index] == face_sign]


def opposite(direction):
    return LATTICE.index(tuple(-entry for entry in LATTICE[direction]))


def lattice_weight(direction):
    return (1.0 / 3.0, 1.0 / 18.0, 1.0 / 36.0)[sum(abs(e) for e in LATTICE[direction])]


def along(direction, vector):
    total = None
    for entry, part in zip(LATTICE[direction], vector):
        if entry:
            term = part if entry > 0 else -part
            total = term if total is None else total + term
    return total


def moments(pops):
    density = pops[0]
    for q in range(1, 19):
        density = density + pops[q]
    momentum = []
    for axis in range(3):
        plus = sum_of([pops[q] for q in crossing(axis, 1)])
        minus = sum_of([pops[q] for q in crossing(axis, -1)])
        momentum.append(plus - minus)
    return density, momentum


def sum_of(values):
    total = values[0]
    for value in values[1:]:
        total = total + value
    return total


def collide(pops, density, momentum, force):
    source_scale = 1.0 - 0.5 / relax_time
    gain = 1.0 / relax_time
    inverse = 1.0 / density
    carried = [m + 0.5 * f for m, f in zip(momentum, force)]
    velocity = [c * inverse for c in carried]
    energy = sum_of([c * v for c, v in zip(carried, velocity)])
    power = sum_of([v * f for v, f in zip(velocity, force)])
    base = gain * density - (1.5 * gain) * energy - (3.0 * source_scale) * power
    relaxed = {}
    for q in pops:
        weight = lattice_weight(q)
        kept = (1.0 - gain) * pops[q]
        if q == 0:
            relaxed[q] = kept + weight * base
            continue
        if q in relaxed:
            continue
        p, g, rp = along(q, velocity), along(q, force), along(q, carried)
        even = weight * base + p * ((4.5 * gain * weight) * rp + (9.0 * source_scale * weight) * g)
        odd = (3.0 * gain * weight) * rp + (3.0 * source_scale * weight) * g
        relaxed[q] = kept + (even + odd)
        back = opposite(q)
        if back in pops:
            relaxed[back] = (1.0 - gain) * pops[back] + (even - odd)
    return relaxed, velocity


def ring_pairs(axis):
    size = lax.axis_size(axis)
    up = [(i, (i + 1) % size) for i in range(size)]
    return up, [(j, i) for i, j in up]


def pack_source(tiles, band_cols, ids, charge, mask, out):
    out[...] = jnp.zeros_like(out)
    lane = lax.broadcasted_iota(jnp.int32, (8, DEPTH), 1)
    header = jnp.zeros((8, DEPTH), jnp.int32)
    for t in range(tiles):
        owner = ids[t] % band_cols // TILE_COLS
        header = jnp.where(lane == t, ids[t], header)
        for i in range(EDGE):
            flags = mask[t, i + 1, 1 : EDGE + 1, :].astype(jnp.float32)
            out[owner, pl.ds(i * EDGE, EDGE), :] = charge[t, pl.ds(i * EDGE, EDGE), :] * flags
    for peer in range(out.shape[0]):
        out[peer, pl.ds(AREA, 8), :] = header.astype(jnp.float32)


def assemble(band, tiles, slot_of, arrived, block, left, right):
    for local in range(TILE_ROWS * TILE_COLS):
        r, c = local // TILE_COLS, local % TILE_COLS
        slot = slot_of[band + local] // tiles
        for i in range(EDGE):
            row = r * EDGE + i
            cells = arrived[slot, pl.ds(i * EDGE, EDGE), :]
            block[row, pl.ds(c * EDGE, EDGE), :] = cells
            if c == 0:
                left[row] = cells[:SIDE]
            if c == TILE_COLS - 1:
                right[row] = cells[EDGE - SIDE :]


def tick(_, out):
    out[...] = jnp.zeros_like(out)


def edge_rows(block, left, right, ups, downs):
    rows = block.shape[0]
    for row in range(WIDE):
        low = rows - WIDE + row
        ups[row] = jnp.concatenate([left[low], block[low], right[low]], axis=0)
        downs[row] = jnp.concatenate([left[row], block[row], right[row]], axis=0)


def harmonic(a, b):
    return 2.0 * a * b / (a + b)


def face_weights(table, labels, before, after, left, right, wx, wy, wz, inverse, permit):
    rows = labels.shape[0]
    total = rows + 2 * WIDER

    def look(label):
        value = jnp.full(label.shape, table[PHASES - 1], jnp.float32)
        for phase in range(PHASES - 1):
            value = jnp.where(label == phase, table[phase], value)
        return value

    for row in range(WIDER):
        low, high = row, WIDER + rows + row
        permit[low] = look(jnp.concatenate([left[low], before[row], right[low]], axis=0))
        permit[high] = look(jnp.concatenate([left[high], after[row], right[high]], axis=0))

    def fill(row, carry):
        row = WIDER + row
        permit[row] = look(jnp.concatenate([left[row], labels[row - WIDER], right[row]], axis=0))
        return carry

    lax.fori_loop(0, rows, fill, 0, unroll=2)
    width = permit.shape[1]
    wx[0] = harmonic(permit[0], permit[1])

    def weigh(row, carry):
        here = permit[row]
        x_plus = harmonic(here, permit[row + 1])
        y_plus = harmonic(here, pltpu.roll(here, width - 1, 0))
        z_plus = harmonic(here, pltpu.roll(here, DEPTH - 1, 1))
        wx[row] = x_plus
        wy[row] = y_plus
        wz[row] = z_plus
        diagonal = x_plus + wx[row - 1] + y_plus + pltpu.roll(y_plus, 1, 0)
        diagonal = diagonal + z_plus + pltpu.roll(z_plus, 1, 1) + screening
        inverse[row] = 1.0 / diagonal
        return carry

    lax.fori_loop(1, total - 1, weigh, 0, unroll=6)


def solve(band, tiles, slot_of, middle, left, right, before, after, wx, wy, wz, inverse, _, out, frames, u0, u1, residual, potential):
    rows, width = middle.shape[0], wx.shape[1]
    center_value = 0.5 * (spectrum_high + spectrum_low)
    half_width = 0.5 * (spectrum_high - spectrum_low)
    ratio = center_value / half_width

    def start(row, source):
        r = source * inverse[row]
        residual[row] = r
        u = r * (1.0 / center_value)
        u0[row] = u
        potential[row] = u

    for row in range(WIDE):
        start(1 + row, before[row])
        start(1 + WIDE + rows + row, after[row])

    def begin(row, carry):
        start(1 + WIDE + row, jnp.concatenate([left[row], middle[row], right[row]], axis=0))
        return carry

    lax.fori_loop(0, rows, begin, 0, unroll=2)
    old, new = u0, u1
    rho = 1.0 / ratio
    for sweep in range(1, SWEEPS):
        rho_new = 1.0 / (2.0 * ratio - rho)
        a, b = rho_new * rho, 2.0 * rho_new / half_width
        last = sweep == SWEEPS - 1

        def step(row, carry):
            u = old[row]
            y_weight, z_weight = wy[row], wz[row]
            spread = wx[row] * old[row + 1] + wx[row - 1] * old[row - 1]
            spread = spread + y_weight * pltpu.roll(u, width - 1, 0) + pltpu.roll(y_weight * u, 1, 0)
            spread = spread + z_weight * pltpu.roll(u, DEPTH - 1, 1) + pltpu.roll(z_weight * u, 1, 1)
            r = residual[row] - u + inverse[row] * spread
            u = a * u + b * r
            potential[row] = potential[row] + u
            if not last:
                residual[row] = r
                new[row] = u
            return carry

        lax.fori_loop(1 + sweep, rows + 2 * WIDER - 1 - sweep, step, 0, unroll=4)
        old, new = new, old
        rho = rho_new
    inner = width - 2 * SIDE

    def give(row, carry):
        out[row] = potential[WIDER + row, pl.ds(SIDE, inner), :]
        return carry

    lax.fori_loop(0, rows, give, 0, unroll=2)
    frames[...] = jnp.zeros_like(frames)
    for local in range(TILE_ROWS * TILE_COLS):
        r, c = local // TILE_COLS, local % TILE_COLS
        slot = slot_of[band + local] // tiles
        for a in range(FRAME):
            frames[slot, pl.ds(a * FRAME, FRAME), :] = potential[
                WIDER + r * EDGE - RING + a, pl.ds(SIDE + c * EDGE - RING, FRAME), :
            ]


def unit_counts(peers):
    per_x = -(-HALVES // peers)
    per_y = -(-2 * HALVES // peers)
    return per_x, per_y


def unit_places(peers):
    per_x, per_y = unit_counts(peers)
    places = {}
    for unit in range(HALVES):
        for face in range(2):
            places[face, unit // 2, unit % 2] = (unit % peers, (face * per_x + unit // peers) * 8)
    for unit in range(2 * HALVES):
        face, rest = 2 + unit // HALVES, unit % HALVES
        places[face, rest // 2, rest % 2] = (unit % peers, (2 * per_x + unit // peers) * 8)
    return places


FACES = ((0, -1), (0, 1), (1, -1), (1, 1))


def open_sides(mask, bits, flags):
    column = lax.broadcasted_iota(jnp.int32, (EDGE + 2, DEPTH), 0)
    inner = (column > 0) & (column < EDGE + 1)
    for i in range(EDGE + 2):
        row = jnp.where(inner, mask[0, i], 0) if 0 < i < EDGE + 1 else jnp.zeros((EDGE + 2, DEPTH), jnp.int32)
        flags[1, i, pl.ds(SIDE - 1, EDGE + 2), :] = row
        flags[2, i, pl.ds(SIDE - 1, EDGE + 2), :] = pltpu.roll(row, 1, 1)
        flags[0, i, pl.ds(SIDE - 1, EDGE + 2), :] = pltpu.roll(row, DEPTH - 1, 1)

    def gather(i, carry):
        total = jnp.zeros((EDGE, DEPTH), jnp.int32)
        for q in range(19):
            cx, cy, cz = LATTICE[q]
            total = total + flags[cz + 1, i + 1 - cx, pl.ds(SIDE - cy, EDGE), :] * (1 << q)
        own = flags[1, i + 1, pl.ds(SIDE, EDGE), :]
        bits[0, pl.ds(pl.multiple_of(i * EDGE, EDGE), EDGE), :] = jnp.where(own == 1, total, 0)
        return carry

    lax.fori_loop(0, EDGE, gather, 0, unroll=4)


def raw_faces(peers, pops, charge, mask, out, bits, flags):
    open_sides(mask, bits, flags)
    places = unit_places(peers)
    taken = set(places.values())
    for peer in range(peers):
        for row in range(0, out.shape[2], 8):
            if (peer, row) not in taken:
                out[peer, 0, pl.ds(row, 8), :] = jnp.zeros((8, DEPTH), jnp.float32)
    for face, (axis, sign) in enumerate(FACES):
        layer = 0 if sign < 0 else EDGE - 1
        for half in range(2):
            if axis == 0:
                where = pl.ds(layer * EDGE + 8 * half, 8)
            else:
                where = pl.ds(8 * half * EDGE + layer, 8, stride=EDGE)
            values = [pops[q, 0, where, :] for q in range(19)]
            density, momentum = moments(values)
            channels = [values[q] for q in crossing(axis, sign)]
            channels += [density] + momentum + [charge[0, where, :]]
            for channel, value in enumerate(channels):
                peer, row = places[face, channel, half]
                out[peer, 0, pl.ds(row, 8), :] = value


def outer_rows(band_cols, per_x, slot_of, arrived, low, high):
    size = per_x * 8
    for col in range(band_cols):
        low[col] = arrived[slot_of[col], pl.ds(0, size), :]
        high[col] = arrived[slot_of[(TILE_ROWS - 1) * band_cols + col], pl.ds(size, size), :]


def turn_faces(band_cols, per_x, slot_of, tile_at, odd, arrived, below, above, out, from_low, from_high):
    size = per_x * 8
    rest = arrived.shape[1] - 2 * size

    def lay(col, carry):
        from_low[col] = below[col]
        from_high[(TILE_ROWS - 1) * band_cols + col] = above[col]
        for row in range(1, TILE_ROWS):
            from_low[row * band_cols + col] = arrived[slot_of[(row - 1) * band_cols + col], pl.ds(size, size), :]
            from_high[(row - 1) * band_cols + col] = arrived[slot_of[row * band_cols + col], pl.ds(0, size), :]
        return carry

    lax.fori_loop(0, band_cols, lay, 0)
    half = odd[0]
    pick = 7 * half
    per_y = rest // 8
    me = odd[1]
    peers = out.shape[0] // (out.shape[0] // (band_cols // TILE_COLS))

    def send(d, carry):
        p = tile_at[d]
        row, col = p // band_cols, p % band_cols
        right, left = (col + 1) % band_cols, (col + band_cols - 1) % band_cols
        out[d, pl.ds(0, size), :] = from_high[p]
        out[d, pl.ds(size, size), :] = from_low[p]
        slot_right = slot_of[row * band_cols + right]
        slot_left = slot_of[row * band_cols + left]
        for q in range(per_y):
            is_low = q * peers + me < HALVES
            slot = jnp.where(is_low, slot_right, slot_left)
            out[d, pl.ds(2 * size + q * 8, 8), :] = arrived[slot, pl.ds(2 * size + q * 8, 8), :]
        beside = row * band_cols + jnp.where(half == 0, right, left)
        for q in range(per_x):
            out[d, pl.ds(2 * size + rest + q, 1), :] = from_high[beside, pl.ds(q * 8 + pick, 1), :]
            out[d, pl.ds(2 * size + rest + per_x + q, 1), :] = from_low[beside, pl.ds(q * 8 + pick, 1), :]
        return carry

    lax.fori_loop(0, out.shape[0], send, 0)


ACROSS_X = [q for q in range(19) if LATTICE[q][0]]
ACROSS_Y = [q for q in range(19) if LATTICE[q][1]]


def field_of(x_low, x_high, y_low, y_high, here):
    return [
        0.5 * (x_low - x_high),
        0.5 * (y_low - y_high),
        0.5 * (pltpu.roll(here, 1, 1) - pltpu.roll(here, DEPTH - 1, 1)),
    ]


def flux(speed_a, speed_b, a, b, flag_a, flag_b):
    face = 0.5 * (speed_a + speed_b)
    return jnp.where((flag_a == 1) & (flag_b == 1), face * jnp.where(face > 0, a, b), 0.0)


def step_inside(ids, pops, charge, bits, frame, out, charge_out, edges, bands, lines, near, relaxed, conc, vx, vy, vz):
    for a in range(FRAME):
        near[a, pl.ds(SIDE - RING, FRAME), :] = frame[0, pl.ds(a * FRAME, FRAME), :]

    def relax_row(i, carry):
        cells = pl.ds(pl.multiple_of(i * EDGE, EDGE), EDGE)
        field = field_of(
            near[i + RING - 1, pl.ds(SIDE, EDGE), :], near[i + RING + 1, pl.ds(SIDE, EDGE), :],
            near[i + RING, pl.ds(SIDE - 1, EDGE), :], near[i + RING, pl.ds(SIDE + 1, EDGE), :],
            near[i + RING, pl.ds(SIDE, EDGE), :],
        )
        values = [pops[q, 0, cells, :] for q in range(19)]
        held = charge[0, cells, :]
        force = [held * f for f in field]
        density, momentum = moments(values)
        done, velocity = collide(dict(enumerate(values)), density, momentum, force)
        for q in range(19):
            relaxed[q, i + 1, pl.ds(SIDE, EDGE), :] = done[q]
        conc[i + 1, pl.ds(SIDE, EDGE), :] = held
        vx[i + 1, pl.ds(SIDE, EDGE), :] = velocity[0]
        vy[i + 1, pl.ds(SIDE, EDGE), :] = velocity[1]
        vz[i + 1, pl.ds(SIDE, EDGE), :] = velocity[2]
        return carry

    lax.fori_loop(0, EDGE, relax_row, 0, unroll=4)
    flat_vy = vy.reshape((EDGE + 2) * PADDED, DEPTH)
    edges[0, 0] = vx[1, pl.ds(SIDE, EDGE), :]
    edges[0, 1] = vx[EDGE, pl.ds(SIDE, EDGE), :]
    edges[0, 2] = flat_vy[pl.ds(PADDED + SIDE, EDGE, stride=PADDED), :]
    edges[0, 3] = flat_vy[pl.ds(PADDED + SIDE + EDGE - 1, EDGE, stride=PADDED), :]

    def stream_row(i, carry):
        cells = pl.ds(pl.multiple_of(i * EDGE, EDGE), EDGE)
        here = i + 1
        mid = pl.ds(SIDE, EDGE)
        bit = bits[0, cells, :]
        is_open = [(bit & (1 << q)) != 0 for q in range(19)]
        for q in range(19):
            cx, cy, cz = LATTICE[q]
            pulled = relaxed[q, here - cx, pl.ds(SIDE - cy, EDGE), :]
            if cz:
                pulled = pltpu.roll(pulled, cz % DEPTH, 1)
            kept = pops[q, 0, cells, :]
            if q:
                kept = jnp.where(is_open[0], relaxed[opposite(q), here, mid, :], kept)
            out[q, 0, cells, :] = jnp.where(is_open[q], pulled, kept)
        held = conc[here, mid, :]

        def through(q, speed_a, speed_b, a, b):
            face = 0.5 * (speed_a + speed_b)
            return jnp.where(is_open[q], face * jnp.where(face > 0, a, b), 0.0)

        change = through(2, vx[here, mid, :], vx[here + 1, mid, :], held, conc[here + 1, mid, :])
        change = change - through(1, vx[here - 1, mid, :], vx[here, mid, :], conc[here - 1, mid, :], held)
        low, high = pl.ds(SIDE - 1, EDGE), pl.ds(SIDE + 1, EDGE)
        change = change + through(4, vy[here, mid, :], vy[here, high, :], held, conc[here, high, :])
        change = change - through(3, vy[here, low, :], vy[here, mid, :], conc[here, low, :], held)
        speed = vz[here, mid, :]
        z_flux = through(6, speed, pltpu.roll(speed, DEPTH - 1, 1), held, pltpu.roll(held, DEPTH - 1, 1))
        change = change + (z_flux - pltpu.roll(z_flux, 1, 1))
        charge_out[0, cells, :] = held - change
        return carry

    lax.fori_loop(0, EDGE, stream_row, 0, unroll=4)
    for n, q in enumerate(ACROSS_Y):
        first = 0 if LATTICE[q][1] > 0 else EDGE - 8
        for row in range(EDGE):
            bands[0, n, row] = out[q, 0, pl.ds(row * EDGE + first, 8), :]
    for n, q in enumerate(ACROSS_X):
        lines[0, n] = out[q, 0, pl.ds(0 if LATTICE[q][0] > 0 else AREA - EDGE, EDGE), :]


def step_faces(peers, tiles, band_cols, ids, charge, mask, frames, rims, edges, bands, lines, charge_in, _,
               charge_out, out, all_near, all_flags, all_rim, all_x, all_y, new_bands, new_lines, sems):
    per_x, per_y = unit_counts(peers)
    places = unit_places(peers)
    corner_row = (2 * per_x + per_y) * 8
    all_flat_near = all_near.reshape(tiles, FRAME * PADDED, DEPTH)
    all_flat_flags = all_flags.reshape(tiles, (EDGE + 2) * PADDED, DEPTH)
    flat_bands = new_bands.reshape(tiles, len(ACROSS_Y), EDGE * 8, DEPTH)

    def pieces(tile):
        made = []
        for n, q in enumerate(ACROSS_Y):
            first = 0 if LATTICE[q][1] > 0 else EDGE - 8
            made.append((new_bands.at[tile, n], out.at[q, tile, :, pl.ds(first, 8)]))
        for n, q in enumerate(ACROSS_X):
            layer = 0 if LATTICE[q][0] > 0 else EDGE - 1
            if LATTICE[q][1]:
                cells = pl.ds(8 if LATTICE[q][1] > 0 else 0, 8)
                made.append((new_lines.at[tile, n, cells], out.at[q, tile, layer, cells]))
            else:
                made.append((new_lines.at[tile, n], out.at[q, tile, layer]))
        return [pltpu.make_async_copy(a, b, sems.at[tile, n]) for n, (a, b) in enumerate(made)]

    def incoming(tile):
        return pltpu.make_async_copy(bands.at[tile], new_bands.at[tile], sems.at[tile, len(ACROSS_Y + ACROSS_X)])

    for tile in range(tiles):
        incoming(tile).start()

    def patch(t, carry):
        near, flags, rim, beside_x, beside_y = (x.at[t] for x in (all_near, all_flags, all_rim, all_x, all_y))
        flat_near, flat_flags = all_flat_near.at[t], all_flat_flags.at[t]
        owner = ids[t] % band_cols // TILE_COLS
        for a in range(FRAME):
            near[a, pl.ds(SIDE - RING, FRAME), :] = frames[owner, pl.ds(a * FRAME, FRAME), :]
        for i in range(EDGE + 2):
            flags[i, pl.ds(SIDE - 1, EDGE + 2), :] = mask[t, i]
        charge_out[t] = charge_in[t]
        incoming(t).wait()

        for side, face, layer in ((0, 1, 0), (1, 0, EDGE + 1)):
            for channel in range(CHANNELS):
                for half in range(2):
                    peer, row = places[face, channel, half]
                    rim[channel, pl.ds(SIDE + 8 * half, 8), :] = rims[peer, t, pl.ds(row, 8), :]
                    corner = corner_row + row // 8
                    column = SIDE + EDGE if half == 0 else SIDE - 1
                    rim[channel, pl.ds(column, 1), :] = rims[peer, t, pl.ds(corner, 1), :]
            here = near[layer + 1]
            field = field_of(
                near[layer], near[layer + 2], pltpu.roll(here, 1, 0), pltpu.roll(here, PADDED - 1, 0), here
            )
            density, momentum, held = rim[5], [rim[6], rim[7], rim[8]], rim[9]
            force = [held * f for f in field]
            dirs = crossing(*FACES[face])
            done, velocity = collide({q: rim[n] for n, q in enumerate(dirs)}, density, momentum, force)
            for n, q in enumerate(dirs):
                beside_x[side, n] = done[q]
            cells = pl.ds(0 if side == 0 else AREA - EDGE, EDGE)
            own_layer = 0 if side == 0 else EDGE - 1
            inner = slice(SIDE, SIDE + EDGE)
            speed, own_speed = velocity[0][inner], edges[t, side]
            amount, own_amount = held[inner], charge[t, cells, :]
            flag, own_flag = flags[layer, pl.ds(SIDE, EDGE), :], flags[own_layer + 1, pl.ds(SIDE, EDGE), :]
            if side == 0:
                charge_out[t, cells, :] += flux(speed, own_speed, amount, own_amount, flag, own_flag)
            else:
                charge_out[t, cells, :] -= flux(own_speed, speed, own_amount, amount, own_flag, flag)
            for n, q in enumerate(dirs):
                _, cy, cz = LATTICE[q]
                columns = pl.ds(SIDE - cy, EDGE)
                value, flag = beside_x[side, n, columns, :], flags[layer, columns, :]
                if cz:
                    value, flag = pltpu.roll(value, cz % DEPTH, 1), pltpu.roll(flag, cz % DEPTH, 1)
                line = ACROSS_X.index(q)
                taken = (flag == 1) & (own_flag == 1)
                merged = jnp.where(taken, value, lines[t, line])
                new_lines[t, line] = merged
                if cy:
                    new_bands[t, ACROSS_Y.index(q), own_layer] = merged[:8] if cy > 0 else merged[8:]

        for side, face, column in ((0, 3, SIDE - 1), (1, 2, SIDE + EDGE)):
            dirs = crossing(*FACES[face])
            x_dirs = [crossing(*FACES[1]), crossing(*FACES[0])]
            own_column = 0 if side == 0 else EDGE - 1
            for half in range(2):
                def at(row, col):
                    return flat_near[pl.ds((RING + 8 * half + row) * PADDED + col, 8, stride=PADDED), :]

                raw = [rims[places[face, c, half][0], t, pl.ds(places[face, c, half][1], 8), :]
                       for c in range(CHANNELS)]
                field = field_of(at(-1, column), at(1, column), at(0, column - 1), at(0, column + 1), at(0, column))
                force = [raw[9] * f for f in field]
                done, velocity = collide({q: raw[n] for n, q in enumerate(dirs)}, raw[5], raw[6:9], force)
                for n, q in enumerate(dirs):
                    beside_y[side, n, pl.ds(SIDE + 8 * half, 8), :] = done[q]
                cells = pl.ds(8 * half * EDGE + own_column, 8, stride=EDGE)
                own_flag = flat_flags[pl.ds((1 + 8 * half) * PADDED + SIDE + own_column, 8, stride=PADDED), :]
                flag = flat_flags[pl.ds((1 + 8 * half) * PADDED + column, 8, stride=PADDED), :]
                own_speed, own_amount = edges[t, 2 + side, pl.ds(8 * half, 8), :], charge[t, cells, :]
                if side == 0:
                    charge_out[t, cells, :] += flux(velocity[1], own_speed, raw[9], own_amount, flag, own_flag)
                else:
                    charge_out[t, cells, :] -= flux(own_speed, velocity[1], own_amount, raw[9], own_flag, flag)
            own_flag = flat_flags[pl.ds(PADDED + SIDE + own_column, EDGE, stride=PADDED), :]
            for n, q in enumerate(dirs):
                cx, _, cz = LATTICE[q]
                if cx:
                    end = 0 if cx > 0 else 1
                    row = SIDE - 1 if cx > 0 else SIDE + EDGE
                    beside_y[side, n, pl.ds(row, 1), :] = beside_x[end, x_dirs[end].index(q), pl.ds(column, 1), :]
                value = beside_y[side, n, pl.ds(SIDE - cx, EDGE), :]
                flag = flat_flags[pl.ds((1 - cx) * PADDED + column, EDGE, stride=PADDED), :]
                if cz:
                    value, flag = pltpu.roll(value, cz % DEPTH, 1), pltpu.roll(flag, cz % DEPTH, 1)
                band = ACROSS_Y.index(q)
                rows = pl.ds(own_column % 8, EDGE, stride=8)
                kept = flat_bands[t, band, rows, :]
                flat_bands[t, band, rows, :] = jnp.where((flag == 1) & (own_flag == 1), value, kept)
        for copy in pieces(t):
            copy.start()
        return carry

    lax.fori_loop(0, tiles, patch, 0, unroll=2)
    for tile in range(tiles):
        for copy in pieces(tile):
            copy.wait()


def per_device(populations, charge, fluid_mask, tile_ids, phase_label, permittivity):
    peers = lax.axis_size("gy")
    tiles = charge.shape[0]
    rows, cols = phase_label.shape[0], phase_label.shape[1]
    band_cols = TILE_COLS * peers
    band = peers * tiles
    per_x, per_y = unit_counts(peers)
    out_rows = (2 * per_x + per_y) * 8
    in_rows = out_rows + -(-2 * per_x // 8) * 8
    f32 = jnp.float32
    shape = jax.ShapeDtypeStruct
    gx_up, gx_down = ring_pairs("gx")
    gy_up, gy_down = ring_pairs("gy")
    me = lax.axis_index("gy").astype(jnp.int32)
    pops = pltpu.with_memory_space_constraint(populations.reshape(19, tiles, AREA, DEPTH), pltpu.HBM)
    held = charge.reshape(tiles, AREA, DEPTH)

    outgoing = pl.pallas_call(
        functools.partial(pack_source, tiles, band_cols),
        out_shape=pltpu.HBM((peers, AREA + 8, DEPTH), f32),
        in_specs=[SMEM, VMEM, VMEM], out_specs=VMEM, compiler_params=room(6), name="pack_source",
    )(tile_ids, held, fluid_mask)
    outgoing, phase_label = lax.optimization_barrier((outgoing, phase_label))
    arrived = lax.all_to_all(outgoing, "gy", split_axis=0, concat_axis=0, tiled=True)

    beside = [lax.ppermute(phase_label[rows - WIDER :], "gx", gx_up)]
    beside.append(lax.ppermute(phase_label[:WIDER], "gx", gx_down))
    beside = list(lax.optimization_barrier(tuple(beside)))
    tall = jnp.concatenate([beside[0][:, cols - SIDE :], phase_label[:, cols - SIDE :], beside[1][:, cols - SIDE :]])
    beside.append(lax.ppermute(tall, "gy", gy_up))
    tall = jnp.concatenate([beside[0][:, :SIDE], phase_label[:, :SIDE], beside[1][:, :SIDE]])
    beside.append(lax.ppermute(tall, "gy", gy_down))

    one_tile = pl.BlockSpec((1, AREA, DEPTH), lambda t: (t, 0, 0))
    raw, bits = pl.pallas_call(
        functools.partial(raw_faces, peers),
        grid=(tiles,),
        out_shape=[pltpu.HBM((peers, tiles, out_rows, DEPTH), f32), pltpu.HBM(held.shape, jnp.int32)],
        in_specs=[
            pl.BlockSpec((19, 1, AREA, DEPTH), lambda t: (0, t, 0, 0)),
            one_tile,
            pl.BlockSpec((1, EDGE + 2, EDGE + 2, DEPTH), lambda t: (t, 0, 0, 0)),
        ],
        out_specs=[pl.BlockSpec((peers, 1, out_rows, DEPTH), lambda t: (0, t, 0, 0)), one_tile],
        scratch_shapes=[pltpu.VMEM((3, EDGE + 2, PADDED, DEPTH), jnp.int32)],
        compiler_params=room(14), name="raw_faces",
    )(pops, held, fluid_mask)
    arrived, raw, beside = lax.optimization_barrier((arrived, raw, beside))
    beside = list(beside)

    tile_at = arrived[:, AREA, :tiles].astype(jnp.int32).reshape(band)
    slots = jnp.arange(band, dtype=jnp.int32)
    local = jnp.arange(tiles, dtype=jnp.int32)
    mine = local // TILE_COLS * band_cols + TILE_COLS * me + local % TILE_COLS
    wanted = jnp.concatenate([slots, mine])
    slot_of = jnp.sum(jnp.where(tile_at[None, :] == wanted[:, None], slots[None, :], 0), axis=1)

    block, left, right = pl.pallas_call(
        functools.partial(assemble, band, tiles),
        out_shape=[pltpu.VMEM((rows, cols, DEPTH), f32), shape((rows, SIDE, DEPTH), f32), shape((rows, SIDE, DEPTH), f32)],
        in_specs=[SMEM, VMEM], out_specs=[VMEM] * 3, compiler_params=room(5), name="assemble",
    )(slot_of, arrived)
    left, right = lax.ppermute(right, "gy", gy_up), lax.ppermute(left, "gy", gy_down)
    ends = shape((WIDE, cols + 2 * SIDE, DEPTH), f32)
    ups, downs = pl.pallas_call(
        edge_rows, out_shape=[ends, ends], in_specs=[VMEM] * 3, out_specs=[VMEM] * 2,
        compiler_params=room(3), name="edge_rows",
    )(block, left, right)
    ups, downs, beside[0] = lax.optimization_barrier((ups, downs, beside[0]))
    before, after = lax.ppermute(ups, "gx", gx_up), lax.ppermute(downs, "gx", gx_down)
    hbm = pl.BlockSpec(memory_space=pl.ANY)
    token = pl.pallas_call(
        tick, out_shape=shape((8, DEPTH), f32), in_specs=[hbm], out_specs=VMEM, compiler_params=room(1), name="tick"
    )(downs)
    raw, token = lax.optimization_barrier((raw, token))
    token, beside[0] = lax.optimization_barrier((token, beside[0]))
    wide = shape((rows + 2 * WIDER, cols + 2 * SIDE, DEPTH), f32)
    scratch = pltpu.VMEM(wide.shape, f32)
    weights = pl.pallas_call(
        face_weights, out_shape=[pltpu.VMEM(wide.shape, f32)] * 4, in_specs=[SMEM] + [VMEM] * 5, out_specs=[VMEM] * 4,
        scratch_shapes=[scratch], compiler_params=room(12), name="face_weights",
    )(permittivity, phase_label, *beside)

    faces = lax.all_to_all(raw, "gy", split_axis=0, concat_axis=0, tiled=True).reshape(band, out_rows, DEPTH)
    faces = pltpu.with_memory_space_constraint(faces, pltpu.HBM)
    potential, frames = pl.pallas_call(
        functools.partial(solve, band, tiles),
        out_shape=[shape((rows, cols, DEPTH), f32), pltpu.HBM((peers, FRAME * FRAME, DEPTH), f32)],
        in_specs=[SMEM] + [VMEM] * 9 + [hbm], out_specs=[VMEM, VMEM],
        scratch_shapes=[scratch] * 4, compiler_params=room(16), name="solve",
    )(slot_of, block, left, right, before, after, *weights, token)
    frames = lax.all_to_all(frames, "gy", split_axis=0, concat_axis=0, tiled=True)

    strip = shape((band_cols, per_x * 8, DEPTH), f32)
    low, high = pl.pallas_call(
        functools.partial(outer_rows, band_cols, per_x),
        out_shape=[strip, strip], in_specs=[SMEM, VMEM], out_specs=[VMEM] * 2,
        compiler_params=room(5), name="outer_rows",
    )(slot_of, faces)
    below = lax.ppermute(high, "gx", gx_up)
    above = lax.ppermute(low, "gx", gx_down)
    table = pltpu.VMEM((band, per_x * 8, DEPTH), f32)
    turned = pl.pallas_call(
        functools.partial(turn_faces, band_cols, per_x),
        out_shape=pltpu.HBM((band, in_rows, DEPTH), f32),
        in_specs=[SMEM, SMEM, SMEM, VMEM, VMEM, VMEM], out_specs=VMEM,
        scratch_shapes=[table, table], compiler_params=room(8), name="turn_faces",
    )(slot_of, tile_at, jnp.stack([me % 2, me]), faces, below, above)
    rims = lax.all_to_all(turned.reshape(peers, tiles, in_rows, DEPTH), "gy", split_axis=0, concat_axis=0, tiled=True)

    padded = pltpu.VMEM((EDGE + 2, PADDED, DEPTH), f32)
    near = pltpu.VMEM((FRAME, PADDED, DEPTH), f32)
    by_tile = pl.BlockSpec((1, AREA, DEPTH), lambda t, ids: (t, 0, 0))
    of_pops = pl.BlockSpec((19, 1, AREA, DEPTH), lambda t, ids: (0, t, 0, 0))
    of_frame = pl.BlockSpec((1, FRAME * FRAME, DEPTH), lambda t, ids: (ids[t] % band_cols // TILE_COLS, 0, 0))
    of_edges = pl.BlockSpec((1, 4, EDGE, DEPTH), lambda t, ids: (t, 0, 0, 0))
    bits = pltpu.with_memory_space_constraint(bits, pltpu.HBM)
    closed, closed_charge, edges, bands, lines = pl.pallas_call(
        step_inside,
        grid_spec=pltpu.PrefetchScalarGridSpec(
            num_scalar_prefetch=1,
            grid=(tiles,),
            in_specs=[of_pops, by_tile, by_tile, of_frame],
            out_specs=[
                of_pops, by_tile, of_edges,
                pl.BlockSpec((1, len(ACROSS_Y), EDGE, 8, DEPTH), lambda t, ids: (t, 0, 0, 0, 0)),
                pl.BlockSpec((1, len(ACROSS_X), EDGE, DEPTH), lambda t, ids: (t, 0, 0, 0)),
            ],
            scratch_shapes=[
                near,
                pltpu.VMEM((19, EDGE + 2, PADDED, DEPTH), f32),
                padded, padded, padded, padded,
            ],
        ),
        out_shape=[
            shape(pops.shape, f32), pltpu.HBM(held.shape, f32), shape((tiles, 4, EDGE, DEPTH), f32),
            pltpu.HBM((tiles, len(ACROSS_Y), EDGE, 8, DEPTH), f32),
            pltpu.HBM((tiles, len(ACROSS_X), EDGE, DEPTH), f32),
        ],
        compiler_params=room(24), name="step_inside",
    )(tile_ids, pops, held, bits, frames)
    bands, lines, closed_charge = (
        pltpu.with_memory_space_constraint(x, pltpu.HBM) for x in (bands, lines, closed_charge)
    )
    charge_next, populations_next = pl.pallas_call(
        functools.partial(step_faces, peers, tiles, band_cols),
        in_specs=[SMEM] + [VMEM] * 5 + [hbm, VMEM, VMEM, hbm],
        out_specs=[VMEM, hbm],
        scratch_shapes=[
            pltpu.VMEM((tiles, FRAME, PADDED, DEPTH), f32),
            pltpu.VMEM((tiles, EDGE + 2, PADDED, DEPTH), jnp.int32),
            pltpu.VMEM((tiles, CHANNELS, PADDED, DEPTH), f32),
            pltpu.VMEM((tiles, 2, 5, PADDED, DEPTH), f32),
            pltpu.VMEM((tiles, 2, 5, PADDED, DEPTH), f32),
            pltpu.VMEM((tiles, len(ACROSS_Y), EDGE, 8, DEPTH), f32),
            pltpu.VMEM((tiles, len(ACROSS_X), EDGE, DEPTH), f32),
            pltpu.SemaphoreType.DMA((tiles, 1 + len(ACROSS_Y + ACROSS_X))),
        ],
        out_shape=[shape(held.shape, f32), shape(populations.shape, f32)],
        input_output_aliases={9: 1},
        compiler_params=room(20), name="step_faces",
    )(tile_ids, held, fluid_mask, frames, rims, edges, bands, lines, closed_charge, closed.reshape(populations.shape))
    return (populations_next, charge_next.reshape(charge.shape), potential)


def solution(mesh):
    placed = (
        P(None, ("gx", "gy"), None, None, None),
        P(("gx", "gy"), None, None, None),
        P(("gx", "gy"), None, None, None),
        P(("gx", "gy")),
        P("gx", "gy", None),
        P(),
    )
    return jax.shard_map(
        per_device,
        mesh=mesh,
        in_specs=placed,
        out_specs=(
            P(None, ("gx", "gy"), None, None, None),
            P(("gx", "gy"), None, None, None),
            P("gx", "gy", None),
        ),
        check_vma=False,
    )
```

```python
import functools

import jax
import jax.numpy as jnp
from jax import lax
from jax.experimental import pallas as pl
from jax.experimental.pallas import tpu as pltpu
from jax.sharding import PartitionSpec as P

EDGE = 16
DEPTH = 128
TILE_ROWS = 2
TILE_COLS = 2
PHASES = 4
SWEEPS = 4

LATTICE = (
    (0, 0, 0),
    (1, 0, 0),
    (-1, 0, 0),
    (0, 1, 0),
    (0, -1, 0),
    (0, 0, 1),
    (0, 0, -1),
    (1, 1, 0),
    (-1, -1, 0),
    (1, -1, 0),
    (-1, 1, 0),
    (1, 0, 1),
    (-1, 0, -1),
    (1, 0, -1),
    (-1, 0, 1),
    (0, 1, 1),
    (0, -1, -1),
    (0, 1, -1),
    (0, -1, 1),
)
relax_time = 0.8
screening = 0.001
spectrum_low = 0.1
spectrum_high = 2.0

AREA = EDGE * EDGE
SIDE = 8
RING = 2
WIDE = RING + SWEEPS - 1
WIDER = WIDE + 1
FRAME = EDGE + 2 * RING
PADDED = EDGE + 2 * SIDE
CHANNELS = 10
HALVES = 2 * CHANNELS
VMEM = pl.BlockSpec(memory_space=pltpu.VMEM)
SMEM = pl.BlockSpec(memory_space=pltpu.SMEM)


def room(mebibytes):
    return pltpu.CompilerParams(vmem_limit_bytes=mebibytes * 2**20)


def crossing(axis_index, face_sign):
    return [q for q in range(19) if LATTICE[q][axis_index] == face_sign]


def opposite(direction):
    return LATTICE.index(tuple(-entry for entry in LATTICE[direction]))


def lattice_weight(direction):
    return (1.0 / 3.0, 1.0 / 18.0, 1.0 / 36.0)[sum(abs(e) for e in LATTICE[direction])]


def along(direction, vector):
    total = None
    for entry, part in zip(LATTICE[direction], vector):
        if entry:
            term = part if entry > 0 else -part
            total = term if total is None else total + term
    return total


def moments(pops):
    density = pops[0]
    for q in range(1, 19):
        density = density + pops[q]
    momentum = []
    for axis in range(3):
        plus = sum_of([pops[q] for q in crossing(axis, 1)])
        minus = sum_of([pops[q] for q in crossing(axis, -1)])
        momentum.append(plus - minus)
    return density, momentum


def sum_of(values):
    total = values[0]
    for value in values[1:]:
        total = total + value
    return total


def collide(pops, density, momentum, force):
    source_scale = 1.0 - 0.5 / relax_time
    gain = 1.0 / relax_time
    inverse = 1.0 / density
    carried = [m + 0.5 * f for m, f in zip(momentum, force)]
    velocity = [c * inverse for c in carried]
    energy = sum_of([c * v for c, v in zip(carried, velocity)])
    power = sum_of([v * f for v, f in zip(velocity, force)])
    base = gain * density - (1.5 * gain) * energy - (3.0 * source_scale) * power
    relaxed = {}
    for q in pops:
        weight = lattice_weight(q)
        kept = (1.0 - gain) * pops[q]
        if q == 0:
            relaxed[q] = kept + weight * base
            continue
        if q in relaxed:
            continue
        p, g, rp = along(q, velocity), along(q, force), along(q, carried)
        even = weight * base + p * ((4.5 * gain * weight) * rp + (9.0 * source_scale * weight) * g)
        odd = (3.0 * gain * weight) * rp + (3.0 * source_scale * weight) * g
        relaxed[q] = kept + (even + odd)
        back = opposite(q)
        if back in pops:
            relaxed[back] = (1.0 - gain) * pops[back] + (even - odd)
    return relaxed, velocity


def ring_pairs(axis):
    size = lax.axis_size(axis)
    up = [(i, (i + 1) % size) for i in range(size)]
    return up, [(j, i) for i, j in up]


def pack_source(tiles, band_cols, ids, charge, mask, out):
    out[...] = jnp.zeros_like(out)
    lane = lax.broadcasted_iota(jnp.int32, (8, DEPTH), 1)
    header = jnp.zeros((8, DEPTH), jnp.int32)
    for t in range(tiles):
        owner = ids[t] % band_cols // TILE_COLS
        header = jnp.where(lane == t, ids[t], header)
        for i in range(EDGE):
            flags = mask[t, i + 1, 1 : EDGE + 1, :].astype(jnp.float32)
            out[owner, pl.ds(i * EDGE, EDGE), :] = charge[t, pl.ds(i * EDGE, EDGE), :] * flags
    for peer in range(out.shape[0]):
        out[peer, pl.ds(AREA, 8), :] = header.astype(jnp.float32)


def assemble(band, tiles, slot_of, arrived, block, left, right):
    for local in range(TILE_ROWS * TILE_COLS):
        r, c = local // TILE_COLS, local % TILE_COLS
        slot = slot_of[band + local] // tiles
        for i in range(EDGE):
            row = r * EDGE + i
            cells = arrived[slot, pl.ds(i * EDGE, EDGE), :]
            block[row, pl.ds(c * EDGE, EDGE), :] = cells
            if c == 0:
                left[row] = cells[:SIDE]
            if c == TILE_COLS - 1:
                right[row] = cells[EDGE - SIDE :]


def tick(_, out):
    out[...] = jnp.zeros_like(out)


def edge_rows(block, left, right, ups, downs):
    rows = block.shape[0]
    for row in range(WIDE):
        low = rows - WIDE + row
        ups[row] = jnp.concatenate([left[low], block[low], right[low]], axis=0)
        downs[row] = jnp.concatenate([left[row], block[row], right[row]], axis=0)


def harmonic(a, b):
    return 2.0 * a * b / (a + b)


def face_weights(table, labels, before, after, left, right, wx, wy, wz, inverse, permit):
    rows = labels.shape[0]
    total = rows + 2 * WIDER

    def look(label):
        value = jnp.full(label.shape, table[PHASES - 1], jnp.float32)
        for phase in range(PHASES - 1):
            value = jnp.where(label == phase, table[phase], value)
        return value

    for row in range(WIDER):
        low, high = row, WIDER + rows + row
        permit[low] = look(jnp.concatenate([left[low], before[row], right[low]], axis=0))
        permit[high] = look(jnp.concatenate([left[high], after[row], right[high]], axis=0))

    def fill(row, carry):
        row = WIDER + row
        permit[row] = look(jnp.concatenate([left[row], labels[row - WIDER], right[row]], axis=0))
        return carry

    lax.fori_loop(0, rows, fill, 0, unroll=2)
    width = permit.shape[1]
    wx[0] = harmonic(permit[0], permit[1])

    def weigh(row, carry):
        here = permit[row]
        x_plus = harmonic(here, permit[row + 1])
        y_plus = harmonic(here, pltpu.roll(here, width - 1, 0))
        z_plus = harmonic(here, pltpu.roll(here, DEPTH - 1, 1))
        wx[row] = x_plus
        wy[row] = y_plus
        wz[row] = z_plus
        diagonal = x_plus + wx[row - 1] + y_plus + pltpu.roll(y_plus, 1, 0)
        diagonal = diagonal + z_plus + pltpu.roll(z_plus, 1, 1) + screening
        inverse[row] = 1.0 / diagonal
        return carry

    lax.fori_loop(1, total - 1, weigh, 0, unroll=6)


def solve(band, tiles, slot_of, middle, left, right, before, after, wx, wy, wz, inverse, _, out, frames, u0, u1, residual, potential):
    rows, width = middle.shape[0], wx.shape[1]
    center_value = 0.5 * (spectrum_high + spectrum_low)
    half_width = 0.5 * (spectrum_high - spectrum_low)
    ratio = center_value / half_width

    def start(row, source):
        r = source * inverse[row]
        residual[row] = r
        u = r * (1.0 / center_value)
        u0[row] = u
        potential[row] = u

    for row in range(WIDE):
        start(1 + row, before[row])
        start(1 + WIDE + rows + row, after[row])

    def begin(row, carry):
        start(1 + WIDE + row, jnp.concatenate([left[row], middle[row], right[row]], axis=0))
        return carry

    lax.fori_loop(0, rows, begin, 0, unroll=2)
    old, new = u0, u1
    rho = 1.0 / ratio
    for sweep in range(1, SWEEPS):
        rho_new = 1.0 / (2.0 * ratio - rho)
        a, b = rho_new * rho, 2.0 * rho_new / half_width
        last = sweep == SWEEPS - 1

        def step(row, carry):
            u = old[row]
            y_weight, z_weight = wy[row], wz[row]
            spread = wx[row] * old[row + 1] + wx[row - 1] * old[row - 1]
            spread = spread + y_weight * pltpu.roll(u, width - 1, 0) + pltpu.roll(y_weight * u, 1, 0)
            spread = spread + z_weight * pltpu.roll(u, DEPTH - 1, 1) + pltpu.roll(z_weight * u, 1, 1)
            r = residual[row] - u + inverse[row] * spread
            u = a * u + b * r
            potential[row] = potential[row] + u
            if not last:
                residual[row] = r
                new[row] = u
            return carry

        lax.fori_loop(1 + sweep, rows + 2 * WIDER - 1 - sweep, step, 0, unroll=4)
        old, new = new, old
        rho = rho_new
    inner = width - 2 * SIDE

    def give(row, carry):
        out[row] = potential[WIDER + row, pl.ds(SIDE, inner), :]
        return carry

    lax.fori_loop(0, rows, give, 0, unroll=2)
    frames[...] = jnp.zeros_like(frames)
    for local in range(TILE_ROWS * TILE_COLS):
        r, c = local // TILE_COLS, local % TILE_COLS
        slot = slot_of[band + local] // tiles
        for a in range(FRAME):
            frames[slot, pl.ds(a * FRAME, FRAME), :] = potential[
                WIDER + r * EDGE - RING + a, pl.ds(SIDE + c * EDGE - RING, FRAME), :
            ]


def unit_count(peers):
    return -(-2 * HALVES // peers)


def unit_places(peers):
    places = {}
    for face in range(4):
        for rest in range(HALVES):
            unit = face % 2 * HALVES + rest
            row = (face // 2 * unit_count(peers) + unit // peers) * 8
            places[face, rest // 2, rest % 2] = (unit % peers, row)
    return places


def x_slots(peers):
    return -(-HALVES // peers), HALVES // peers


FACES = ((0, -1), (0, 1), (1, -1), (1, 1))


def open_sides(mask, bits, flags):
    column = lax.broadcasted_iota(jnp.int32, (EDGE + 2, DEPTH), 0)
    inner = (column > 0) & (column < EDGE + 1)
    for i in range(EDGE + 2):
        row = jnp.where(inner, mask[0, i], 0) if 0 < i < EDGE + 1 else jnp.zeros((EDGE + 2, DEPTH), jnp.int32)
        flags[1, i, pl.ds(SIDE - 1, EDGE + 2), :] = row
        flags[2, i, pl.ds(SIDE - 1, EDGE + 2), :] = pltpu.roll(row, 1, 1)
        flags[0, i, pl.ds(SIDE - 1, EDGE + 2), :] = pltpu.roll(row, DEPTH - 1, 1)

    def gather(i, carry):
        total = jnp.zeros((EDGE, DEPTH), jnp.int32)
        for q in range(19):
            cx, cy, cz = LATTICE[q]
            total = total + flags[cz + 1, i + 1 - cx, pl.ds(SIDE - cy, EDGE), :] * (1 << q)
        own = flags[1, i + 1, pl.ds(SIDE, EDGE), :]
        bits[0, pl.ds(pl.multiple_of(i * EDGE, EDGE), EDGE), :] = jnp.where(own == 1, total, 0)
        return carry

    lax.fori_loop(0, EDGE, gather, 0, unroll=4)


def raw_faces(peers, pops, charge, mask, out, bits, flags):
    open_sides(mask, bits, flags)
    places = unit_places(peers)
    taken = set(places.values())
    for peer in range(peers):
        for row in range(0, out.shape[2], 8):
            if (peer, row) not in taken:
                out[peer, 0, pl.ds(row, 8), :] = jnp.zeros((8, DEPTH), jnp.float32)
    for face, (axis, sign) in enumerate(FACES):
        layer = 0 if sign < 0 else EDGE - 1
        for half in range(2):
            if axis == 0:
                where = pl.ds(layer * EDGE + 8 * half, 8)
            else:
                where = pl.ds(8 * half * EDGE + layer, 8, stride=EDGE)
            values = [pops[q, 0, where, :] for q in range(19)]
            density, momentum = moments(values)
            channels = [values[q] for q in crossing(axis, sign)]
            channels += [density] + momentum + [charge[0, where, :]]
            for channel, value in enumerate(channels):
                peer, row = places[face, channel, half]
                out[peer, 0, pl.ds(row, 8), :] = value


def outer_rows(peers, band_cols, slot_of, arrived, low, high):
    count = unit_count(peers)
    low_count, first_high = x_slots(peers)
    for col in range(band_cols):
        low[col] = arrived[slot_of[col], pl.ds(0, low_count * 8), :]
        slot = slot_of[(TILE_ROWS - 1) * band_cols + col]
        high[col] = arrived[slot, pl.ds(first_high * 8, (count - first_high) * 8), :]


def turn_faces(peers, band_cols, slot_of, tile_at, me_ref, arrived, below, above, out, from_low, from_high):
    count = unit_count(peers)
    low_count, first_high = x_slots(peers)
    lows, highs = pl.ds(0, low_count * 8), pl.ds(first_high * 8, (count - first_high) * 8)

    def lay(col, carry):
        from_low[col] = below[col]
        from_high[(TILE_ROWS - 1) * band_cols + col] = above[col]
        for row in range(1, TILE_ROWS):
            from_low[row * band_cols + col] = arrived[slot_of[(row - 1) * band_cols + col], highs, :]
            from_high[(row - 1) * band_cols + col] = arrived[slot_of[row * band_cols + col], lows, :]
        return carry

    lax.fori_loop(0, band_cols, lay, 0, unroll=2)
    me = me_ref[0]
    half = me % 2
    is_low = [n * peers + me < HALVES for n in range(count)]

    def across_x(position, n, row, size):
        if n < low_count:
            value = from_high[position, pl.ds(n * 8 + row, size), :]
        if n >= first_high:
            other = from_low[position, pl.ds((n - first_high) * 8 + row, size), :]
            value = jnp.where(is_low[n], value, other) if n < low_count else other
        return value

    def send(d, carry):
        p = tile_at[d]
        row, col = p // band_cols, p % band_cols
        right, left = (col + 1) % band_cols, (col + band_cols - 1) % band_cols
        slot_right = slot_of[row * band_cols + right]
        slot_left = slot_of[row * band_cols + left]
        beside = row * band_cols + jnp.where(half == 0, right, left)
        for n in range(count):
            out[d, pl.ds(n * 8, 8), :] = across_x(p, n, 0, 8)
            cells = pl.ds((count + n) * 8, 8)
            out[d, cells, :] = arrived[jnp.where(is_low[n], slot_right, slot_left), cells, :]
            out[d, pl.ds(2 * count * 8 + n, 1), :] = across_x(beside, n, 7 * half, 1)
        return carry

    lax.fori_loop(0, out.shape[0], send, 0, unroll=2)


ACROSS_X = [q for q in range(19) if LATTICE[q][0]]
ACROSS_Y = [q for q in range(19) if LATTICE[q][1]]


def field_of(x_low, x_high, y_low, y_high, here):
    return [
        0.5 * (x_low - x_high),
        0.5 * (y_low - y_high),
        0.5 * (pltpu.roll(here, 1, 1) - pltpu.roll(here, DEPTH - 1, 1)),
    ]


def flux(speed_a, speed_b, a, b, flag_a, flag_b):
    face = 0.5 * (speed_a + speed_b)
    return jnp.where((flag_a == 1) & (flag_b == 1), face * jnp.where(face > 0, a, b), 0.0)


def step_inside(ids, pops, charge, bits, frame, out, charge_out, edges, bands, lines, near, relaxed, conc, vx, vy, vz):
    for a in range(FRAME):
        near[a, pl.ds(SIDE - RING, FRAME), :] = frame[0, pl.ds(a * FRAME, FRAME), :]

    def relax_row(i, carry):
        cells = pl.ds(pl.multiple_of(i * EDGE, EDGE), EDGE)
        field = field_of(
            near[i + RING - 1, pl.ds(SIDE, EDGE), :], near[i + RING + 1, pl.ds(SIDE, EDGE), :],
            near[i + RING, pl.ds(SIDE - 1, EDGE), :], near[i + RING, pl.ds(SIDE + 1, EDGE), :],
            near[i + RING, pl.ds(SIDE, EDGE), :],
        )
        values = [pops[q, 0, cells, :] for q in range(19)]
        held = charge[0, cells, :]
        force = [held * f for f in field]
        density, momentum = moments(values)
        done, velocity = collide(dict(enumerate(values)), density, momentum, force)
        for q in range(19):
            relaxed[q, i + 1, pl.ds(SIDE, EDGE), :] = done[q]
        conc[i + 1, pl.ds(SIDE, EDGE), :] = held
        vx[i + 1, pl.ds(SIDE, EDGE), :] = velocity[0]
        vy[i + 1, pl.ds(SIDE, EDGE), :] = velocity[1]
        vz[i + 1, pl.ds(SIDE, EDGE), :] = velocity[2]
        return carry

    lax.fori_loop(0, EDGE, relax_row, 0, unroll=4)
    flat_vy = vy.reshape((EDGE + 2) * PADDED, DEPTH)
    edges[0, 0] = vx[1, pl.ds(SIDE, EDGE), :]
    edges[0, 1] = vx[EDGE, pl.ds(SIDE, EDGE), :]
    edges[0, 2] = flat_vy[pl.ds(PADDED + SIDE, EDGE, stride=PADDED), :]
    edges[0, 3] = flat_vy[pl.ds(PADDED + SIDE + EDGE - 1, EDGE, stride=PADDED), :]

    def stream_row(i, carry):
        cells = pl.ds(pl.multiple_of(i * EDGE, EDGE), EDGE)
        here = i + 1
        mid = pl.ds(SIDE, EDGE)
        bit = bits[0, cells, :]
        is_open = [(bit & (1 << q)) != 0 for q in range(19)]
        for q in range(19):
            cx, cy, cz = LATTICE[q]
            pulled = relaxed[q, here - cx, pl.ds(SIDE - cy, EDGE), :]
            if cz:
                pulled = pltpu.roll(pulled, cz % DEPTH, 1)
            kept = pops[q, 0, cells, :]
            if q:
                kept = jnp.where(is_open[0], relaxed[opposite(q), here, mid, :], kept)
            out[q, 0, cells, :] = jnp.where(is_open[q], pulled, kept)
        held = conc[here, mid, :]

        def through(q, speed_a, speed_b, a, b):
            face = 0.5 * (speed_a + speed_b)
            return jnp.where(is_open[q], face * jnp.where(face > 0, a, b), 0.0)

        change = through(2, vx[here, mid, :], vx[here + 1, mid, :], held, conc[here + 1, mid, :])
        change = change - through(1, vx[here - 1, mid, :], vx[here, mid, :], conc[here - 1, mid, :], held)
        low, high = pl.ds(SIDE - 1, EDGE), pl.ds(SIDE + 1, EDGE)
        change = change + through(4, vy[here, mid, :], vy[here, high, :], held, conc[here, high, :])
        change = change - through(3, vy[here, low, :], vy[here, mid, :], conc[here, low, :], held)
        speed = vz[here, mid, :]
        z_flux = through(6, speed, pltpu.roll(speed, DEPTH - 1, 1), held, pltpu.roll(held, DEPTH - 1, 1))
        change = change + (z_flux - pltpu.roll(z_flux, 1, 1))
        charge_out[0, cells, :] = held - change
        return carry

    lax.fori_loop(0, EDGE, stream_row, 0, unroll=4)
    for n, q in enumerate(ACROSS_Y):
        bands[0, n] = out[q, 0, pl.ds(0 if LATTICE[q][1] > 0 else EDGE - 1, EDGE, stride=EDGE), :]
    for n, q in enumerate(ACROSS_X):
        lines[0, n] = out[q, 0, pl.ds(0 if LATTICE[q][0] > 0 else AREA - EDGE, EDGE), :]


def step_faces(peers, tiles, band_cols, ids, charge_at, mask_at, frames_at, rims_at, edges_at, bands_at, lines_at,
               charge_in_at, _, charge_out_at, out, charge, mask, frames, rims, edges, new_bands, lines, charge_out,
               all_near, all_flags, all_rim, all_x, all_y, new_lines, in_sems, out_sems):
    places = unit_places(peers)
    corner_row = 2 * unit_count(peers) * 8
    all_flat_near = all_near.reshape(tiles, FRAME * PADDED, DEPTH)
    all_flat_flags = all_flags.reshape(tiles, (EDGE + 2) * PADDED, DEPTH)

    def pieces(tile):
        made = []
        for n, q in enumerate(ACROSS_Y):
            made.append((new_bands.at[tile, n], out.at[q, tile, :, 0 if LATTICE[q][1] > 0 else EDGE - 1]))
        for n, q in enumerate(ACROSS_X):
            layer = 0 if LATTICE[q][0] > 0 else EDGE - 1
            if LATTICE[q][1]:
                cells = pl.ds(1 if LATTICE[q][1] > 0 else 0, EDGE - 1)
                made.append((new_lines.at[tile, n, cells], out.at[q, tile, layer, cells]))
            else:
                made.append((new_lines.at[tile, n], out.at[q, tile, layer]))
        made.append((charge_out.at[tile], charge_out_at.at[tile]))
        return [pltpu.make_async_copy(a, b, out_sems.at[tile, n]) for n, (a, b) in enumerate(made)]

    def incoming(tile):
        owner = ids[tile] % band_cols // TILE_COLS
        pairs = [
            (mask_at.at[tile], mask.at[tile]),
            (frames_at.at[owner], frames.at[tile]),
            (rims_at.at[:, tile], rims.at[:, tile]),
            (charge_at.at[tile], charge.at[tile]),
            (charge_in_at.at[tile], charge_out.at[tile]),
            (edges_at.at[tile], edges.at[tile]),
            (lines_at.at[tile], lines.at[tile]),
            (bands_at.at[tile], new_bands.at[tile]),
        ]
        return [pltpu.make_async_copy(a, b, in_sems.at[tile, n]) for n, (a, b) in enumerate(pairs)]

    for tile in range(tiles):
        for copy in incoming(tile):
            copy.start()

    def patch(t, carry):
        near, flags, rim, beside_x, beside_y = (x.at[t] for x in (all_near, all_flags, all_rim, all_x, all_y))
        flat_near, flat_flags = all_flat_near.at[t], all_flat_flags.at[t]
        for copy in incoming(t):
            copy.wait()
        for a in range(FRAME):
            near[a, pl.ds(SIDE - RING, FRAME), :] = frames[t, pl.ds(a * FRAME, FRAME), :]
        for i in range(EDGE + 2):
            flags[i, pl.ds(SIDE - 1, EDGE + 2), :] = mask[t, i]

        for side, face, layer in ((0, 1, 0), (1, 0, EDGE + 1)):
            for channel in range(CHANNELS):
                for half in range(2):
                    peer, row = places[face, channel, half]
                    rim[channel, pl.ds(SIDE + 8 * half, 8), :] = rims[peer, t, pl.ds(row, 8), :]
                    corner = corner_row + row // 8
                    column = SIDE + EDGE if half == 0 else SIDE - 1
                    rim[channel, pl.ds(column, 1), :] = rims[peer, t, pl.ds(corner, 1), :]
            here = near[layer + 1]
            field = field_of(
                near[layer], near[layer + 2], pltpu.roll(here, 1, 0), pltpu.roll(here, PADDED - 1, 0), here
            )
            density, momentum, held = rim[5], [rim[6], rim[7], rim[8]], rim[9]
            force = [held * f for f in field]
            dirs = crossing(*FACES[face])
            done, velocity = collide({q: rim[n] for n, q in enumerate(dirs)}, density, momentum, force)
            for n, q in enumerate(dirs):
                beside_x[side, n] = done[q]
            cells = pl.ds(0 if side == 0 else AREA - EDGE, EDGE)
            own_layer = 0 if side == 0 else EDGE - 1
            inner = slice(SIDE, SIDE + EDGE)
            speed, own_speed = velocity[0][inner], edges[t, side]
            amount, own_amount = held[inner], charge[t, cells, :]
            flag, own_flag = flags[layer, pl.ds(SIDE, EDGE), :], flags[own_layer + 1, pl.ds(SIDE, EDGE), :]
            if side == 0:
                charge_out[t, cells, :] += flux(speed, own_speed, amount, own_amount, flag, own_flag)
            else:
                charge_out[t, cells, :] -= flux(own_speed, speed, own_amount, amount, own_flag, flag)
            for n, q in enumerate(dirs):
                _, cy, cz = LATTICE[q]
                columns = pl.ds(SIDE - cy, EDGE)
                value, flag = beside_x[side, n, columns, :], flags[layer, columns, :]
                if cz:
                    value, flag = pltpu.roll(value, cz % DEPTH, 1), pltpu.roll(flag, cz % DEPTH, 1)
                line = ACROSS_X.index(q)
                taken = (flag == 1) & (own_flag == 1)
                merged = jnp.where(taken, value, lines[t, line])
                new_lines[t, line] = merged

        for side, face, column in ((0, 3, SIDE - 1), (1, 2, SIDE + EDGE)):
            dirs = crossing(*FACES[face])
            x_dirs = [crossing(*FACES[1]), crossing(*FACES[0])]
            own_column = 0 if side == 0 else EDGE - 1
            for half in range(2):
                def at(row, col):
                    return flat_near[pl.ds((RING + 8 * half + row) * PADDED + col, 8, stride=PADDED), :]

                raw = [rims[places[face, c, half][0], t, pl.ds(places[face, c, half][1], 8), :]
                       for c in range(CHANNELS)]
                field = field_of(at(-1, column), at(1, column), at(0, column - 1), at(0, column + 1), at(0, column))
                force = [raw[9] * f for f in field]
                done, velocity = collide({q: raw[n] for n, q in enumerate(dirs)}, raw[5], raw[6:9], force)
                for n, q in enumerate(dirs):
                    beside_y[side, n, pl.ds(SIDE + 8 * half, 8), :] = done[q]
                cells = pl.ds(8 * half * EDGE + own_column, 8, stride=EDGE)
                own_flag = flat_flags[pl.ds((1 + 8 * half) * PADDED + SIDE + own_column, 8, stride=PADDED), :]
                flag = flat_flags[pl.ds((1 + 8 * half) * PADDED + column, 8, stride=PADDED), :]
                own_speed, own_amount = edges[t, 2 + side, pl.ds(8 * half, 8), :], charge[t, cells, :]
                if side == 0:
                    charge_out[t, cells, :] += flux(velocity[1], own_speed, raw[9], own_amount, flag, own_flag)
                else:
                    charge_out[t, cells, :] -= flux(own_speed, velocity[1], own_amount, raw[9], own_flag, flag)
            own_flag = flat_flags[pl.ds(PADDED + SIDE + own_column, EDGE, stride=PADDED), :]
            for n, q in enumerate(dirs):
                cx, _, cz = LATTICE[q]
                if cx:
                    end = 0 if cx > 0 else 1
                    row = SIDE - 1 if cx > 0 else SIDE + EDGE
                    beside_y[side, n, pl.ds(row, 1), :] = beside_x[end, x_dirs[end].index(q), pl.ds(column, 1), :]
                value = beside_y[side, n, pl.ds(SIDE - cx, EDGE), :]
                flag = flat_flags[pl.ds((1 - cx) * PADDED + column, EDGE, stride=PADDED), :]
                if cz:
                    value, flag = pltpu.roll(value, cz % DEPTH, 1), pltpu.roll(flag, cz % DEPTH, 1)
                band = ACROSS_Y.index(q)
                new_bands[t, band] = jnp.where((flag == 1) & (own_flag == 1), value, new_bands[t, band])
        for copy in pieces(t):
            copy.start()
        return carry

    lax.fori_loop(0, tiles, patch, 0, unroll=2)
    for tile in range(tiles):
        for copy in pieces(tile):
            copy.wait()


def per_device(populations, charge, fluid_mask, tile_ids, phase_label, permittivity):
    peers = lax.axis_size("gy")
    tiles = charge.shape[0]
    rows, cols = phase_label.shape[0], phase_label.shape[1]
    band_cols = TILE_COLS * peers
    band = peers * tiles
    count = unit_count(peers)
    low_count, first_high = x_slots(peers)
    out_rows = 2 * count * 8
    in_rows = out_rows + -(-count // 8) * 8
    f32 = jnp.float32
    shape = jax.ShapeDtypeStruct
    gx_up, gx_down = ring_pairs("gx")
    gy_up, gy_down = ring_pairs("gy")
    me = lax.axis_index("gy").astype(jnp.int32)
    pops = pltpu.with_memory_space_constraint(populations.reshape(19, tiles, AREA, DEPTH), pltpu.HBM)
    held = charge.reshape(tiles, AREA, DEPTH)

    outgoing = pl.pallas_call(
        functools.partial(pack_source, tiles, band_cols),
        out_shape=pltpu.HBM((peers, AREA + 8, DEPTH), f32),
        in_specs=[SMEM, VMEM, VMEM], out_specs=VMEM, compiler_params=room(6), name="pack_source",
    )(tile_ids, held, fluid_mask)
    outgoing, phase_label = lax.optimization_barrier((outgoing, phase_label))
    arrived = lax.all_to_all(outgoing, "gy", split_axis=0, concat_axis=0, tiled=True)

    beside = [lax.ppermute(phase_label[rows - WIDER :], "gx", gx_up)]
    beside.append(lax.ppermute(phase_label[:WIDER], "gx", gx_down))
    beside = list(lax.optimization_barrier(tuple(beside)))
    tall = jnp.concatenate([beside[0][:, cols - SIDE :], phase_label[:, cols - SIDE :], beside[1][:, cols - SIDE :]])
    beside.append(lax.ppermute(tall, "gy", gy_up))
    tall = jnp.concatenate([beside[0][:, :SIDE], phase_label[:, :SIDE], beside[1][:, :SIDE]])
    beside.append(lax.ppermute(tall, "gy", gy_down))

    one_tile = pl.BlockSpec((1, AREA, DEPTH), lambda t: (t, 0, 0))
    raw, bits = pl.pallas_call(
        functools.partial(raw_faces, peers),
        grid=(tiles,),
        out_shape=[pltpu.HBM((peers, tiles, out_rows, DEPTH), f32), pltpu.HBM(held.shape, jnp.int32)],
        in_specs=[
            pl.BlockSpec((19, 1, AREA, DEPTH), lambda t: (0, t, 0, 0)),
            one_tile,
            pl.BlockSpec((1, EDGE + 2, EDGE + 2, DEPTH), lambda t: (t, 0, 0, 0)),
        ],
        out_specs=[pl.BlockSpec((peers, 1, out_rows, DEPTH), lambda t: (0, t, 0, 0)), one_tile],
        scratch_shapes=[pltpu.VMEM((3, EDGE + 2, PADDED, DEPTH), jnp.int32)],
        compiler_params=room(14), name="raw_faces",
    )(pops, held, fluid_mask)
    arrived, raw, beside = lax.optimization_barrier((arrived, raw, beside))
    beside = list(beside)

    tile_at = arrived[:, AREA, :tiles].astype(jnp.int32).reshape(band)
    slots = jnp.arange(band, dtype=jnp.int32)
    local = jnp.arange(tiles, dtype=jnp.int32)
    mine = local // TILE_COLS * band_cols + TILE_COLS * me + local % TILE_COLS
    wanted = jnp.concatenate([slots, mine])
    slot_of = jnp.sum(jnp.where(tile_at[None, :] == wanted[:, None], slots[None, :], 0), axis=1)

    block, left, right = pl.pallas_call(
        functools.partial(assemble, band, tiles),
        out_shape=[pltpu.VMEM((rows, cols, DEPTH), f32), shape((rows, SIDE, DEPTH), f32), shape((rows, SIDE, DEPTH), f32)],
        in_specs=[SMEM, VMEM], out_specs=[VMEM] * 3, compiler_params=room(5), name="assemble",
    )(slot_of, arrived)
    left, right = lax.ppermute(right, "gy", gy_up), lax.ppermute(left, "gy", gy_down)
    ends = shape((WIDE, cols + 2 * SIDE, DEPTH), f32)
    ups, downs = pl.pallas_call(
        edge_rows, out_shape=[ends, ends], in_specs=[VMEM] * 3, out_specs=[VMEM] * 2,
        compiler_params=room(3), name="edge_rows",
    )(block, left, right)
    ups, downs, beside[0] = lax.optimization_barrier((ups, downs, beside[0]))
    before, after = lax.ppermute(ups, "gx", gx_up), lax.ppermute(downs, "gx", gx_down)
    hbm = pl.BlockSpec(memory_space=pl.ANY)
    token = pl.pallas_call(
        tick, out_shape=shape((8, DEPTH), f32), in_specs=[hbm], out_specs=VMEM, compiler_params=room(1), name="tick"
    )(downs)
    raw, token = lax.optimization_barrier((raw, token))
    token, beside[0] = lax.optimization_barrier((token, beside[0]))
    wide = shape((rows + 2 * WIDER, cols + 2 * SIDE, DEPTH), f32)
    scratch = pltpu.VMEM(wide.shape, f32)
    weights = pl.pallas_call(
        face_weights, out_shape=[pltpu.VMEM(wide.shape, f32)] * 4, in_specs=[SMEM] + [VMEM] * 5, out_specs=[VMEM] * 4,
        scratch_shapes=[scratch], compiler_params=room(12), name="face_weights",
    )(permittivity, phase_label, *beside)

    faces = lax.all_to_all(raw, "gy", split_axis=0, concat_axis=0, tiled=True).reshape(band, out_rows, DEPTH)
    faces = pltpu.with_memory_space_constraint(faces, pltpu.HBM)
    potential, frames = pl.pallas_call(
        functools.partial(solve, band, tiles),
        out_shape=[shape((rows, cols, DEPTH), f32), pltpu.HBM((peers, FRAME * FRAME, DEPTH), f32)],
        in_specs=[SMEM] + [VMEM] * 9 + [hbm], out_specs=[VMEM, VMEM],
        scratch_shapes=[scratch] * 4, compiler_params=room(16), name="solve",
    )(slot_of, block, left, right, before, after, *weights, token)
    frames = lax.all_to_all(frames, "gy", split_axis=0, concat_axis=0, tiled=True)

    lows = (band_cols, low_count * 8, DEPTH)
    highs = (band_cols, (count - first_high) * 8, DEPTH)
    low, high = pl.pallas_call(
        functools.partial(outer_rows, peers, band_cols),
        out_shape=[shape(lows, f32), shape(highs, f32)], in_specs=[SMEM, VMEM], out_specs=[VMEM] * 2,
        compiler_params=room(5), name="outer_rows",
    )(slot_of, faces)
    below = lax.ppermute(high, "gx", gx_up)
    above = lax.ppermute(low, "gx", gx_down)
    turned = pl.pallas_call(
        functools.partial(turn_faces, peers, band_cols),
        out_shape=pltpu.HBM((band, in_rows, DEPTH), f32),
        in_specs=[SMEM, SMEM, SMEM, VMEM, VMEM, VMEM], out_specs=VMEM,
        scratch_shapes=[pltpu.VMEM((band,) + highs[1:], f32), pltpu.VMEM((band,) + lows[1:], f32)], compiler_params=room(8), name="turn_faces",
    )(slot_of, tile_at, me[None], faces, below, above)
    rims = lax.all_to_all(turned.reshape(peers, tiles, in_rows, DEPTH), "gy", split_axis=0, concat_axis=0, tiled=True)

    padded = pltpu.VMEM((EDGE + 2, PADDED, DEPTH), f32)
    near = pltpu.VMEM((FRAME, PADDED, DEPTH), f32)
    by_tile = pl.BlockSpec((1, AREA, DEPTH), lambda t, ids: (t, 0, 0))
    of_pops = pl.BlockSpec((19, 1, AREA, DEPTH), lambda t, ids: (0, t, 0, 0))
    of_frame = pl.BlockSpec((1, FRAME * FRAME, DEPTH), lambda t, ids: (ids[t] % band_cols // TILE_COLS, 0, 0))
    of_edges = pl.BlockSpec((1, 4, EDGE, DEPTH), lambda t, ids: (t, 0, 0, 0))
    bits = pltpu.with_memory_space_constraint(bits, pltpu.HBM)
    closed, closed_charge, edges, bands, lines = pl.pallas_call(
        step_inside,
        grid_spec=pltpu.PrefetchScalarGridSpec(
            num_scalar_prefetch=1,
            grid=(tiles,),
            in_specs=[of_pops, by_tile, by_tile, of_frame],
            out_specs=[
                of_pops, by_tile, of_edges,
                pl.BlockSpec((1, len(ACROSS_Y), EDGE, DEPTH), lambda t, ids: (t, 0, 0, 0)),
                pl.BlockSpec((1, len(ACROSS_X), EDGE, DEPTH), lambda t, ids: (t, 0, 0, 0)),
            ],
            scratch_shapes=[
                near,
                pltpu.VMEM((19, EDGE + 2, PADDED, DEPTH), f32),
                padded, padded, padded, padded,
            ],
        ),
        out_shape=[
            shape(pops.shape, f32), pltpu.HBM(held.shape, f32), shape((tiles, 4, EDGE, DEPTH), f32),
            pltpu.HBM((tiles, len(ACROSS_Y), EDGE, DEPTH), f32),
            pltpu.HBM((tiles, len(ACROSS_X), EDGE, DEPTH), f32),
        ],
        compiler_params=room(24), name="step_inside",
    )(tile_ids, pops, held, bits, frames)
    bands, lines, closed_charge = (
        pltpu.with_memory_space_constraint(x, pltpu.HBM) for x in (bands, lines, closed_charge)
    )
    charge_next, populations_next = pl.pallas_call(
        functools.partial(step_faces, peers, tiles, band_cols),
        in_specs=[SMEM] + [hbm] * 9,
        out_specs=[hbm, hbm],
        scratch_shapes=[
            pltpu.VMEM(held.shape, f32),
            pltpu.VMEM(fluid_mask.shape, jnp.int32),
            pltpu.VMEM((tiles, FRAME * FRAME, DEPTH), f32),
            pltpu.VMEM(rims.shape, f32),
            pltpu.VMEM(edges.shape, f32),
            pltpu.VMEM(bands.shape, f32),
            pltpu.VMEM(lines.shape, f32),
            pltpu.VMEM(held.shape, f32),
            pltpu.VMEM((tiles, FRAME, PADDED, DEPTH), f32),
            pltpu.VMEM((tiles, EDGE + 2, PADDED, DEPTH), jnp.int32),
            pltpu.VMEM((tiles, CHANNELS, PADDED, DEPTH), f32),
            pltpu.VMEM((tiles, 2, 5, PADDED, DEPTH), f32),
            pltpu.VMEM((tiles, 2, 5, PADDED, DEPTH), f32),
            pltpu.VMEM(lines.shape, f32),
            pltpu.SemaphoreType.DMA((tiles, 8)),
            pltpu.SemaphoreType.DMA((tiles, 1 + len(ACROSS_Y + ACROSS_X))),
        ],
        out_shape=[shape(held.shape, f32), shape(populations.shape, f32)],
        input_output_aliases={9: 1},
        compiler_params=room(20), name="step_faces",
    )(tile_ids, held, fluid_mask, frames, rims, edges, bands, lines, closed_charge, closed.reshape(populations.shape))
    return (populations_next, charge_next.reshape(charge.shape), potential)


def solution(mesh):
    placed = (
        P(None, ("gx", "gy"), None, None, None),
        P(("gx", "gy"), None, None, None),
        P(("gx", "gy"), None, None, None),
        P(("gx", "gy")),
        P("gx", "gy", None),
        P(),
    )
    return jax.shard_map(
        per_device,
        mesh=mesh,
        in_specs=placed,
        out_specs=(
            P(None, ("gx", "gy"), None, None, None),
            P(("gx", "gy"), None, None, None),
            P("gx", "gy", None),
        ),
        check_vma=False,
    )
```

```python
import functools

import jax
import jax.numpy as jnp
from jax import lax
from jax.experimental import pallas as pl
from jax.experimental.pallas import tpu as pltpu
from jax.sharding import PartitionSpec as P

EDGE = 16
DEPTH = 128
TILE_ROWS = 2
TILE_COLS = 2
PHASES = 4
SWEEPS = 4

LATTICE = (
    (0, 0, 0),
    (1, 0, 0),
    (-1, 0, 0),
    (0, 1, 0),
    (0, -1, 0),
    (0, 0, 1),
    (0, 0, -1),
    (1, 1, 0),
    (-1, -1, 0),
    (1, -1, 0),
    (-1, 1, 0),
    (1, 0, 1),
    (-1, 0, -1),
    (1, 0, -1),
    (-1, 0, 1),
    (0, 1, 1),
    (0, -1, -1),
    (0, 1, -1),
    (0, -1, 1),
)
relax_time = 0.8
screening = 0.001
spectrum_low = 0.1
spectrum_high = 2.0

AREA = EDGE * EDGE
SIDE = 8
RING = 2
WIDE = RING + SWEEPS - 1
WIDER = WIDE + 1
FRAME = EDGE + 2 * RING
PADDED = EDGE + 2 * SIDE
CHANNELS = 10
HALVES = 2 * CHANNELS
VMEM = pl.BlockSpec(memory_space=pltpu.VMEM)
SMEM = pl.BlockSpec(memory_space=pltpu.SMEM)


def room(mebibytes):
    return pltpu.CompilerParams(vmem_limit_bytes=mebibytes * 2**20)


def crossing(axis_index, face_sign):
    return [q for q in range(19) if LATTICE[q][axis_index] == face_sign]


def opposite(direction):
    return LATTICE.index(tuple(-entry for entry in LATTICE[direction]))


def lattice_weight(direction):
    return (1.0 / 3.0, 1.0 / 18.0, 1.0 / 36.0)[sum(abs(e) for e in LATTICE[direction])]


def along(direction, vector):
    total = None
    for entry, part in zip(LATTICE[direction], vector):
        if entry:
            term = part if entry > 0 else -part
            total = term if total is None else total + term
    return total


def moments(pops):
    density = pops[0]
    for q in range(1, 19):
        density = density + pops[q]
    momentum = []
    for axis in range(3):
        plus = sum_of([pops[q] for q in crossing(axis, 1)])
        minus = sum_of([pops[q] for q in crossing(axis, -1)])
        momentum.append(plus - minus)
    return density, momentum


def sum_of(values):
    total = values[0]
    for value in values[1:]:
        total = total + value
    return total


def collide(pops, density, momentum, force):
    source_scale = 1.0 - 0.5 / relax_time
    gain = 1.0 / relax_time
    inverse = 1.0 / density
    carried = [m + 0.5 * f for m, f in zip(momentum, force)]
    velocity = [c * inverse for c in carried]
    energy = sum_of([c * v for c, v in zip(carried, velocity)])
    power = sum_of([v * f for v, f in zip(velocity, force)])
    base = gain * density - (1.5 * gain) * energy - (3.0 * source_scale) * power
    relaxed = {}
    for q in pops:
        weight = lattice_weight(q)
        kept = (1.0 - gain) * pops[q]
        if q == 0:
            relaxed[q] = kept + weight * base
            continue
        if q in relaxed:
            continue
        p, g, rp = along(q, velocity), along(q, force), along(q, carried)
        even = weight * base + p * ((4.5 * gain * weight) * rp + (9.0 * source_scale * weight) * g)
        odd = (3.0 * gain * weight) * rp + (3.0 * source_scale * weight) * g
        relaxed[q] = kept + (even + odd)
        back = opposite(q)
        if back in pops:
            relaxed[back] = (1.0 - gain) * pops[back] + (even - odd)
    return relaxed, velocity


def ring_pairs(axis):
    size = lax.axis_size(axis)
    up = [(i, (i + 1) % size) for i in range(size)]
    return up, [(j, i) for i, j in up]


def pack_source(tiles, band_cols, ids, charge, mask, out):
    out[...] = jnp.zeros_like(out)
    lane = lax.broadcasted_iota(jnp.int32, (8, DEPTH), 1)
    header = jnp.zeros((8, DEPTH), jnp.int32)
    for t in range(tiles):
        owner = ids[t] % band_cols // TILE_COLS
        header = jnp.where(lane == t, ids[t], header)
        for i in range(EDGE):
            flags = mask[t, i + 1, 1 : EDGE + 1, :].astype(jnp.float32)
            out[owner, pl.ds(i * EDGE, EDGE), :] = charge[t, pl.ds(i * EDGE, EDGE), :] * flags
    for peer in range(out.shape[0]):
        out[peer, pl.ds(AREA, 8), :] = header.astype(jnp.float32)


def assemble(band, tiles, slot_of, arrived, block, left, right):
    for local in range(TILE_ROWS * TILE_COLS):
        r, c = local // TILE_COLS, local % TILE_COLS
        slot = slot_of[band + local] // tiles
        for i in range(EDGE):
            row = r * EDGE + i
            cells = arrived[slot, pl.ds(i * EDGE, EDGE), :]
            block[row, pl.ds(c * EDGE, EDGE), :] = cells
            if c == 0:
                left[pl.ds(row * WIDE, WIDE), :] = cells[:WIDE]
            if c == TILE_COLS - 1:
                right[pl.ds(row * WIDE, WIDE), :] = cells[EDGE - WIDE :]


def edge_columns(before, labels, after, lows, highs):
    rows, cols = labels.shape[0], labels.shape[1]
    for row in range(rows + 2 * WIDER):
        if row < WIDER:
            line = before.at[row]
        elif row < WIDER + rows:
            line = labels.at[row - WIDER]
        else:
            line = after.at[row - WIDER - rows]
        lows[pl.ds(row * WIDER, WIDER), :] = line[pl.ds(0, WIDER), :]
        highs[pl.ds(row * WIDER, WIDER), :] = line[pl.ds(cols - WIDER, WIDER), :]


def edge_rows(block, left, right, ups, downs):
    rows, cols = block.shape[0], block.shape[1]
    for row in range(WIDE):
        for out, source in ((ups, rows - WIDE + row), (downs, row)):
            out[row, pl.ds(0, SIDE), :] = jnp.zeros((SIDE, DEPTH), jnp.float32)
            out[row, pl.ds(SIDE + cols, SIDE), :] = jnp.zeros((SIDE, DEPTH), jnp.float32)
            out[row, pl.ds(SIDE - WIDE, WIDE), :] = left[pl.ds(source * WIDE, WIDE), :]
            out[row, pl.ds(SIDE, cols), :] = block[source]
            out[row, pl.ds(SIDE + cols, WIDE), :] = right[pl.ds(source * WIDE, WIDE), :]


def harmonic(a, b):
    return 2.0 * a * b / (a + b)


def face_weights(table, labels, before, after, left, right, wx, wy, wz, inverse, permit):
    rows, cols = labels.shape[0], labels.shape[1]
    total = rows + 2 * WIDER

    def look(label):
        value = jnp.full(label.shape, table[PHASES - 1], jnp.float32)
        for phase in range(PHASES - 1):
            value = jnp.where(label == phase, table[phase], value)
        return value

    for row in range(WIDER):
        permit[row, pl.ds(SIDE, cols), :] = look(before[row])
        permit[WIDER + rows + row, pl.ds(SIDE, cols), :] = look(after[row])

    for row in range(total):
        permit[row, pl.ds(0, SIDE), :] = jnp.ones((SIDE, DEPTH), jnp.float32)
        permit[row, pl.ds(SIDE + cols, SIDE), :] = jnp.ones((SIDE, DEPTH), jnp.float32)
        permit[row, pl.ds(SIDE - WIDER, WIDER), :] = look(left[pl.ds(row * WIDER, WIDER), :])
        permit[row, pl.ds(SIDE + cols, WIDER), :] = look(right[pl.ds(row * WIDER, WIDER), :])

    def fill(row, carry):
        permit[WIDER + row, pl.ds(SIDE, cols), :] = look(labels[row])
        return carry

    lax.fori_loop(0, rows, fill, 0, unroll=2)
    width = permit.shape[1]
    wx[0] = harmonic(permit[0], permit[1])

    def weigh(row, carry):
        here = permit[row]
        x_plus = harmonic(here, permit[row + 1])
        y_plus = harmonic(here, pltpu.roll(here, width - 1, 0))
        z_plus = harmonic(here, pltpu.roll(here, DEPTH - 1, 1))
        wx[row] = x_plus
        wy[row] = y_plus
        wz[row] = z_plus
        diagonal = x_plus + wx[row - 1] + y_plus + pltpu.roll(y_plus, 1, 0)
        diagonal = diagonal + z_plus + pltpu.roll(z_plus, 1, 1) + screening
        inverse[row] = 1.0 / diagonal
        return carry

    lax.fori_loop(1, total - 1, weigh, 0, unroll=6)


def solve(band, tiles, slot_of, middle, left, right, before, after, wx, wy, wz, inverse, out, frames, u0, u1, residual, potential):
    rows, width = middle.shape[0], wx.shape[1]
    center_value = 0.5 * (spectrum_high + spectrum_low)
    half_width = 0.5 * (spectrum_high - spectrum_low)
    ratio = center_value / half_width

    def start(row, source):
        r = source * inverse[row]
        residual[row] = r
        u = r * (1.0 / center_value)
        u0[row] = u
        potential[row] = u

    for row in range(WIDE):
        start(1 + row, before[row])
        start(1 + WIDE + rows + row, after[row])

    nothing = jnp.zeros((SIDE, DEPTH), jnp.float32)
    for row in range(rows):
        u1[row, pl.ds(0, SIDE), :] = nothing
        u1[row, pl.ds(width - SIDE, SIDE), :] = nothing
        u1[row, pl.ds(SIDE - WIDE, WIDE), :] = left[pl.ds(row * WIDE, WIDE), :]
        u1[row, pl.ds(width - SIDE, WIDE), :] = right[pl.ds(row * WIDE, WIDE), :]

    def begin(row, carry):
        lows, highs = u1[row, pl.ds(0, SIDE), :], u1[row, pl.ds(width - SIDE, SIDE), :]
        start(1 + WIDE + row, jnp.concatenate([lows, middle[row], highs], axis=0))
        return carry

    lax.fori_loop(0, rows, begin, 0, unroll=2)
    old, new = u0, u1
    rho = 1.0 / ratio
    for sweep in range(1, SWEEPS):
        rho_new = 1.0 / (2.0 * ratio - rho)
        a, b = rho_new * rho, 2.0 * rho_new / half_width
        last = sweep == SWEEPS - 1

        def step(row, carry):
            u = old[row]
            y_weight, z_weight = wy[row], wz[row]
            spread = wx[row] * old[row + 1] + wx[row - 1] * old[row - 1]
            spread = spread + y_weight * pltpu.roll(u, width - 1, 0) + pltpu.roll(y_weight * u, 1, 0)
            spread = spread + z_weight * pltpu.roll(u, DEPTH - 1, 1) + pltpu.roll(z_weight * u, 1, 1)
            r = residual[row] - u + inverse[row] * spread
            u = a * u + b * r
            potential[row] = potential[row] + u
            if not last:
                residual[row] = r
                new[row] = u
            return carry

        lax.fori_loop(1 + sweep, rows + 2 * WIDER - 1 - sweep, step, 0, unroll=4)
        old, new = new, old
        rho = rho_new
    inner = width - 2 * SIDE

    def give(row, carry):
        out[row] = potential[WIDER + row, pl.ds(SIDE, inner), :]
        return carry

    lax.fori_loop(0, rows, give, 0, unroll=2)
    frames[...] = jnp.zeros_like(frames)
    for local in range(TILE_ROWS * TILE_COLS):
        r, c = local // TILE_COLS, local % TILE_COLS
        slot = slot_of[band + local] // tiles
        for a in range(FRAME):
            frames[slot, pl.ds(a * FRAME, FRAME), :] = potential[
                WIDER + r * EDGE - RING + a, pl.ds(SIDE + c * EDGE - RING, FRAME), :
            ]


def unit_count(peers):
    return -(-2 * HALVES // peers)


def unit_places(peers):
    places = {}
    for face in range(4):
        for rest in range(HALVES):
            unit = face % 2 * HALVES + rest
            row = (face // 2 * unit_count(peers) + unit // peers) * 8
            places[face, rest // 2, rest % 2] = (unit % peers, row)
    return places


def x_slots(peers):
    return -(-HALVES // peers), HALVES // peers


FACES = ((0, -1), (0, 1), (1, -1), (1, 1))


def open_sides(mask, bits, flags):
    column = lax.broadcasted_iota(jnp.int32, (EDGE + 2, DEPTH), 0)
    inner = (column > 0) & (column < EDGE + 1)
    for i in range(EDGE + 2):
        row = jnp.where(inner, mask[0, i], 0) if 0 < i < EDGE + 1 else jnp.zeros((EDGE + 2, DEPTH), jnp.int32)
        flags[1, i, pl.ds(SIDE - 1, EDGE + 2), :] = row
        flags[2, i, pl.ds(SIDE - 1, EDGE + 2), :] = pltpu.roll(row, 1, 1)
        flags[0, i, pl.ds(SIDE - 1, EDGE + 2), :] = pltpu.roll(row, DEPTH - 1, 1)

    def gather(i, carry):
        total = jnp.zeros((EDGE, DEPTH), jnp.int32)
        for q in range(19):
            cx, cy, cz = LATTICE[q]
            total = total + flags[cz + 1, i + 1 - cx, pl.ds(SIDE - cy, EDGE), :] * (1 << q)
        own = flags[1, i + 1, pl.ds(SIDE, EDGE), :]
        bits[0, pl.ds(pl.multiple_of(i * EDGE, EDGE), EDGE), :] = jnp.where(own == 1, total, 0)
        return carry

    lax.fori_loop(0, EDGE, gather, 0, unroll=4)


def raw_faces(peers, pops, charge, mask, out, bits, flags):
    open_sides(mask, bits, flags)
    places = unit_places(peers)
    taken = set(places.values())
    for peer in range(peers):
        for row in range(0, out.shape[2], 8):
            if (peer, row) not in taken:
                out[peer, 0, pl.ds(row, 8), :] = jnp.zeros((8, DEPTH), jnp.float32)
    for face, (axis, sign) in enumerate(FACES):
        layer = 0 if sign < 0 else EDGE - 1
        for half in range(2):
            if axis == 0:
                where = pl.ds(layer * EDGE + 8 * half, 8)
            else:
                where = pl.ds(8 * half * EDGE + layer, 8, stride=EDGE)
            values = [pops[q, 0, where, :] for q in range(19)]
            density, momentum = moments(values)
            channels = [values[q] for q in crossing(axis, sign)]
            channels += [density] + momentum + [charge[0, where, :]]
            for channel, value in enumerate(channels):
                peer, row = places[face, channel, half]
                out[peer, 0, pl.ds(row, 8), :] = value


def outer_rows(peers, band_cols, slot_of, arrived, low, high):
    count = unit_count(peers)
    low_count, first_high = x_slots(peers)
    for col in range(band_cols):
        low[col] = arrived[slot_of[col], pl.ds(0, low_count * 8), :]
        slot = slot_of[(TILE_ROWS - 1) * band_cols + col]
        high[col] = arrived[slot, pl.ds(first_high * 8, (count - first_high) * 8), :]


def turn_faces(peers, band_cols, slot_of, tile_at, me_ref, arrived, below, above, out, from_low, from_high):
    count = unit_count(peers)
    low_count, first_high = x_slots(peers)
    lows, highs = pl.ds(0, low_count * 8), pl.ds(first_high * 8, (count - first_high) * 8)

    def lay(col, carry):
        from_low[col] = below[col]
        from_high[(TILE_ROWS - 1) * band_cols + col] = above[col]
        for row in range(1, TILE_ROWS):
            from_low[row * band_cols + col] = arrived[slot_of[(row - 1) * band_cols + col], highs, :]
            from_high[(row - 1) * band_cols + col] = arrived[slot_of[row * band_cols + col], lows, :]
        return carry

    lax.fori_loop(0, band_cols, lay, 0, unroll=2)
    me = me_ref[0]
    half = me % 2
    is_low = [n * peers + me < HALVES for n in range(count)]

    def across_x(position, n, row, size):
        if n < low_count:
            value = from_high[position, pl.ds(n * 8 + row, size), :]
        if n >= first_high:
            other = from_low[position, pl.ds((n - first_high) * 8 + row, size), :]
            value = jnp.where(is_low[n], value, other) if n < low_count else other
        return value

    def send(d, carry):
        p = tile_at[d]
        row, col = p // band_cols, p % band_cols
        right, left = (col + 1) % band_cols, (col + band_cols - 1) % band_cols
        slot_right = slot_of[row * band_cols + right]
        slot_left = slot_of[row * band_cols + left]
        beside = row * band_cols + jnp.where(half == 0, right, left)
        for n in range(count):
            out[d, pl.ds(n * 8, 8), :] = across_x(p, n, 0, 8)
            cells = pl.ds((count + n) * 8, 8)
            out[d, cells, :] = arrived[jnp.where(is_low[n], slot_right, slot_left), cells, :]
            out[d, pl.ds(2 * count * 8 + n, 1), :] = across_x(beside, n, 7 * half, 1)
        return carry

    lax.fori_loop(0, out.shape[0], send, 0, unroll=2)


ACROSS_X = [q for q in range(19) if LATTICE[q][0]]
ACROSS_Y = [q for q in range(19) if LATTICE[q][1]]


def field_of(x_low, x_high, y_low, y_high, here):
    return [
        0.5 * (x_low - x_high),
        0.5 * (y_low - y_high),
        0.5 * (pltpu.roll(here, 1, 1) - pltpu.roll(here, DEPTH - 1, 1)),
    ]


def flux(speed_a, speed_b, a, b, flag_a, flag_b):
    face = 0.5 * (speed_a + speed_b)
    return jnp.where((flag_a == 1) & (flag_b == 1), face * jnp.where(face > 0, a, b), 0.0)


def step_inside(ids, pops, charge, bits, frame, out, charge_out, edges, bands, lines, near, relaxed, conc, vx, vy, vz):
    for a in range(FRAME):
        near[a, pl.ds(SIDE - RING, FRAME), :] = frame[0, pl.ds(a * FRAME, FRAME), :]

    def relax_row(i, carry):
        cells = pl.ds(pl.multiple_of(i * EDGE, EDGE), EDGE)
        field = field_of(
            near[i + RING - 1, pl.ds(SIDE, EDGE), :], near[i + RING + 1, pl.ds(SIDE, EDGE), :],
            near[i + RING, pl.ds(SIDE - 1, EDGE), :], near[i + RING, pl.ds(SIDE + 1, EDGE), :],
            near[i + RING, pl.ds(SIDE, EDGE), :],
        )
        values = [pops[q, 0, cells, :] for q in range(19)]
        held = charge[0, cells, :]
        force = [held * f for f in field]
        density, momentum = moments(values)
        done, velocity = collide(dict(enumerate(values)), density, momentum, force)
        for q in range(19):
            relaxed[q, i + 1, pl.ds(SIDE, EDGE), :] = done[q]
        conc[i + 1, pl.ds(SIDE, EDGE), :] = held
        vx[i + 1, pl.ds(SIDE, EDGE), :] = velocity[0]
        vy[i + 1, pl.ds(SIDE, EDGE), :] = velocity[1]
        vz[i + 1, pl.ds(SIDE, EDGE), :] = velocity[2]
        return carry

    lax.fori_loop(0, EDGE, relax_row, 0, unroll=4)
    flat_vy = vy.reshape((EDGE + 2) * PADDED, DEPTH)
    edges[0, 0] = vx[1, pl.ds(SIDE, EDGE), :]
    edges[0, 1] = vx[EDGE, pl.ds(SIDE, EDGE), :]
    edges[0, 2] = flat_vy[pl.ds(PADDED + SIDE, EDGE, stride=PADDED), :]
    edges[0, 3] = flat_vy[pl.ds(PADDED + SIDE + EDGE - 1, EDGE, stride=PADDED), :]

    def stream_row(i, carry):
        cells = pl.ds(pl.multiple_of(i * EDGE, EDGE), EDGE)
        here = i + 1
        mid = pl.ds(SIDE, EDGE)
        bit = bits[0, cells, :]
        is_open = [(bit & (1 << q)) != 0 for q in range(19)]
        for q in range(19):
            cx, cy, cz = LATTICE[q]
            pulled = relaxed[q, here - cx, pl.ds(SIDE - cy, EDGE), :]
            if cz:
                pulled = pltpu.roll(pulled, cz % DEPTH, 1)
            kept = pops[q, 0, cells, :]
            if q:
                kept = jnp.where(is_open[0], relaxed[opposite(q), here, mid, :], kept)
            out[q, 0, cells, :] = jnp.where(is_open[q], pulled, kept)
        held = conc[here, mid, :]

        def through(q, speed_a, speed_b, a, b):
            face = 0.5 * (speed_a + speed_b)
            return jnp.where(is_open[q], face * jnp.where(face > 0, a, b), 0.0)

        change = through(2, vx[here, mid, :], vx[here + 1, mid, :], held, conc[here + 1, mid, :])
        change = change - through(1, vx[here - 1, mid, :], vx[here, mid, :], conc[here - 1, mid, :], held)
        low, high = pl.ds(SIDE - 1, EDGE), pl.ds(SIDE + 1, EDGE)
        change = change + through(4, vy[here, mid, :], vy[here, high, :], held, conc[here, high, :])
        change = change - through(3, vy[here, low, :], vy[here, mid, :], conc[here, low, :], held)
        speed = vz[here, mid, :]
        z_flux = through(6, speed, pltpu.roll(speed, DEPTH - 1, 1), held, pltpu.roll(held, DEPTH - 1, 1))
        change = change + (z_flux - pltpu.roll(z_flux, 1, 1))
        charge_out[0, cells, :] = held - change
        return carry

    lax.fori_loop(0, EDGE, stream_row, 0, unroll=4)
    for n, q in enumerate(ACROSS_Y):
        bands[0, n] = out[q, 0, pl.ds(0 if LATTICE[q][1] > 0 else EDGE - 1, EDGE, stride=EDGE), :]
    for n, q in enumerate(ACROSS_X):
        lines[0, n] = out[q, 0, pl.ds(0 if LATTICE[q][0] > 0 else AREA - EDGE, EDGE), :]


def step_faces(peers, tiles, band_cols, ids, charge_at, mask_at, frames_at, rims_at, edges_at, bands_at, lines_at,
               charge_in_at, _, charge_out_at, out, charge, mask, frames, rims, edges, new_bands, lines, charge_out,
               all_near, all_flags, all_rim, all_x, all_y, new_lines, in_sems, out_sems):
    places = unit_places(peers)
    corner_row = 2 * unit_count(peers) * 8
    all_flat_near = all_near.reshape(tiles, FRAME * PADDED, DEPTH)
    all_flat_flags = all_flags.reshape(tiles, (EDGE + 2) * PADDED, DEPTH)

    def pieces(tile):
        made = []
        for n, q in enumerate(ACROSS_Y):
            made.append((new_bands.at[tile, n], out.at[q, tile, :, 0 if LATTICE[q][1] > 0 else EDGE - 1]))
        for n, q in enumerate(ACROSS_X):
            layer = 0 if LATTICE[q][0] > 0 else EDGE - 1
            if LATTICE[q][1]:
                cells = pl.ds(1 if LATTICE[q][1] > 0 else 0, EDGE - 1)
                made.append((new_lines.at[tile, n, cells], out.at[q, tile, layer, cells]))
            else:
                made.append((new_lines.at[tile, n], out.at[q, tile, layer]))
        made.append((charge_out.at[tile], charge_out_at.at[tile]))
        return [pltpu.make_async_copy(a, b, out_sems.at[tile, n]) for n, (a, b) in enumerate(made)]

    def incoming(tile):
        owner = ids[tile] % band_cols // TILE_COLS
        pairs = [
            (mask_at.at[tile], mask.at[tile]),
            (frames_at.at[owner], frames.at[tile]),
            (rims_at.at[:, tile], rims.at[:, tile]),
            (charge_at.at[tile], charge.at[tile]),
            (charge_in_at.at[tile], charge_out.at[tile]),
            (edges_at.at[tile], edges.at[tile]),
            (lines_at.at[tile], lines.at[tile]),
            (bands_at.at[tile], new_bands.at[tile]),
        ]
        return [pltpu.make_async_copy(a, b, in_sems.at[tile, n]) for n, (a, b) in enumerate(pairs)]

    for tile in range(tiles):
        for copy in incoming(tile):
            copy.start()

    def patch(t, carry):
        near, flags, rim, beside_x, beside_y = (x.at[t] for x in (all_near, all_flags, all_rim, all_x, all_y))
        flat_near, flat_flags = all_flat_near.at[t], all_flat_flags.at[t]
        for copy in incoming(t):
            copy.wait()
        for a in range(FRAME):
            near[a, pl.ds(SIDE - RING, FRAME), :] = frames[t, pl.ds(a * FRAME, FRAME), :]
        for i in range(EDGE + 2):
            flags[i, pl.ds(SIDE - 1, EDGE + 2), :] = mask[t, i]

        for side, face, layer in ((0, 1, 0), (1, 0, EDGE + 1)):
            for channel in range(CHANNELS):
                for half in range(2):
                    peer, row = places[face, channel, half]
                    rim[channel, pl.ds(SIDE + 8 * half, 8), :] = rims[peer, t, pl.ds(row, 8), :]
                    corner = corner_row + row // 8
                    column = SIDE + EDGE if half == 0 else SIDE - 1
                    rim[channel, pl.ds(column, 1), :] = rims[peer, t, pl.ds(corner, 1), :]
            here = near[layer + 1]
            field = field_of(
                near[layer], near[layer + 2], pltpu.roll(here, 1, 0), pltpu.roll(here, PADDED - 1, 0), here
            )
            density, momentum, held = rim[5], [rim[6], rim[7], rim[8]], rim[9]
            force = [held * f for f in field]
            dirs = crossing(*FACES[face])
            done, velocity = collide({q: rim[n] for n, q in enumerate(dirs)}, density, momentum, force)
            for n, q in enumerate(dirs):
                beside_x[side, n] = done[q]
            cells = pl.ds(0 if side == 0 else AREA - EDGE, EDGE)
            own_layer = 0 if side == 0 else EDGE - 1
            inner = slice(SIDE, SIDE + EDGE)
            speed, own_speed = velocity[0][inner], edges[t, side]
            amount, own_amount = held[inner], charge[t, cells, :]
            flag, own_flag = flags[layer, pl.ds(SIDE, EDGE), :], flags[own_layer + 1, pl.ds(SIDE, EDGE), :]
            if side == 0:
                charge_out[t, cells, :] += flux(speed, own_speed, amount, own_amount, flag, own_flag)
            else:
                charge_out[t, cells, :] -= flux(own_speed, speed, own_amount, amount, own_flag, flag)
            for n, q in enumerate(dirs):
                _, cy, cz = LATTICE[q]
                columns = pl.ds(SIDE - cy, EDGE)
                value, flag = beside_x[side, n, columns, :], flags[layer, columns, :]
                if cz:
                    value, flag = pltpu.roll(value, cz % DEPTH, 1), pltpu.roll(flag, cz % DEPTH, 1)
                line = ACROSS_X.index(q)
                taken = (flag == 1) & (own_flag == 1)
                merged = jnp.where(taken, value, lines[t, line])
                new_lines[t, line] = merged

        for side, face, column in ((0, 3, SIDE - 1), (1, 2, SIDE + EDGE)):
            dirs = crossing(*FACES[face])
            x_dirs = [crossing(*FACES[1]), crossing(*FACES[0])]
            own_column = 0 if side == 0 else EDGE - 1
            for half in range(2):
                def at(row, col):
                    return flat_near[pl.ds((RING + 8 * half + row) * PADDED + col, 8, stride=PADDED), :]

                raw = [rims[places[face, c, half][0], t, pl.ds(places[face, c, half][1], 8), :]
                       for c in range(CHANNELS)]
                field = field_of(at(-1, column), at(1, column), at(0, column - 1), at(0, column + 1), at(0, column))
                force = [raw[9] * f for f in field]
                done, velocity = collide({q: raw[n] for n, q in enumerate(dirs)}, raw[5], raw[6:9], force)
                for n, q in enumerate(dirs):
                    beside_y[side, n, pl.ds(SIDE + 8 * half, 8), :] = done[q]
                cells = pl.ds(8 * half * EDGE + own_column, 8, stride=EDGE)
                own_flag = flat_flags[pl.ds((1 + 8 * half) * PADDED + SIDE + own_column, 8, stride=PADDED), :]
                flag = flat_flags[pl.ds((1 + 8 * half) * PADDED + column, 8, stride=PADDED), :]
                own_speed, own_amount = edges[t, 2 + side, pl.ds(8 * half, 8), :], charge[t, cells, :]
                if side == 0:
                    charge_out[t, cells, :] += flux(velocity[1], own_speed, raw[9], own_amount, flag, own_flag)
                else:
                    charge_out[t, cells, :] -= flux(own_speed, velocity[1], own_amount, raw[9], own_flag, flag)
            own_flag = flat_flags[pl.ds(PADDED + SIDE + own_column, EDGE, stride=PADDED), :]
            for n, q in enumerate(dirs):
                cx, _, cz = LATTICE[q]
                if cx:
                    end = 0 if cx > 0 else 1
                    row = SIDE - 1 if cx > 0 else SIDE + EDGE
                    beside_y[side, n, pl.ds(row, 1), :] = beside_x[end, x_dirs[end].index(q), pl.ds(column, 1), :]
                value = beside_y[side, n, pl.ds(SIDE - cx, EDGE), :]
                flag = flat_flags[pl.ds((1 - cx) * PADDED + column, EDGE, stride=PADDED), :]
                if cz:
                    value, flag = pltpu.roll(value, cz % DEPTH, 1), pltpu.roll(flag, cz % DEPTH, 1)
                band = ACROSS_Y.index(q)
                new_bands[t, band] = jnp.where((flag == 1) & (own_flag == 1), value, new_bands[t, band])
        for copy in pieces(t):
            copy.start()
        return carry

    lax.fori_loop(0, tiles, patch, 0, unroll=2)
    for tile in range(tiles):
        for copy in pieces(tile):
            copy.wait()


def per_device(populations, charge, fluid_mask, tile_ids, phase_label, permittivity):
    peers = lax.axis_size("gy")
    tiles = charge.shape[0]
    rows, cols = phase_label.shape[0], phase_label.shape[1]
    band_cols = TILE_COLS * peers
    band = peers * tiles
    count = unit_count(peers)
    low_count, first_high = x_slots(peers)
    out_rows = 2 * count * 8
    in_rows = out_rows + -(-count // 8) * 8
    f32 = jnp.float32
    shape = jax.ShapeDtypeStruct
    gx_up, gx_down = ring_pairs("gx")
    gy_up, gy_down = ring_pairs("gy")
    me = lax.axis_index("gy").astype(jnp.int32)
    pops = pltpu.with_memory_space_constraint(populations.reshape(19, tiles, AREA, DEPTH), pltpu.HBM)
    held = charge.reshape(tiles, AREA, DEPTH)

    outgoing = pl.pallas_call(
        functools.partial(pack_source, tiles, band_cols),
        out_shape=pltpu.HBM((peers, AREA + 8, DEPTH), f32),
        in_specs=[SMEM, VMEM, VMEM], out_specs=VMEM, compiler_params=room(6), name="pack_source",
    )(tile_ids, held, fluid_mask)
    outgoing, phase_label = lax.optimization_barrier((outgoing, phase_label))
    arrived = lax.all_to_all(outgoing, "gy", split_axis=0, concat_axis=0, tiled=True)

    beside = [lax.ppermute(phase_label[rows - WIDER :], "gx", gx_up)]
    beside.append(lax.ppermute(phase_label[:WIDER], "gx", gx_down))

    one_tile = pl.BlockSpec((1, AREA, DEPTH), lambda t: (t, 0, 0))
    raw, bits = pl.pallas_call(
        functools.partial(raw_faces, peers),
        grid=(tiles,),
        out_shape=[pltpu.HBM((peers, tiles, out_rows, DEPTH), f32), pltpu.HBM(held.shape, jnp.int32)],
        in_specs=[
            pl.BlockSpec((19, 1, AREA, DEPTH), lambda t: (0, t, 0, 0)),
            one_tile,
            pl.BlockSpec((1, EDGE + 2, EDGE + 2, DEPTH), lambda t: (t, 0, 0, 0)),
        ],
        out_specs=[pl.BlockSpec((peers, 1, out_rows, DEPTH), lambda t: (0, t, 0, 0)), one_tile],
        scratch_shapes=[pltpu.VMEM((3, EDGE + 2, PADDED, DEPTH), jnp.int32)],
        compiler_params=room(14), name="raw_faces",
    )(pops, held, fluid_mask)
    beside[0], beside[1], raw = lax.optimization_barrier((beside[0], beside[1], raw))
    columns = (rows + 2 * WIDER) * WIDER
    lows, highs = pl.pallas_call(
        edge_columns, out_shape=[shape((columns, DEPTH), jnp.int32)] * 2, in_specs=[VMEM] * 3, out_specs=[VMEM] * 2,
        compiler_params=room(4), name="edge_columns",
    )(beside[0], phase_label, beside[1])
    beside += [lax.ppermute(highs, "gy", gy_up), lax.ppermute(lows, "gy", gy_down)]
    arrived, raw, beside = lax.optimization_barrier((arrived, raw, beside))
    beside = list(beside)

    tile_at = arrived[:, AREA, :tiles].astype(jnp.int32).reshape(band)
    slots = jnp.arange(band, dtype=jnp.int32)
    local = jnp.arange(tiles, dtype=jnp.int32)
    mine = local // TILE_COLS * band_cols + TILE_COLS * me + local % TILE_COLS
    wanted = jnp.concatenate([slots, mine])
    slot_of = jnp.sum(jnp.where(tile_at[None, :] == wanted[:, None], slots[None, :], 0), axis=1)

    block, left, right = pl.pallas_call(
        functools.partial(assemble, band, tiles),
        out_shape=[pltpu.VMEM((rows, cols, DEPTH), f32), shape((rows * WIDE, DEPTH), f32), shape((rows * WIDE, DEPTH), f32)],
        in_specs=[SMEM, VMEM], out_specs=[VMEM] * 3, compiler_params=room(5), name="assemble",
    )(slot_of, arrived)
    left, right = lax.ppermute(right, "gy", gy_up), lax.ppermute(left, "gy", gy_down)
    left, right, raw = lax.optimization_barrier((left, right, raw))
    ends = shape((WIDE, cols + 2 * SIDE, DEPTH), f32)
    ups, downs = pl.pallas_call(
        edge_rows, out_shape=[ends, ends], in_specs=[VMEM] * 3, out_specs=[VMEM] * 2,
        compiler_params=room(3), name="edge_rows",
    )(block, left, right)
    ups, downs, beside[0] = lax.optimization_barrier((ups, downs, beside[0]))
    before, after = lax.ppermute(ups, "gx", gx_up), lax.ppermute(downs, "gx", gx_down)
    hbm = pl.BlockSpec(memory_space=pl.ANY)
    wide = shape((rows + 2 * WIDER, cols + 2 * SIDE, DEPTH), f32)
    scratch = pltpu.VMEM(wide.shape, f32)
    weights = pl.pallas_call(
        face_weights, out_shape=[pltpu.VMEM(wide.shape, f32)] * 4, in_specs=[SMEM] + [VMEM] * 5, out_specs=[VMEM] * 4,
        scratch_shapes=[scratch], compiler_params=room(12), name="face_weights",
    )(permittivity, phase_label, *beside)

    faces = lax.all_to_all(raw, "gy", split_axis=0, concat_axis=0, tiled=True).reshape(band, out_rows, DEPTH)
    faces = pltpu.with_memory_space_constraint(faces, pltpu.HBM)
    potential, frames = pl.pallas_call(
        functools.partial(solve, band, tiles),
        out_shape=[shape((rows, cols, DEPTH), f32), pltpu.HBM((peers, FRAME * FRAME, DEPTH), f32)],
        in_specs=[SMEM] + [VMEM] * 9, out_specs=[VMEM, VMEM],
        scratch_shapes=[scratch] * 4, compiler_params=room(16), name="solve",
    )(slot_of, block, left, right, before, after, *weights)
    frames = lax.all_to_all(frames, "gy", split_axis=0, concat_axis=0, tiled=True)

    lows = (band_cols, low_count * 8, DEPTH)
    highs = (band_cols, (count - first_high) * 8, DEPTH)
    low, high = pl.pallas_call(
        functools.partial(outer_rows, peers, band_cols),
        out_shape=[shape(lows, f32), shape(highs, f32)], in_specs=[SMEM, VMEM], out_specs=[VMEM] * 2,
        compiler_params=room(5), name="outer_rows",
    )(slot_of, faces)
    below = lax.ppermute(high, "gx", gx_up)
    above = lax.ppermute(low, "gx", gx_down)
    turned = pl.pallas_call(
        functools.partial(turn_faces, peers, band_cols),
        out_shape=pltpu.HBM((band, in_rows, DEPTH), f32),
        in_specs=[SMEM, SMEM, SMEM, VMEM, VMEM, VMEM], out_specs=VMEM,
        scratch_shapes=[pltpu.VMEM((band,) + highs[1:], f32), pltpu.VMEM((band,) + lows[1:], f32)], compiler_params=room(8), name="turn_faces",
    )(slot_of, tile_at, me[None], faces, below, above)
    rims = lax.all_to_all(turned.reshape(peers, tiles, in_rows, DEPTH), "gy", split_axis=0, concat_axis=0, tiled=True)

    padded = pltpu.VMEM((EDGE + 2, PADDED, DEPTH), f32)
    near = pltpu.VMEM((FRAME, PADDED, DEPTH), f32)
    by_tile = pl.BlockSpec((1, AREA, DEPTH), lambda t, ids: (t, 0, 0))
    of_pops = pl.BlockSpec((19, 1, AREA, DEPTH), lambda t, ids: (0, t, 0, 0))
    of_frame = pl.BlockSpec((1, FRAME * FRAME, DEPTH), lambda t, ids: (ids[t] % band_cols // TILE_COLS, 0, 0))
    of_edges = pl.BlockSpec((1, 4, EDGE, DEPTH), lambda t, ids: (t, 0, 0, 0))
    bits = pltpu.with_memory_space_constraint(bits, pltpu.HBM)
    closed, closed_charge, edges, bands, lines = pl.pallas_call(
        step_inside,
        grid_spec=pltpu.PrefetchScalarGridSpec(
            num_scalar_prefetch=1,
            grid=(tiles,),
            in_specs=[of_pops, by_tile, by_tile, of_frame],
            out_specs=[
                of_pops, by_tile, of_edges,
                pl.BlockSpec((1, len(ACROSS_Y), EDGE, DEPTH), lambda t, ids: (t, 0, 0, 0)),
                pl.BlockSpec((1, len(ACROSS_X), EDGE, DEPTH), lambda t, ids: (t, 0, 0, 0)),
            ],
            scratch_shapes=[
                near,
                pltpu.VMEM((19, EDGE + 2, PADDED, DEPTH), f32),
                padded, padded, padded, padded,
            ],
        ),
        out_shape=[
            shape(pops.shape, f32), pltpu.HBM(held.shape, f32), shape((tiles, 4, EDGE, DEPTH), f32),
            pltpu.HBM((tiles, len(ACROSS_Y), EDGE, DEPTH), f32),
            pltpu.HBM((tiles, len(ACROSS_X), EDGE, DEPTH), f32),
        ],
        compiler_params=room(24), name="step_inside",
    )(tile_ids, pops, held, bits, frames)
    bands, lines, closed_charge = (
        pltpu.with_memory_space_constraint(x, pltpu.HBM) for x in (bands, lines, closed_charge)
    )
    charge_next, populations_next = pl.pallas_call(
        functools.partial(step_faces, peers, tiles, band_cols),
        in_specs=[SMEM] + [hbm] * 9,
        out_specs=[hbm, hbm],
        scratch_shapes=[
            pltpu.VMEM(held.shape, f32),
            pltpu.VMEM(fluid_mask.shape, jnp.int32),
            pltpu.VMEM((tiles, FRAME * FRAME, DEPTH), f32),
            pltpu.VMEM(rims.shape, f32),
            pltpu.VMEM(edges.shape, f32),
            pltpu.VMEM(bands.shape, f32),
            pltpu.VMEM(lines.shape, f32),
            pltpu.VMEM(held.shape, f32),
            pltpu.VMEM((tiles, FRAME, PADDED, DEPTH), f32),
            pltpu.VMEM((tiles, EDGE + 2, PADDED, DEPTH), jnp.int32),
            pltpu.VMEM((tiles, CHANNELS, PADDED, DEPTH), f32),
            pltpu.VMEM((tiles, 2, 5, PADDED, DEPTH), f32),
            pltpu.VMEM((tiles, 2, 5, PADDED, DEPTH), f32),
            pltpu.VMEM(lines.shape, f32),
            pltpu.SemaphoreType.DMA((tiles, 8)),
            pltpu.SemaphoreType.DMA((tiles, 1 + len(ACROSS_Y + ACROSS_X))),
        ],
        out_shape=[shape(held.shape, f32), shape(populations.shape, f32)],
        input_output_aliases={9: 1},
        compiler_params=room(20), name="step_faces",
    )(tile_ids, held, fluid_mask, frames, rims, edges, bands, lines, closed_charge, closed.reshape(populations.shape))
    return (populations_next, charge_next.reshape(charge.shape), potential)


def solution(mesh):
    placed = (
        P(None, ("gx", "gy"), None, None, None),
        P(("gx", "gy"), None, None, None),
        P(("gx", "gy"), None, None, None),
        P(("gx", "gy")),
        P("gx", "gy", None),
        P(),
    )
    return jax.shard_map(
        per_device,
        mesh=mesh,
        in_specs=placed,
        out_specs=(
            P(None, ("gx", "gy"), None, None, None),
            P(("gx", "gy"), None, None, None),
            P("gx", "gy", None),
        ),
        check_vma=False,
    )
```

```python
import functools

import jax
import jax.numpy as jnp
from jax import lax
from jax.experimental import pallas as pl
from jax.experimental.pallas import tpu as pltpu
from jax.sharding import PartitionSpec as P

EDGE = 16
DEPTH = 128
TILE_ROWS = 2
TILE_COLS = 2
PHASES = 4
SWEEPS = 4

LATTICE = (
    (0, 0, 0),
    (1, 0, 0),
    (-1, 0, 0),
    (0, 1, 0),
    (0, -1, 0),
    (0, 0, 1),
    (0, 0, -1),
    (1, 1, 0),
    (-1, -1, 0),
    (1, -1, 0),
    (-1, 1, 0),
    (1, 0, 1),
    (-1, 0, -1),
    (1, 0, -1),
    (-1, 0, 1),
    (0, 1, 1),
    (0, -1, -1),
    (0, 1, -1),
    (0, -1, 1),
)
relax_time = 0.8
screening = 0.001
spectrum_low = 0.1
spectrum_high = 2.0

AREA = EDGE * EDGE
SIDE = 8
RING = 2
WIDE = RING + SWEEPS - 1
WIDER = WIDE + 1
FRAME = EDGE + 2 * RING
PADDED = EDGE + 2 * SIDE
CHANNELS = 10
HALVES = 2 * CHANNELS
VMEM = pl.BlockSpec(memory_space=pltpu.VMEM)
SMEM = pl.BlockSpec(memory_space=pltpu.SMEM)


def room(mebibytes):
    return pltpu.CompilerParams(vmem_limit_bytes=mebibytes * 2**20)


def crossing(axis_index, face_sign):
    return [q for q in range(19) if LATTICE[q][axis_index] == face_sign]


def opposite(direction):
    return LATTICE.index(tuple(-entry for entry in LATTICE[direction]))


def lattice_weight(direction):
    return (1.0 / 3.0, 1.0 / 18.0, 1.0 / 36.0)[sum(abs(e) for e in LATTICE[direction])]


def along(direction, vector):
    total = None
    for entry, part in zip(LATTICE[direction], vector):
        if entry:
            term = part if entry > 0 else -part
            total = term if total is None else total + term
    return total


def moments(pops):
    density = pops[0]
    for q in range(1, 19):
        density = density + pops[q]
    momentum = []
    for axis in range(3):
        plus = sum_of([pops[q] for q in crossing(axis, 1)])
        minus = sum_of([pops[q] for q in crossing(axis, -1)])
        momentum.append(plus - minus)
    return density, momentum


def sum_of(values):
    total = values[0]
    for value in values[1:]:
        total = total + value
    return total


def collide(pops, density, momentum, force):
    source_scale = 1.0 - 0.5 / relax_time
    gain = 1.0 / relax_time
    inverse = 1.0 / density
    carried = [m + 0.5 * f for m, f in zip(momentum, force)]
    velocity = [c * inverse for c in carried]
    energy = sum_of([c * v for c, v in zip(carried, velocity)])
    power = sum_of([v * f for v, f in zip(velocity, force)])
    base = gain * density - (1.5 * gain) * energy - (3.0 * source_scale) * power
    relaxed = {}
    for q in pops:
        weight = lattice_weight(q)
        kept = (1.0 - gain) * pops[q]
        if q == 0:
            relaxed[q] = kept + weight * base
            continue
        if q in relaxed:
            continue
        p, g, rp = along(q, velocity), along(q, force), along(q, carried)
        even = weight * base + p * ((4.5 * gain * weight) * rp + (9.0 * source_scale * weight) * g)
        odd = (3.0 * gain * weight) * rp + (3.0 * source_scale * weight) * g
        relaxed[q] = kept + (even + odd)
        back = opposite(q)
        if back in pops:
            relaxed[back] = (1.0 - gain) * pops[back] + (even - odd)
    return relaxed, velocity


def ring_pairs(axis):
    size = lax.axis_size(axis)
    up = [(i, (i + 1) % size) for i in range(size)]
    return up, [(j, i) for i, j in up]


def pack_source(tiles, band_cols, ids, charge, mask, out):
    out[...] = jnp.zeros_like(out)
    lane = lax.broadcasted_iota(jnp.int32, (8, DEPTH), 1)
    header = jnp.zeros((8, DEPTH), jnp.int32)
    for t in range(tiles):
        owner = ids[t] % band_cols // TILE_COLS
        header = jnp.where(lane == t, ids[t], header)
        for i in range(EDGE):
            flags = mask[t, i + 1, 1 : EDGE + 1, :].astype(jnp.float32)
            out[owner, pl.ds(i * EDGE, EDGE), :] = charge[t, pl.ds(i * EDGE, EDGE), :] * flags
    for peer in range(out.shape[0]):
        out[peer, pl.ds(AREA, 8), :] = header.astype(jnp.float32)


def assemble(band, tiles, slot_of, arrived, block, left, right):
    for local in range(TILE_ROWS * TILE_COLS):
        r, c = local // TILE_COLS, local % TILE_COLS
        slot = slot_of[band + local] // tiles
        for i in range(EDGE):
            row = r * EDGE + i
            cells = arrived[slot, pl.ds(i * EDGE, EDGE), :]
            block[row, pl.ds(c * EDGE, EDGE), :] = cells
            if c == 0:
                left[pl.ds(row * WIDE, WIDE), :] = cells[:WIDE]
            if c == TILE_COLS - 1:
                right[pl.ds(row * WIDE, WIDE), :] = cells[EDGE - WIDE :]


def edge_columns(before, labels, after, lows, highs):
    rows, cols = labels.shape[0], labels.shape[1]
    for row in range(rows + 2 * WIDER):
        if row < WIDER:
            line = before.at[row]
        elif row < WIDER + rows:
            line = labels.at[row - WIDER]
        else:
            line = after.at[row - WIDER - rows]
        lows[pl.ds(row * WIDER, WIDER), :] = line[pl.ds(0, WIDER), :]
        highs[pl.ds(row * WIDER, WIDER), :] = line[pl.ds(cols - WIDER, WIDER), :]


def edge_rows(block, left, right, ups, downs):
    rows, cols = block.shape[0], block.shape[1]
    for row in range(WIDE):
        for out, source in ((ups, rows - WIDE + row), (downs, row)):
            out[row, pl.ds(0, SIDE), :] = jnp.zeros((SIDE, DEPTH), jnp.float32)
            out[row, pl.ds(SIDE + cols, SIDE), :] = jnp.zeros((SIDE, DEPTH), jnp.float32)
            out[row, pl.ds(SIDE - WIDE, WIDE), :] = left[pl.ds(source * WIDE, WIDE), :]
            out[row, pl.ds(SIDE, cols), :] = block[source]
            out[row, pl.ds(SIDE + cols, WIDE), :] = right[pl.ds(source * WIDE, WIDE), :]


def harmonic(a, b):
    return 2.0 * a * b / (a + b)


def face_weights(table, labels, before, after, left, right, wx, wy, wz, inverse, permit):
    rows, cols = labels.shape[0], labels.shape[1]
    total = rows + 2 * WIDER

    def look(label):
        value = jnp.full(label.shape, table[PHASES - 1], jnp.float32)
        for phase in range(PHASES - 1):
            value = jnp.where(label == phase, table[phase], value)
        return value

    for row in range(WIDER):
        permit[row, pl.ds(SIDE, cols), :] = look(before[row])
        permit[WIDER + rows + row, pl.ds(SIDE, cols), :] = look(after[row])

    for row in range(total):
        permit[row, pl.ds(0, SIDE), :] = jnp.ones((SIDE, DEPTH), jnp.float32)
        permit[row, pl.ds(SIDE + cols, SIDE), :] = jnp.ones((SIDE, DEPTH), jnp.float32)
        permit[row, pl.ds(SIDE - WIDER, WIDER), :] = look(left[pl.ds(row * WIDER, WIDER), :])
        permit[row, pl.ds(SIDE + cols, WIDER), :] = look(right[pl.ds(row * WIDER, WIDER), :])

    def fill(row, carry):
        permit[WIDER + row, pl.ds(SIDE, cols), :] = look(labels[row])
        return carry

    lax.fori_loop(0, rows, fill, 0, unroll=2)
    width = permit.shape[1]
    wx[0] = harmonic(permit[0], permit[1])

    def weigh(row, carry):
        here = permit[row]
        x_plus = harmonic(here, permit[row + 1])
        y_plus = harmonic(here, pltpu.roll(here, width - 1, 0))
        z_plus = harmonic(here, pltpu.roll(here, DEPTH - 1, 1))
        wx[row] = x_plus
        wy[row] = y_plus
        wz[row] = z_plus
        diagonal = x_plus + wx[row - 1] + y_plus + pltpu.roll(y_plus, 1, 0)
        diagonal = diagonal + z_plus + pltpu.roll(z_plus, 1, 1) + screening
        inverse[row] = 1.0 / diagonal
        return carry

    lax.fori_loop(1, total - 1, weigh, 0, unroll=6)


def solve(band, tiles, slot_of, middle, left, right, before, after, wx, wy, wz, inverse, out, frames, u0, u1, residual, potential):
    rows, width = middle.shape[0], wx.shape[1]
    center_value = 0.5 * (spectrum_high + spectrum_low)
    half_width = 0.5 * (spectrum_high - spectrum_low)
    ratio = center_value / half_width

    def start(row, source):
        r = source * inverse[row]
        residual[row] = r
        u = r * (1.0 / center_value)
        u0[row] = u
        potential[row] = u

    for row in range(WIDE):
        start(1 + row, before[row])
        start(1 + WIDE + rows + row, after[row])

    nothing = jnp.zeros((SIDE, DEPTH), jnp.float32)
    for row in range(rows):
        u1[row, pl.ds(0, SIDE), :] = nothing
        u1[row, pl.ds(width - SIDE, SIDE), :] = nothing
        u1[row, pl.ds(SIDE - WIDE, WIDE), :] = left[pl.ds(row * WIDE, WIDE), :]
        u1[row, pl.ds(width - SIDE, WIDE), :] = right[pl.ds(row * WIDE, WIDE), :]

    def begin(row, carry):
        lows, highs = u1[row, pl.ds(0, SIDE), :], u1[row, pl.ds(width - SIDE, SIDE), :]
        start(1 + WIDE + row, jnp.concatenate([lows, middle[row], highs], axis=0))
        return carry

    lax.fori_loop(0, rows, begin, 0, unroll=2)
    old, new = u0, u1
    rho = 1.0 / ratio
    for sweep in range(1, SWEEPS):
        rho_new = 1.0 / (2.0 * ratio - rho)
        a, b = rho_new * rho, 2.0 * rho_new / half_width
        last = sweep == SWEEPS - 1

        def step(row, carry):
            u = old[row]
            y_weight, z_weight = wy[row], wz[row]
            spread = wx[row] * old[row + 1] + wx[row - 1] * old[row - 1]
            spread = spread + y_weight * pltpu.roll(u, width - 1, 0) + pltpu.roll(y_weight * u, 1, 0)
            spread = spread + z_weight * pltpu.roll(u, DEPTH - 1, 1) + pltpu.roll(z_weight * u, 1, 1)
            r = residual[row] - u + inverse[row] * spread
            u = a * u + b * r
            potential[row] = potential[row] + u
            if not last:
                residual[row] = r
                new[row] = u
            return carry

        lax.fori_loop(1 + sweep, rows + 2 * WIDER - 1 - sweep, step, 0, unroll=4)
        old, new = new, old
        rho = rho_new
    inner = width - 2 * SIDE

    def give(row, carry):
        out[row] = potential[WIDER + row, pl.ds(SIDE, inner), :]
        return carry

    lax.fori_loop(0, rows, give, 0, unroll=2)
    frames[...] = jnp.zeros_like(frames)
    for local in range(TILE_ROWS * TILE_COLS):
        r, c = local // TILE_COLS, local % TILE_COLS
        slot = slot_of[band + local] // tiles
        for a in range(FRAME):
            frames[slot, pl.ds(a * FRAME, FRAME), :] = potential[
                WIDER + r * EDGE - RING + a, pl.ds(SIDE + c * EDGE - RING, FRAME), :
            ]


def unit_count(peers):
    return -(-2 * HALVES // peers)


def unit_places(peers):
    places = {}
    for face in range(4):
        for rest in range(HALVES):
            unit = face % 2 * HALVES + rest
            row = (face // 2 * unit_count(peers) + unit // peers) * 8
            places[face, rest // 2, rest % 2] = (unit % peers, row)
    return places


def x_slots(peers):
    return -(-HALVES // peers), HALVES // peers


FACES = ((0, -1), (0, 1), (1, -1), (1, 1))


def open_sides(mask, bits, flags):
    column = lax.broadcasted_iota(jnp.int32, (EDGE + 2, DEPTH), 0)
    inner = (column > 0) & (column < EDGE + 1)
    for i in range(EDGE + 2):
        row = jnp.where(inner, mask[0, i], 0) if 0 < i < EDGE + 1 else jnp.zeros((EDGE + 2, DEPTH), jnp.int32)
        flags[1, i, pl.ds(SIDE - 1, EDGE + 2), :] = row
        flags[2, i, pl.ds(SIDE - 1, EDGE + 2), :] = pltpu.roll(row, 1, 1)
        flags[0, i, pl.ds(SIDE - 1, EDGE + 2), :] = pltpu.roll(row, DEPTH - 1, 1)

    def gather(i, carry):
        total = jnp.zeros((EDGE, DEPTH), jnp.int32)
        for q in range(19):
            cx, cy, cz = LATTICE[q]
            total = total + flags[cz + 1, i + 1 - cx, pl.ds(SIDE - cy, EDGE), :] * (1 << q)
        own = flags[1, i + 1, pl.ds(SIDE, EDGE), :]
        bits[0, pl.ds(pl.multiple_of(i * EDGE, EDGE), EDGE), :] = jnp.where(own == 1, total, 0)
        return carry

    lax.fori_loop(0, EDGE, gather, 0, unroll=4)


def raw_faces(peers, pops, charge, mask, out, bits, flags):
    open_sides(mask, bits, flags)
    places = unit_places(peers)
    taken = set(places.values())
    for peer in range(peers):
        for row in range(0, out.shape[2], 8):
            if (peer, row) not in taken:
                out[peer, 0, pl.ds(row, 8), :] = jnp.zeros((8, DEPTH), jnp.float32)
    for face, (axis, sign) in enumerate(FACES):
        layer = 0 if sign < 0 else EDGE - 1
        for half in range(2):
            if axis == 0:
                where = pl.ds(layer * EDGE + 8 * half, 8)
            else:
                where = pl.ds(8 * half * EDGE + layer, 8, stride=EDGE)
            values = [pops[q, 0, where, :] for q in range(19)]
            density, momentum = moments(values)
            channels = [values[q] for q in crossing(axis, sign)]
            channels += [density] + momentum + [charge[0, where, :]]
            for channel, value in enumerate(channels):
                peer, row = places[face, channel, half]
                out[peer, 0, pl.ds(row, 8), :] = value


def outer_rows(peers, band_cols, slot_of, arrived, low, high):
    count = unit_count(peers)
    low_count, first_high = x_slots(peers)
    for col in range(band_cols):
        low[col] = arrived[slot_of[col], pl.ds(0, low_count * 8), :]
        slot = slot_of[(TILE_ROWS - 1) * band_cols + col]
        high[col] = arrived[slot, pl.ds(first_high * 8, (count - first_high) * 8), :]


def turn_faces(peers, band_cols, slot_of, tile_at, me_ref, arrived, below, above, out, from_low, from_high):
    count = unit_count(peers)
    low_count, first_high = x_slots(peers)
    lows, highs = pl.ds(0, low_count * 8), pl.ds(first_high * 8, (count - first_high) * 8)

    def lay(col, carry):
        from_low[col] = below[col]
        from_high[(TILE_ROWS - 1) * band_cols + col] = above[col]
        for row in range(1, TILE_ROWS):
            from_low[row * band_cols + col] = arrived[slot_of[(row - 1) * band_cols + col], highs, :]
            from_high[(row - 1) * band_cols + col] = arrived[slot_of[row * band_cols + col], lows, :]
        return carry

    lax.fori_loop(0, band_cols, lay, 0, unroll=2)
    me = me_ref[0]
    half = me % 2
    is_low = [n * peers + me < HALVES for n in range(count)]

    def across_x(position, n, row, size):
        if n < low_count:
            value = from_high[position, pl.ds(n * 8 + row, size), :]
        if n >= first_high:
            other = from_low[position, pl.ds((n - first_high) * 8 + row, size), :]
            value = jnp.where(is_low[n], value, other) if n < low_count else other
        return value

    def send(d, carry):
        p = tile_at[d]
        row, col = p // band_cols, p % band_cols
        right, left = (col + 1) % band_cols, (col + band_cols - 1) % band_cols
        slot_right = slot_of[row * band_cols + right]
        slot_left = slot_of[row * band_cols + left]
        beside = row * band_cols + jnp.where(half == 0, right, left)
        for n in range(count):
            out[d, pl.ds(n * 8, 8), :] = across_x(p, n, 0, 8)
            cells = pl.ds((count + n) * 8, 8)
            out[d, cells, :] = arrived[jnp.where(is_low[n], slot_right, slot_left), cells, :]
            out[d, pl.ds(2 * count * 8 + n, 1), :] = across_x(beside, n, 7 * half, 1)
        return carry

    lax.fori_loop(0, out.shape[0], send, 0, unroll=2)


ACROSS_X = [q for q in range(19) if LATTICE[q][0]]
ACROSS_Y = [q for q in range(19) if LATTICE[q][1]]


def field_of(x_low, x_high, y_low, y_high, here):
    return [
        0.5 * (x_low - x_high),
        0.5 * (y_low - y_high),
        0.5 * (pltpu.roll(here, 1, 1) - pltpu.roll(here, DEPTH - 1, 1)),
    ]


def flux(speed_a, speed_b, a, b, flag_a, flag_b):
    face = 0.5 * (speed_a + speed_b)
    return jnp.where((flag_a == 1) & (flag_b == 1), face * jnp.where(face > 0, a, b), 0.0)


def step_inside(ids, pops, charge, bits, frame, out, charge_out, edges, bands, lines, near, relaxed, conc, vx, vy, vz):
    for a in range(FRAME):
        near[a, pl.ds(SIDE - RING, FRAME), :] = frame[0, pl.ds(a * FRAME, FRAME), :]

    def relax_row(i, carry):
        cells = pl.ds(pl.multiple_of(i * EDGE, EDGE), EDGE)
        field = field_of(
            near[i + RING - 1, pl.ds(SIDE, EDGE), :], near[i + RING + 1, pl.ds(SIDE, EDGE), :],
            near[i + RING, pl.ds(SIDE - 1, EDGE), :], near[i + RING, pl.ds(SIDE + 1, EDGE), :],
            near[i + RING, pl.ds(SIDE, EDGE), :],
        )
        values = [pops[q, 0, cells, :] for q in range(19)]
        held = charge[0, cells, :]
        force = [held * f for f in field]
        density, momentum = moments(values)
        done, velocity = collide(dict(enumerate(values)), density, momentum, force)
        for q in range(19):
            relaxed[q, i + 1, pl.ds(SIDE, EDGE), :] = done[q]
        conc[i + 1, pl.ds(SIDE, EDGE), :] = held
        vx[i + 1, pl.ds(SIDE, EDGE), :] = velocity[0]
        vy[i + 1, pl.ds(SIDE, EDGE), :] = velocity[1]
        vz[i + 1, pl.ds(SIDE, EDGE), :] = velocity[2]
        return carry

    lax.fori_loop(0, EDGE, relax_row, 0, unroll=4)
    flat_vy = vy.reshape((EDGE + 2) * PADDED, DEPTH)
    edges[0, 0] = vx[1, pl.ds(SIDE, EDGE), :]
    edges[0, 1] = vx[EDGE, pl.ds(SIDE, EDGE), :]
    edges[0, 2] = flat_vy[pl.ds(PADDED + SIDE, EDGE, stride=PADDED), :]
    edges[0, 3] = flat_vy[pl.ds(PADDED + SIDE + EDGE - 1, EDGE, stride=PADDED), :]

    def stream_row(i, carry):
        cells = pl.ds(pl.multiple_of(i * EDGE, EDGE), EDGE)
        here = i + 1
        mid = pl.ds(SIDE, EDGE)
        bit = bits[0, cells, :]
        is_open = [(bit & (1 << q)) != 0 for q in range(19)]
        for q in range(19):
            cx, cy, cz = LATTICE[q]
            pulled = relaxed[q, here - cx, pl.ds(SIDE - cy, EDGE), :]
            if cz:
                pulled = pltpu.roll(pulled, cz % DEPTH, 1)
            kept = pops[q, 0, cells, :]
            if q:
                kept = jnp.where(is_open[0], relaxed[opposite(q), here, mid, :], kept)
            out[q, 0, cells, :] = jnp.where(is_open[q], pulled, kept)
        held = conc[here, mid, :]

        def through(q, speed_a, speed_b, a, b):
            face = 0.5 * (speed_a + speed_b)
            return jnp.where(is_open[q], face * jnp.where(face > 0, a, b), 0.0)

        change = through(2, vx[here, mid, :], vx[here + 1, mid, :], held, conc[here + 1, mid, :])
        change = change - through(1, vx[here - 1, mid, :], vx[here, mid, :], conc[here - 1, mid, :], held)
        low, high = pl.ds(SIDE - 1, EDGE), pl.ds(SIDE + 1, EDGE)
        change = change + through(4, vy[here, mid, :], vy[here, high, :], held, conc[here, high, :])
        change = change - through(3, vy[here, low, :], vy[here, mid, :], conc[here, low, :], held)
        speed = vz[here, mid, :]
        z_flux = through(6, speed, pltpu.roll(speed, DEPTH - 1, 1), held, pltpu.roll(held, DEPTH - 1, 1))
        change = change + (z_flux - pltpu.roll(z_flux, 1, 1))
        charge_out[0, cells, :] = held - change
        return carry

    lax.fori_loop(0, EDGE, stream_row, 0, unroll=4)
    for n, q in enumerate(ACROSS_Y):
        bands[0, n] = out[q, 0, pl.ds(0 if LATTICE[q][1] > 0 else EDGE - 1, EDGE, stride=EDGE), :]
    for n, q in enumerate(ACROSS_X):
        lines[0, n] = out[q, 0, pl.ds(0 if LATTICE[q][0] > 0 else AREA - EDGE, EDGE), :]


def step_faces(peers, tiles, band_cols, ids, charge_at, mask_at, frames_at, rims_at, edges_at, bands_at, lines_at,
               charge_in_at, _, charge_out_at, out, charge, mask, frames, rims, edges, new_bands, lines, charge_out,
               all_near, all_flags, all_rim, all_x, all_y, new_lines, in_sems, out_sems):
    places = unit_places(peers)
    corner_row = 2 * unit_count(peers) * 8
    all_flat_near = all_near.reshape(tiles, FRAME * PADDED, DEPTH)
    all_flat_flags = all_flags.reshape(tiles, (EDGE + 2) * PADDED, DEPTH)

    group = tiles // 2 if tiles % 2 == 0 else tiles

    def pieces(part):
        some = pl.ds(part * group, group)
        made = []
        for n, q in enumerate(ACROSS_Y):
            made.append((new_bands.at[some, n], out.at[q, some, :, 0 if LATTICE[q][1] > 0 else EDGE - 1]))
        for n, q in enumerate(ACROSS_X):
            layer = 0 if LATTICE[q][0] > 0 else EDGE - 1
            if LATTICE[q][1]:
                cells = pl.ds(1 if LATTICE[q][1] > 0 else 0, EDGE - 1)
                made.append((new_lines.at[some, n, cells], out.at[q, some, layer, cells]))
            else:
                made.append((new_lines.at[some, n], out.at[q, some, layer]))
        made.append((charge_out.at[some], charge_out_at.at[some]))
        return [pltpu.make_async_copy(a, b, out_sems.at[part, n]) for n, (a, b) in enumerate(made)]

    def incoming(tile):
        owner = ids[tile] % band_cols // TILE_COLS
        pairs = [
            (mask_at.at[tile], mask.at[tile]),
            (frames_at.at[owner], frames.at[tile]),
            (rims_at.at[:, tile], rims.at[:, tile]),
            (charge_at.at[tile], charge.at[tile]),
            (charge_in_at.at[tile], charge_out.at[tile]),
            (edges_at.at[tile], edges.at[tile]),
            (lines_at.at[tile], lines.at[tile]),
            (bands_at.at[tile], new_bands.at[tile]),
        ]
        return [pltpu.make_async_copy(a, b, in_sems.at[tile, n]) for n, (a, b) in enumerate(pairs)]

    for tile in range(tiles):
        for copy in incoming(tile):
            copy.start()

    def patch(t, carry):
        near, flags, rim, beside_x, beside_y = (x.at[t] for x in (all_near, all_flags, all_rim, all_x, all_y))
        flat_near, flat_flags = all_flat_near.at[t], all_flat_flags.at[t]
        for copy in incoming(t):
            copy.wait()
        for a in range(FRAME):
            near[a, pl.ds(SIDE - RING, FRAME), :] = frames[t, pl.ds(a * FRAME, FRAME), :]
        for i in range(EDGE + 2):
            flags[i, pl.ds(SIDE - 1, EDGE + 2), :] = mask[t, i]

        for side, face, layer in ((0, 1, 0), (1, 0, EDGE + 1)):
            for channel in range(CHANNELS):
                for half in range(2):
                    peer, row = places[face, channel, half]
                    rim[channel, pl.ds(SIDE + 8 * half, 8), :] = rims[peer, t, pl.ds(row, 8), :]
                    corner = corner_row + row // 8
                    column = SIDE + EDGE if half == 0 else SIDE - 1
                    rim[channel, pl.ds(column, 1), :] = rims[peer, t, pl.ds(corner, 1), :]
            here = near[layer + 1]
            field = field_of(
                near[layer], near[layer + 2], pltpu.roll(here, 1, 0), pltpu.roll(here, PADDED - 1, 0), here
            )
            density, momentum, held = rim[5], [rim[6], rim[7], rim[8]], rim[9]
            force = [held * f for f in field]
            dirs = crossing(*FACES[face])
            done, velocity = collide({q: rim[n] for n, q in enumerate(dirs)}, density, momentum, force)
            for n, q in enumerate(dirs):
                beside_x[side, n] = done[q]
            cells = pl.ds(0 if side == 0 else AREA - EDGE, EDGE)
            own_layer = 0 if side == 0 else EDGE - 1
            inner = slice(SIDE, SIDE + EDGE)
            speed, own_speed = velocity[0][inner], edges[t, side]
            amount, own_amount = held[inner], charge[t, cells, :]
            flag, own_flag = flags[layer, pl.ds(SIDE, EDGE), :], flags[own_layer + 1, pl.ds(SIDE, EDGE), :]
            if side == 0:
                charge_out[t, cells, :] += flux(speed, own_speed, amount, own_amount, flag, own_flag)
            else:
                charge_out[t, cells, :] -= flux(own_speed, speed, own_amount, amount, own_flag, flag)
            for n, q in enumerate(dirs):
                _, cy, cz = LATTICE[q]
                columns = pl.ds(SIDE - cy, EDGE)
                value, flag = beside_x[side, n, columns, :], flags[layer, columns, :]
                if cz:
                    value, flag = pltpu.roll(value, cz % DEPTH, 1), pltpu.roll(flag, cz % DEPTH, 1)
                line = ACROSS_X.index(q)
                taken = (flag == 1) & (own_flag == 1)
                merged = jnp.where(taken, value, lines[t, line])
                new_lines[t, line] = merged

        for side, face, column in ((0, 3, SIDE - 1), (1, 2, SIDE + EDGE)):
            dirs = crossing(*FACES[face])
            x_dirs = [crossing(*FACES[1]), crossing(*FACES[0])]
            own_column = 0 if side == 0 else EDGE - 1
            for half in range(2):
                def at(row, col):
                    return flat_near[pl.ds((RING + 8 * half + row) * PADDED + col, 8, stride=PADDED), :]

                raw = [rims[places[face, c, half][0], t, pl.ds(places[face, c, half][1], 8), :]
                       for c in range(CHANNELS)]
                field = field_of(at(-1, column), at(1, column), at(0, column - 1), at(0, column + 1), at(0, column))
                force = [raw[9] * f for f in field]
                done, velocity = collide({q: raw[n] for n, q in enumerate(dirs)}, raw[5], raw[6:9], force)
                for n, q in enumerate(dirs):
                    beside_y[side, n, pl.ds(SIDE + 8 * half, 8), :] = done[q]
                cells = pl.ds(8 * half * EDGE + own_column, 8, stride=EDGE)
                own_flag = flat_flags[pl.ds((1 + 8 * half) * PADDED + SIDE + own_column, 8, stride=PADDED), :]
                flag = flat_flags[pl.ds((1 + 8 * half) * PADDED + column, 8, stride=PADDED), :]
                own_speed, own_amount = edges[t, 2 + side, pl.ds(8 * half, 8), :], charge[t, cells, :]
                if side == 0:
                    charge_out[t, cells, :] += flux(velocity[1], own_speed, raw[9], own_amount, flag, own_flag)
                else:
                    charge_out[t, cells, :] -= flux(own_speed, velocity[1], own_amount, raw[9], own_flag, flag)
            own_flag = flat_flags[pl.ds(PADDED + SIDE + own_column, EDGE, stride=PADDED), :]
            for n, q in enumerate(dirs):
                cx, _, cz = LATTICE[q]
                if cx:
                    end = 0 if cx > 0 else 1
                    row = SIDE - 1 if cx > 0 else SIDE + EDGE
                    beside_y[side, n, pl.ds(row, 1), :] = beside_x[end, x_dirs[end].index(q), pl.ds(column, 1), :]
                value = beside_y[side, n, pl.ds(SIDE - cx, EDGE), :]
                flag = flat_flags[pl.ds((1 - cx) * PADDED + column, EDGE, stride=PADDED), :]
                if cz:
                    value, flag = pltpu.roll(value, cz % DEPTH, 1), pltpu.roll(flag, cz % DEPTH, 1)
                band = ACROSS_Y.index(q)
                new_bands[t, band] = jnp.where((flag == 1) & (own_flag == 1), value, new_bands[t, band])
        return carry

    for part in range(tiles // group):
        lax.fori_loop(part * group, (part + 1) * group, patch, 0, unroll=2)
        for copy in pieces(part):
            copy.start()
    for part in range(tiles // group):
        for copy in pieces(part):
            copy.wait()


def per_device(populations, charge, fluid_mask, tile_ids, phase_label, permittivity):
    peers = lax.axis_size("gy")
    tiles = charge.shape[0]
    rows, cols = phase_label.shape[0], phase_label.shape[1]
    band_cols = TILE_COLS * peers
    band = peers * tiles
    count = unit_count(peers)
    low_count, first_high = x_slots(peers)
    out_rows = 2 * count * 8
    in_rows = out_rows + -(-count // 8) * 8
    f32 = jnp.float32
    shape = jax.ShapeDtypeStruct
    gx_up, gx_down = ring_pairs("gx")
    gy_up, gy_down = ring_pairs("gy")
    me = lax.axis_index("gy").astype(jnp.int32)
    pops = pltpu.with_memory_space_constraint(populations.reshape(19, tiles, AREA, DEPTH), pltpu.HBM)
    held = charge.reshape(tiles, AREA, DEPTH)

    outgoing = pl.pallas_call(
        functools.partial(pack_source, tiles, band_cols),
        out_shape=pltpu.HBM((peers, AREA + 8, DEPTH), f32),
        in_specs=[SMEM, VMEM, VMEM], out_specs=VMEM, compiler_params=room(6), name="pack_source",
    )(tile_ids, held, fluid_mask)
    outgoing, phase_label = lax.optimization_barrier((outgoing, phase_label))
    arrived = lax.all_to_all(outgoing, "gy", split_axis=0, concat_axis=0, tiled=True)

    beside = [lax.ppermute(phase_label[rows - WIDER :], "gx", gx_up)]
    beside.append(lax.ppermute(phase_label[:WIDER], "gx", gx_down))

    one_tile = pl.BlockSpec((1, AREA, DEPTH), lambda t: (t, 0, 0))
    raw, bits = pl.pallas_call(
        functools.partial(raw_faces, peers),
        grid=(tiles,),
        out_shape=[pltpu.HBM((peers, tiles, out_rows, DEPTH), f32), pltpu.HBM(held.shape, jnp.int32)],
        in_specs=[
            pl.BlockSpec((19, 1, AREA, DEPTH), lambda t: (0, t, 0, 0)),
            one_tile,
            pl.BlockSpec((1, EDGE + 2, EDGE + 2, DEPTH), lambda t: (t, 0, 0, 0)),
        ],
        out_specs=[pl.BlockSpec((peers, 1, out_rows, DEPTH), lambda t: (0, t, 0, 0)), one_tile],
        scratch_shapes=[pltpu.VMEM((3, EDGE + 2, PADDED, DEPTH), jnp.int32)],
        compiler_params=room(14), name="raw_faces",
    )(pops, held, fluid_mask)
    beside[0], beside[1], raw = lax.optimization_barrier((beside[0], beside[1], raw))
    columns = (rows + 2 * WIDER) * WIDER
    lows, highs = pl.pallas_call(
        edge_columns, out_shape=[shape((columns, DEPTH), jnp.int32)] * 2, in_specs=[VMEM] * 3, out_specs=[VMEM] * 2,
        compiler_params=room(4), name="edge_columns",
    )(beside[0], phase_label, beside[1])
    beside += [lax.ppermute(highs, "gy", gy_up), lax.ppermute(lows, "gy", gy_down)]
    arrived, raw, beside = lax.optimization_barrier((arrived, raw, beside))
    beside = list(beside)

    tile_at = arrived[:, AREA, :tiles].astype(jnp.int32).reshape(band)
    slots = jnp.arange(band, dtype=jnp.int32)
    local = jnp.arange(tiles, dtype=jnp.int32)
    mine = local // TILE_COLS * band_cols + TILE_COLS * me + local % TILE_COLS
    wanted = jnp.concatenate([slots, mine])
    slot_of = jnp.sum(jnp.where(tile_at[None, :] == wanted[:, None], slots[None, :], 0), axis=1)

    block, left, right = pl.pallas_call(
        functools.partial(assemble, band, tiles),
        out_shape=[pltpu.VMEM((rows, cols, DEPTH), f32), shape((rows * WIDE, DEPTH), f32), shape((rows * WIDE, DEPTH), f32)],
        in_specs=[SMEM, VMEM], out_specs=[VMEM] * 3, compiler_params=room(5), name="assemble",
    )(slot_of, arrived)
    left, right = lax.ppermute(right, "gy", gy_up), lax.ppermute(left, "gy", gy_down)
    left, right, raw = lax.optimization_barrier((left, right, raw))
    ends = shape((WIDE, cols + 2 * SIDE, DEPTH), f32)
    ups, downs = pl.pallas_call(
        edge_rows, out_shape=[ends, ends], in_specs=[VMEM] * 3, out_specs=[VMEM] * 2,
        compiler_params=room(3), name="edge_rows",
    )(block, left, right)
    ups, downs, beside[0] = lax.optimization_barrier((ups, downs, beside[0]))
    before, after = lax.ppermute(ups, "gx", gx_up), lax.ppermute(downs, "gx", gx_down)
    hbm = pl.BlockSpec(memory_space=pl.ANY)
    wide = shape((rows + 2 * WIDER, cols + 2 * SIDE, DEPTH), f32)
    scratch = pltpu.VMEM(wide.shape, f32)
    weights = pl.pallas_call(
        face_weights, out_shape=[pltpu.VMEM(wide.shape, f32)] * 4, in_specs=[SMEM] + [VMEM] * 5, out_specs=[VMEM] * 4,
        scratch_shapes=[scratch], compiler_params=room(12), name="face_weights",
    )(permittivity, phase_label, *beside)

    faces = lax.all_to_all(raw, "gy", split_axis=0, concat_axis=0, tiled=True).reshape(band, out_rows, DEPTH)
    faces = pltpu.with_memory_space_constraint(faces, pltpu.HBM)
    potential, frames = pl.pallas_call(
        functools.partial(solve, band, tiles),
        out_shape=[shape((rows, cols, DEPTH), f32), pltpu.HBM((peers, FRAME * FRAME, DEPTH), f32)],
        in_specs=[SMEM] + [VMEM] * 9, out_specs=[VMEM, VMEM],
        scratch_shapes=[scratch] * 4, compiler_params=room(16), name="solve",
    )(slot_of, block, left, right, before, after, *weights)
    frames = lax.all_to_all(frames, "gy", split_axis=0, concat_axis=0, tiled=True)

    lows = (band_cols, low_count * 8, DEPTH)
    highs = (band_cols, (count - first_high) * 8, DEPTH)
    low, high = pl.pallas_call(
        functools.partial(outer_rows, peers, band_cols),
        out_shape=[shape(lows, f32), shape(highs, f32)], in_specs=[SMEM, VMEM], out_specs=[VMEM] * 2,
        compiler_params=room(5), name="outer_rows",
    )(slot_of, faces)
    below = lax.ppermute(high, "gx", gx_up)
    above = lax.ppermute(low, "gx", gx_down)
    turned = pl.pallas_call(
        functools.partial(turn_faces, peers, band_cols),
        out_shape=pltpu.HBM((band, in_rows, DEPTH), f32),
        in_specs=[SMEM, SMEM, SMEM, VMEM, VMEM, VMEM], out_specs=VMEM,
        scratch_shapes=[pltpu.VMEM((band,) + highs[1:], f32), pltpu.VMEM((band,) + lows[1:], f32)], compiler_params=room(8), name="turn_faces",
    )(slot_of, tile_at, me[None], faces, below, above)
    rims = lax.all_to_all(turned.reshape(peers, tiles, in_rows, DEPTH), "gy", split_axis=0, concat_axis=0, tiled=True)

    padded = pltpu.VMEM((EDGE + 2, PADDED, DEPTH), f32)
    near = pltpu.VMEM((FRAME, PADDED, DEPTH), f32)
    by_tile = pl.BlockSpec((1, AREA, DEPTH), lambda t, ids: (t, 0, 0))
    of_pops = pl.BlockSpec((19, 1, AREA, DEPTH), lambda t, ids: (0, t, 0, 0))
    of_frame = pl.BlockSpec((1, FRAME * FRAME, DEPTH), lambda t, ids: (ids[t] % band_cols // TILE_COLS, 0, 0))
    of_edges = pl.BlockSpec((1, 4, EDGE, DEPTH), lambda t, ids: (t, 0, 0, 0))
    bits = pltpu.with_memory_space_constraint(bits, pltpu.HBM)
    closed, closed_charge, edges, bands, lines = pl.pallas_call(
        step_inside,
        grid_spec=pltpu.PrefetchScalarGridSpec(
            num_scalar_prefetch=1,
            grid=(tiles,),
            in_specs=[of_pops, by_tile, by_tile, of_frame],
            out_specs=[
                of_pops, by_tile, of_edges,
                pl.BlockSpec((1, len(ACROSS_Y), EDGE, DEPTH), lambda t, ids: (t, 0, 0, 0)),
                pl.BlockSpec((1, len(ACROSS_X), EDGE, DEPTH), lambda t, ids: (t, 0, 0, 0)),
            ],
            scratch_shapes=[
                near,
                pltpu.VMEM((19, EDGE + 2, PADDED, DEPTH), f32),
                padded, padded, padded, padded,
            ],
        ),
        out_shape=[
            shape(pops.shape, f32), pltpu.HBM(held.shape, f32), shape((tiles, 4, EDGE, DEPTH), f32),
            pltpu.HBM((tiles, len(ACROSS_Y), EDGE, DEPTH), f32),
            pltpu.HBM((tiles, len(ACROSS_X), EDGE, DEPTH), f32),
        ],
        compiler_params=room(24), name="step_inside",
    )(tile_ids, pops, held, bits, frames)
    bands, lines, closed_charge = (
        pltpu.with_memory_space_constraint(x, pltpu.HBM) for x in (bands, lines, closed_charge)
    )
    charge_next, populations_next = pl.pallas_call(
        functools.partial(step_faces, peers, tiles, band_cols),
        in_specs=[SMEM] + [hbm] * 9,
        out_specs=[hbm, hbm],
        scratch_shapes=[
            pltpu.VMEM(held.shape, f32),
            pltpu.VMEM(fluid_mask.shape, jnp.int32),
            pltpu.VMEM((tiles, FRAME * FRAME, DEPTH), f32),
            pltpu.VMEM(rims.shape, f32),
            pltpu.VMEM(edges.shape, f32),
            pltpu.VMEM(bands.shape, f32),
            pltpu.VMEM(lines.shape, f32),
            pltpu.VMEM(held.shape, f32),
            pltpu.VMEM((tiles, FRAME, PADDED, DEPTH), f32),
            pltpu.VMEM((tiles, EDGE + 2, PADDED, DEPTH), jnp.int32),
            pltpu.VMEM((tiles, CHANNELS, PADDED, DEPTH), f32),
            pltpu.VMEM((tiles, 2, 5, PADDED, DEPTH), f32),
            pltpu.VMEM((tiles, 2, 5, PADDED, DEPTH), f32),
            pltpu.VMEM(lines.shape, f32),
            pltpu.SemaphoreType.DMA((tiles, 8)),
            pltpu.SemaphoreType.DMA((2, 1 + len(ACROSS_Y + ACROSS_X))),
        ],
        out_shape=[shape(held.shape, f32), shape(populations.shape, f32)],
        input_output_aliases={9: 1},
        compiler_params=room(20), name="step_faces",
    )(tile_ids, held, fluid_mask, frames, rims, edges, bands, lines, closed_charge, closed.reshape(populations.shape))
    return (populations_next, charge_next.reshape(charge.shape), potential)


def solution(mesh):
    placed = (
        P(None, ("gx", "gy"), None, None, None),
        P(("gx", "gy"), None, None, None),
        P(("gx", "gy"), None, None, None),
        P(("gx", "gy")),
        P("gx", "gy", None),
        P(),
    )
    return jax.shard_map(
        per_device,
        mesh=mesh,
        in_specs=placed,
        out_specs=(
            P(None, ("gx", "gy"), None, None, None),
            P(("gx", "gy"), None, None, None),
            P("gx", "gy", None),
        ),
        check_vma=False,
    )
```
